256 devices in a mesh: tm: 32 (over x, z), head: 8 (over y, core).
Axes of the slice: x: 4, y: 4, z: 8, core: 2. Of those that a mesh axis runs over, the one named last changes fastest.
Arguments:
- query_rows: bfloat16 [8192, 5120], P('tm', 'head'), may hold values from -6 to 6
- key_rows: bfloat16 [8192, 5120], P('tm', 'head'), may hold values from -6 to 6
- value_rows: bfloat16 [8192, 5120], P('tm', 'head'), may hold values from -6 to 6
- residual_in: bfloat16 [8192, 5120], P('tm', 'head'), may hold values from -6 to 6
- out_weight: bfloat16 [5120, 5120], P('head'), may hold values from -0.078125 to 0.078125
- time_proj: bfloat16 [256, 5120], P(None, 'head'), may hold values from -0.375 to 0.375
- levels: int32 [32], P('tm'), may hold values from 0 to 49
- timestep_table: int32 [50], replicated, may hold values from 0 to 999
- window_offset: int32 [1], replicated, may hold values from 0 to 31
Outputs:
- advanced: bfloat16 [8192, 5120], P('tm', 'head')
The draws below stay inside these ranges and needn't reach their ends.
All inputs are finite; a program needn't handle non-finite values.
Results may differ from the reference program's by a relative error of at most 0.0075.
Values may be sent and summed in bfloat16 or wider, within the bound.
No kernel may reach another device: no remote copies, remote signals or barrier semaphores. Data moves between devices by JAX's collectives and lax.ppermute only.
A program may use at most 128 MiB of HBM per device.

```python
import math
import jax
import jax.numpy as jnp
from jax import lax

D = 5120
HEADS = 40
HEAD_DIM = 128
FREQ_DIM = 256
SPAN_ROWS = 256
LEVELS = 50
SPANS = 32
TOKENS = 8192


def draw_query_rows(key, part):
    key = jax.random.fold_in(key, 11)
    return jnp.clip(1.6 * jax.random.normal(key, (TOKENS, HEADS * HEAD_DIM), jnp.float32), -6.0, 6.0).astype(jnp.bfloat16)


def draw_key_rows(key, part):
    key = jax.random.fold_in(key, 23)
    return jnp.clip(1.6 * jax.random.normal(key, (TOKENS, HEADS * HEAD_DIM), jnp.float32), -6.0, 6.0).astype(jnp.bfloat16)


def place_ends(values, own_key, low, largest):
    index_at = [jax.random.randint(jax.random.fold_in(own_key, axis), (), 0, length) for axis, length in enumerate(values.shape)]
    longest = values.shape.index(max(values.shape))
    neighbour = index_at[:longest] + [(index_at[longest] + 1) % values.shape[longest]] + index_at[longest + 1:]
    return values.at[tuple(index_at)].set(low).at[tuple(neighbour)].set(largest)


def block_levels(own_key, shape, pieces, smallest, top_value):
    loudness, own = 1.0, jax.random.fold_in(own_key, 6)
    for dim, parts in pieces:
        draws = jnp.exp(jax.random.uniform(jax.random.fold_in(own, dim), (parts,), jnp.float32, smallest / len(pieces), top_value / len(pieces)))
        loudness = loudness * jnp.repeat(draws, shape[dim] // parts).reshape([-1 if axis == dim else 1 for axis in range(len(shape))])
    return loudness


def scatter_about(own_key, shape, scale, most, split=(), kind=jnp.bfloat16):
    values = jax.random.normal(own_key, shape, jnp.float32) * scale
    if len(split) > 0:
        values = block_levels(own_key, shape, split, -0.22, 0.18) * values
    return jnp.clip(values, min=-most, max=most).astype(kind)


def setup_inputs(seed: int = 0) -> dict:
    keys = jax.random.split(jax.random.key(seed), 10)
    return {
        "query_rows": draw_query_rows(jax.random.fold_in(keys[9], 71), 0),
        "key_rows": draw_key_rows(jax.random.fold_in(keys[9], 71), 0),
        "value_rows": scatter_about(keys[2], (TOKENS, HEADS * HEAD_DIM), 1.0, 6.0, ((0, 32), (1, 8))),
        "residual_in": scatter_about(keys[3], (TOKENS, D), 1.0, 6.0, ((0, 32), (1, 8))),
        "out_weight": scatter_about(keys[4], (HEADS * HEAD_DIM, D), (HEADS * HEAD_DIM) ** -0.5, 0.078125, ((0, 8),)),
        "time_proj": scatter_about(keys[5], (FREQ_DIM, D), FREQ_DIM ** -0.5, 0.375, ((1, 8),)),
        "levels": place_ends(jax.random.randint(keys[6], (SPANS,), 0, LEVELS), jax.random.fold_in(keys[6], 1), 0, LEVELS - 1).astype(jnp.int32),
        "timestep_table": place_ends(jax.random.randint(keys[7], (LEVELS,), 0, 1000), jax.random.fold_in(keys[7], 1), 0, 999).astype(jnp.int32),
        "window_offset": jax.random.randint(keys[8], (1,), 0, SPANS).astype(jnp.int32),
    }


def reference(query_rows, key_rows, value_rows, residual_in, out_weight, time_proj, levels, timestep_table, window_offset):
    query_heads = query_rows.astype(jnp.float32).reshape(TOKENS, HEADS, HEAD_DIM)
    key_heads = key_rows.astype(jnp.float32).reshape(TOKENS, HEADS, HEAD_DIM)
    value_heads = value_rows.astype(jnp.float32).reshape(TOKENS, HEADS, HEAD_DIM)
    offset = window_offset[0].astype(jnp.int32)
    row_index = jnp.arange(TOKENS).astype(jnp.int32)
    key_place = ((row_index // SPAN_ROWS - offset) % SPANS).astype(jnp.int32)
    score_scale = 1.0 / math.sqrt(HEAD_DIM)

    def one_span(span_index):
        queries = lax.dynamic_slice_in_dim(query_heads, (span_index * SPAN_ROWS).astype(jnp.int32), SPAN_ROWS, 0)
        own_place = ((span_index - offset) % SPANS).astype(jnp.int32)
        allowed = key_place <= own_place
        scores = jnp.einsum('qhd,khd->hqk', queries, key_heads) * score_scale
        masked = jnp.where(allowed[None, None, :], scores, -1e+30)
        row_top = lax.optimization_barrier(jnp.max(masked, axis=2, keepdims=True))
        weights = jnp.exp(masked - row_top) * allowed[None, None, :].astype(jnp.float32)
        row_total = lax.optimization_barrier(jnp.sum(weights, axis=2))
        rounded = lax.optimization_barrier(weights.astype(jnp.bfloat16)).astype(jnp.float32)
        summed = jnp.einsum('hqk,khd->qhd', rounded, value_heads)
        result = summed / jnp.transpose(row_total)[:, :, None]
        return result.astype(jnp.bfloat16).reshape(SPAN_ROWS, HEADS * HEAD_DIM)
    attention = lax.map(one_span, jnp.arange(SPANS).astype(jnp.int32)).reshape(TOKENS, HEADS * HEAD_DIM)
    projected = jnp.dot(attention, out_weight, preferred_element_type=jnp.float32)
    stamp_value = timestep_table[levels].astype(jnp.float32)
    half_dim = FREQ_DIM // 2
    frequency = jnp.exp(-math.log(10000.0) * jnp.arange(half_dim, dtype=jnp.float32) / half_dim)
    angles = stamp_value[:, None] * frequency[None, :]
    embedding = jnp.concatenate([jnp.cos(angles), jnp.sin(angles)], axis=1).astype(jnp.bfloat16)
    gate_rows = jnp.dot(embedding, time_proj, preferred_element_type=jnp.float32)
    mixed_rows = residual_in.astype(jnp.float32).reshape(SPANS, SPAN_ROWS, D) + gate_rows[:, None, :] * projected.reshape(SPANS, SPAN_ROWS, D)
    mixed_rows = mixed_rows.astype(jnp.bfloat16).reshape(TOKENS, D)
    return jnp.roll(mixed_rows, SPAN_ROWS, axis=0)
```

```python
import math

import jax
import jax.numpy as jnp
import numpy as np
from jax import lax
from jax.experimental import pallas as pl
from jax.experimental.pallas import tpu as pltpu
from jax.sharding import PartitionSpec as P

HEAD_DIM = 128
SPAN = 256
X, Z, Y, C = 4, 8, 4, 2
HERE = 5
SPANS = X * Z
NEGATIVE = -1e30
SCALE = math.log2(math.e) / math.sqrt(HEAD_DIM)
VMEM_LIMIT = 48 * 1024 * 1024

HOST = ((0, 1, 3, 4, 6), (0, 2, 4, 5, 7))
SHARED = tuple(z for z in HOST[0] if z in HOST[1])
SHIFTS = (0, 1, 7, 4, 2, 6, 3, 5)
AXES = ("tm", "head")


def device(x, z, y, c):
    return ((x % X) * Z + z % Z) * (Y * C) + (y % Y) * C + c


def head_at(c, z):
    return HOST[c].index(z % Z) if z % Z in HOST[c] else -1


def worker(c, z, r):
    if z % Z in SHARED:
        return (2 * c + r // 2, r % 2)
    return (r, c)


def work_of(x, z, c):
    if z in SHARED:
        return (x // 2, 2 * (x % 2) + c)
    return (c, x) if z in HOST[c] else None


ALL = [(x, z, y, c) for x in range(X) for z in range(Z) for y in range(Y) for c in range(C)]


def key_pairs(shift):
    return [
        (device(x, z, y, c), device(x, z + shift, y, c))
        for x, z, y, c in ALL
        if head_at(c, z + shift) >= 0
    ]


def query_pairs(shift):
    found = []
    for x, z, y, c in ALL:
        if head_at(c, z + shift) >= 0:
            to_x, to_c = worker(c, z + shift, (x + z) % X)
            found.append((device(x, z, y, c), device(to_x, z + shift, y, to_c)))
    return found


def result_pairs(shift):
    found = []
    for x, z, y, c in ALL:
        work = work_of(x, z, c)
        if work is not None:
            head_core, r = work
            from_z = (z - shift) % Z
            slot = (((r - from_z) % X) * Z + from_z + 1) % SPANS
            found.append((device(x, z, y, c), device(slot // Z, slot % Z, y, head_core)))
    return found


def across_pairs(m, half):
    found = []
    for x, z, y, c in ALL:
        to_x = (x + m) % X
        if z in SHARED:
            if to_x // 2 == c:
                found.append((device(x, z, y, c), device(to_x, z, y, half)))
        elif z in HOST[c]:
            found.append((device(x, z, y, c), device(to_x, z, y, c)))
    return found


def core_pairs(m, half):
    found = []
    for x, z, y, c in ALL:
        if z in SHARED and c == (x // 2 if m == 0 else half):
            found.append((device(x, z, y, c), device(x, z, y, 1 - c)))
    return found


ROUNDS = len(SHIFTS)
HALF = ROUNDS // 2
PACK, QSPAN, KSPAN, TAKE, FROM_OTHER, FROM_OTHER_0, ACTIVE, PLACE_Y, CORE = 0, 8, 16, 48, 56, 58, 59, 60, 61
WIDTH = 64


def table():
    rows = np.zeros((X * Z * Y * C, WIDTH), np.int32)
    for x, z, y, c in ALL:
        row = rows[device(x, z, y, c)]
        work = work_of(x, z, c)
        slot_before = (x * Z + z - 1) % SPANS
        for i, shift in enumerate(SHIFTS):
            row[PACK + i] = head_at(c, z + shift)
            row[TAKE + i] = head_at(c, slot_before % Z + shift)
            from_z = (z - shift) % Z
            if work is not None:
                row[QSPAN + i] = ((work[1] - from_z) % X) * Z + from_z
            for m in range(X):
                row[KSPAN + m * ROUNDS + i] = ((x - m) % X) * Z + from_z
        for half in range(2):
            row[FROM_OTHER + half] = int(z in SHARED and c != half)
        row[FROM_OTHER_0] = int(z in SHARED and c != x // 2)
        row[ACTIVE] = int(work is not None)
        row[PLACE_Y] = y
        row[CORE] = c
    return rows


def moved(block, pairs):
    return lax.ppermute(block, AXES, pairs)


def in_vmem():
    return pl.BlockSpec(memory_space=pltpu.VMEM)


def in_smem():
    return pl.BlockSpec(memory_space=pltpu.SMEM)


def anywhere():
    return pl.BlockSpec(memory_space=pl.ANY)


def shape(*dims, dtype=jnp.bfloat16):
    return jax.ShapeDtypeStruct(dims, dtype)


def pack_kernel(row_ref, query_ref, key_ref, value_ref, *outs):
    for i in range(ROUNDS):
        head = row_ref[PACK + i]

        @pl.when(head >= 0)
        def _():
            columns = pl.ds(pl.multiple_of(head * HEAD_DIM, HEAD_DIM), HEAD_DIM)
            outs[i][:, :HEAD_DIM] = key_ref[:, columns]
            outs[i][:, HEAD_DIM:] = value_ref[:, columns]
            outs[ROUNDS + i][...] = query_ref[:, columns]


def pack(row, query_rows, key_rows, value_rows):
    outs = pl.pallas_call(
        pack_kernel,
        out_shape=[shape(SPAN, 2 * HEAD_DIM)] * ROUNDS + [shape(SPAN, HEAD_DIM)] * ROUNDS,
        in_specs=[in_smem(), in_vmem(), in_vmem(), in_vmem()],
        out_specs=[in_vmem()] * (2 * ROUNDS),
        compiler_params=pltpu.CompilerParams(vmem_limit_bytes=VMEM_LIMIT),
        name="pack",
    )(row, query_rows, key_rows, value_rows)
    return outs[:ROUNDS], outs[ROUNDS:]


BLOCK = 512


def attend_kernel(row_ref, offset_ref, *refs):
    queries, refs = refs[:ROUNDS], refs[ROUNDS:]
    sources, refs = refs[: 4 * X], refs[4 * X :]
    results, (held, copied) = refs[:ROUNDS], refs[ROUNDS:]
    offset = offset_ref[0]

    def place_of(span):
        return lax.rem(span - offset + SPANS, SPANS)

    def rows_at(place):
        return pl.ds(pl.multiple_of(place * SPAN, SPAN), SPAN)

    @pl.when(row_ref[ACTIVE] == 1)
    def _():
        for m in range(X):
            for half in range(2):
                other = row_ref[FROM_OTHER_0 if m == 0 else FROM_OTHER + half]
                for taken in range(2):

                    @pl.when(other == taken)
                    def _():
                        source = sources[taken * 2 * X + m * 2 + half]
                        for i in range(HALF):
                            place = place_of(row_ref[KSPAN + m * ROUNDS + half * HALF + i])
                            pltpu.make_async_copy(
                                source.at[pl.ds(i * SPAN, SPAN)], held.at[rows_at(place)], copied
                            ).start()

        pltpu.make_async_copy(held, held, copied).wait()

        for i in range(ROUNDS):
            own = place_of(row_ref[QSPAN + i])
            query = queries[i][...]

            def step(at, carry, width):
                top, total, summed = carry
                key_rows = pl.ds(pl.multiple_of(at, SPAN), width)
                scores = lax.dot_general(
                    query,
                    held[key_rows, :HEAD_DIM],
                    (((1,), (1,)), ((), ())),
                    preferred_element_type=jnp.float32,
                )
                top_new = jnp.maximum(top, jnp.max(scores, axis=1, keepdims=True))
                weights = jnp.exp2((scores - top_new) * SCALE)
                factor = jnp.exp2((top - top_new) * SCALE)
                total = total * factor + jnp.sum(weights, axis=1, keepdims=True)
                summed = summed * factor + jnp.dot(
                    weights.astype(jnp.bfloat16),
                    held[key_rows, HEAD_DIM:],
                    preferred_element_type=jnp.float32,
                )
                return top_new, total, summed

            start = (
                jnp.full((SPAN, 1), NEGATIVE, jnp.float32),
                jnp.zeros((SPAN, 1), jnp.float32),
                jnp.zeros((SPAN, HEAD_DIM), jnp.float32),
            )
            visible = own + 1
            pairs = lax.div(visible, 2)
            carry = lax.fori_loop(0, pairs, lambda t, s: step(t * BLOCK, s, BLOCK), start)
            carry = lax.fori_loop(2 * pairs, visible, lambda t, s: step(t * SPAN, s, SPAN), carry)
            results[i][...] = (carry[2] / carry[1]).astype(jnp.bfloat16)


def attend(row, offset, queries, sources):
    return pl.pallas_call(
        attend_kernel,
        out_shape=[shape(SPAN, HEAD_DIM)] * ROUNDS,
        in_specs=[in_smem(), in_smem()] + [in_vmem()] * ROUNDS + [anywhere()] * len(sources),
        out_specs=[in_vmem()] * ROUNDS,
        scratch_shapes=[
            pltpu.VMEM((SPANS * SPAN, 2 * HEAD_DIM), jnp.bfloat16),
            pltpu.SemaphoreType.DMA,
        ],
        compiler_params=pltpu.CompilerParams(vmem_limit_bytes=VMEM_LIMIT),
        name="attend",
    )(row, offset, *queries, *sources)


def gather_kernel(row_ref, *refs):
    parts, out_ref = refs[:ROUNDS], refs[ROUNDS]
    for i in range(ROUNDS):
        head = row_ref[TAKE + i]

        @pl.when(head >= 0)
        def _():
            columns = pl.ds(pl.multiple_of(head * HEAD_DIM, HEAD_DIM), HEAD_DIM)
            out_ref[:, columns] = parts[i][...]


def gather_heads(row, parts):
    return pl.pallas_call(
        gather_kernel,
        out_shape=shape(SPAN, HERE * HEAD_DIM),
        in_specs=[in_smem()] + [in_vmem()] * ROUNDS,
        out_specs=in_vmem(),
        compiler_params=pltpu.CompilerParams(vmem_limit_bytes=VMEM_LIMIT),
        name="heads",
    )(row, *parts)


def project_kernel(row_ref, rows_ref, weight_ref, out_ref):
    out_ref[0] = jnp.dot(
        rows_ref[...], weight_ref[...], preferred_element_type=jnp.float32
    ).astype(jnp.bfloat16)


def project(row, rows, weight, other):
    wide = weight.shape[1] // (Y * C)

    def weight_at(m, row_ref):
        core = row_ref[CORE]
        core = 1 - core if other else core
        return (0, lax.rem(row_ref[PLACE_Y] + m, Y) * C + core)

    return pl.pallas_call(
        project_kernel,
        out_shape=shape(Y, SPAN, wide),
        grid_spec=pltpu.PrefetchScalarGridSpec(
            num_scalar_prefetch=1,
            grid=(Y,),
            in_specs=[
                pl.BlockSpec((SPAN, HERE * HEAD_DIM), lambda m, row_ref: (0, 0)),
                pl.BlockSpec((HERE * HEAD_DIM, wide), weight_at),
            ],
            out_specs=pl.BlockSpec((1, SPAN, wide), lambda m, row_ref: (m, 0, 0)),
        ),
        compiler_params=pltpu.CompilerParams(vmem_limit_bytes=VMEM_LIMIT),
        name="project",
    )(row, rows, weight)


def body(
    query_rows,
    key_rows,
    value_rows,
    residual_in,
    out_weight,
    time_proj,
    levels,
    timestep_table,
    window_offset,
):
    me = lax.axis_index("tm") * (Y * C) + lax.axis_index("head")
    row = lax.dynamic_slice(jnp.asarray(table()), (me, 0), (1, WIDTH))[0]
    packed, packed_queries = pack(row, query_rows, key_rows, value_rows)

    arrived = [
        packed[i] if shift == 0 else moved(packed[i], key_pairs(shift))
        for i, shift in enumerate(SHIFTS)
    ]
    queries = [moved(packed_queries[i], query_pairs(shift)) for i, shift in enumerate(SHIFTS)]

    own = [jnp.concatenate(arrived[half * HALF : (half + 1) * HALF]) for half in range(2)]
    direct, shared = {}, {}
    for half in range(2):
        for m in (2, 1, 3, 0):
            direct[m, half] = moved(own[half], across_pairs(m, half)) if m else own[half]
            shared[m, half] = moved(direct[m, half], core_pairs(m, half))
    order = [(m, half) for m in range(X) for half in range(2)]
    sources = [direct[key] for key in order] + [shared[key] for key in order]

    results = attend(row, window_offset, queries, sources)

    parts = [moved(results[i], result_pairs(shift)) for i, shift in enumerate(SHIFTS)]
    next_slot = [
        (device(x, z, y, c), device((x * Z + z + 1) % SPANS // Z, z + 1, y, c)) for x, z, y, c in ALL
    ]
    residual = moved(residual_in, next_slot)
    level = moved(levels, next_slot)[0]

    attention = gather_heads(row, parts)
    swap = [(device(x, z, y, c), device(x, z, y, 1 - c)) for x, z, y, c in ALL]
    from_core = moved(project(row, attention, out_weight, True), swap)
    kept = project(row, attention, out_weight, False)
    both = [kept[m].astype(jnp.float32) + from_core[m].astype(jnp.float32) for m in range(Y)]
    projected = both[0]
    for m in (2, 1, 3):
        pairs = [(device(x, z, y, c), device(x, z, y + m, c)) for x, z, y, c in ALL]
        projected = projected + moved(both[m].astype(jnp.bfloat16), pairs).astype(jnp.float32)

    half_dim = time_proj.shape[0] // 2
    stamp_value = jnp.sum(
        jnp.where(jnp.arange(timestep_table.shape[0], dtype=jnp.int32) == level, timestep_table, 0)
    ).astype(jnp.float32)
    frequency = jnp.exp(-math.log(10000.0) * jnp.arange(half_dim, dtype=jnp.float32) / half_dim)
    angles = stamp_value * frequency
    embedding = jnp.concatenate([jnp.cos(angles), jnp.sin(angles)])[None, :].astype(jnp.bfloat16)
    gate_row = jnp.dot(embedding, time_proj, preferred_element_type=jnp.float32)
    return (residual.astype(jnp.float32) + gate_row * projected).astype(jnp.bfloat16)


def solution(mesh):
    in_specs = (
        P("tm", "head"),
        P("tm", "head"),
        P("tm", "head"),
        P("tm", "head"),
        P("head", None),
        P(None, "head"),
        P("tm"),
        P(),
        P(),
    )
    out_specs = P("tm", "head")
    return jax.shard_map(body, mesh=mesh, in_specs=in_specs, out_specs=out_specs, check_vma=False)
```

```python
import math

import jax
import jax.numpy as jnp
import numpy as np
from jax import lax
from jax.experimental import pallas as pl
from jax.experimental.pallas import tpu as pltpu
from jax.sharding import PartitionSpec as P

HEAD_DIM = 128
SPAN = 256
X, Z, Y, C = 4, 8, 4, 2
HERE = 5
SPANS = X * Z
NEGATIVE = -1e30
SCALE = math.log2(math.e) / math.sqrt(HEAD_DIM)
VMEM_LIMIT = 48 * 1024 * 1024

HOST = ((0, 1, 3, 4, 6), (0, 2, 4, 5, 7))
SHARED = tuple(z for z in HOST[0] if z in HOST[1])
SHIFTS = (0, 4, 1, 5, 2, 6, 3, 7)
AXES = ("tm", "head")


def device(x, z, y, c):
    return ((x % X) * Z + z % Z) * (Y * C) + (y % Y) * C + c


def head_at(c, z):
    return HOST[c].index(z % Z) if z % Z in HOST[c] else -1


def worker(c, z, r):
    if z % Z in SHARED:
        return (2 * c + r // 2, r % 2)
    return (r, c)


def work_of(x, z, c):
    if z in SHARED:
        return (x // 2, 2 * (x % 2) + c)
    return (c, x) if z in HOST[c] else None


ALL = [(x, z, y, c) for x in range(X) for z in range(Z) for y in range(Y) for c in range(C)]


def plane_pairs(shift):
    return [
        (device(x, z, y, c), device(x, z + shift, y, c))
        for x, z, y, c in ALL
        if head_at(c, z + shift) >= 0
    ]


def query_pairs(m):
    found = []
    for x, z, y, c in ALL:
        if head_at(c, z) >= 0 and (m or z in SHARED):
            to_x, to_c = worker(c, z, (x + m) % X)
            found.append((device(x, z, y, c), device(to_x, z, y, to_c)))
    return found


def result_pairs(shift):
    found = []
    for x, z, y, c in ALL:
        work = work_of(x, z, c)
        if work is not None:
            head_core, r = work
            from_z = (z - shift) % Z
            slot = (((r - shift) % X) * Z + from_z + 1) % SPANS
            found.append((device(x, z, y, c), device(slot // Z, slot % Z, y, head_core)))
    return found


def across_pairs(m, half):
    found = []
    for x, z, y, c in ALL:
        to_x = (x + m) % X
        if z in SHARED:
            if to_x // 2 == c:
                found.append((device(x, z, y, c), device(to_x, z, y, half)))
        elif z in HOST[c]:
            found.append((device(x, z, y, c), device(to_x, z, y, c)))
    return found


def core_pairs(own):
    return [
        (device(x, z, y, c), device(x, z, y, 1 - c))
        for x, z, y, c in ALL
        if z in SHARED and (not own or c == x // 2)
    ]


ROUNDS = len(SHIFTS)
HALF = ROUNDS // 2
PACK, QSPAN, KSPAN, TAKE, OTHER, OTHER_OWN, ACTIVE, PLACE_Y, CORE, SHARES = 0, 8, 16, 48, 56, 58, 59, 60, 61, 62
WIDTH = 64


def table():
    rows = np.zeros((X * Z * Y * C, WIDTH), np.int32)
    for x, z, y, c in ALL:
        row = rows[device(x, z, y, c)]
        work = work_of(x, z, c)
        slot_before = (x * Z + z - 1) % SPANS
        for i, shift in enumerate(SHIFTS):
            row[PACK + i] = head_at(c, z + shift)
            row[TAKE + i] = head_at(c, slot_before % Z + shift)
            from_z = (z - shift) % Z
            if work is not None:
                row[QSPAN + i] = ((work[1] - shift) % X) * Z + from_z
            for m in range(X):
                row[KSPAN + m * ROUNDS + i] = ((x - m) % X) * Z + from_z
        for half in range(2):
            row[OTHER + half] = int(z in SHARED and c != half)
        row[OTHER_OWN] = int(z in SHARED and c != x // 2)
        row[ACTIVE] = int(work is not None)
        row[PLACE_Y] = y
        row[CORE] = c
        row[SHARES] = int(z in SHARED)
    return rows


def moved(block, pairs):
    return lax.ppermute(block, AXES, pairs)


def in_vmem():
    return pl.BlockSpec(memory_space=pltpu.VMEM)


def in_smem():
    return pl.BlockSpec(memory_space=pltpu.SMEM)


def anywhere():
    return pl.BlockSpec(memory_space=pl.ANY)


def shape(*dims, dtype=jnp.bfloat16):
    return jax.ShapeDtypeStruct(dims, dtype)


def pack_kernel(row_ref, query_ref, key_ref, value_ref, *outs):
    for i in range(ROUNDS):
        head = row_ref[PACK + i]

        @pl.when(head >= 0)
        def _():
            columns = pl.ds(pl.multiple_of(head * HEAD_DIM, HEAD_DIM), HEAD_DIM)
            for part, ref in enumerate((key_ref, value_ref, query_ref)):
                outs[i][:, part * HEAD_DIM : (part + 1) * HEAD_DIM] = ref[:, columns]


def pack(row, query_rows, key_rows, value_rows):
    return pl.pallas_call(
        pack_kernel,
        out_shape=[shape(SPAN, 3 * HEAD_DIM)] * ROUNDS,
        in_specs=[in_smem(), in_vmem(), in_vmem(), in_vmem()],
        out_specs=[in_vmem()] * ROUNDS,
        compiler_params=pltpu.CompilerParams(vmem_limit_bytes=VMEM_LIMIT),
        name="pack",
    )(row, query_rows, key_rows, value_rows)


STEP = 4
LARGEST = 1e30


def attend_kernel(row_ref, offset_ref, *refs):
    queries, refs = refs[: X + 1], refs[X + 1 :]
    (own_0, own_1, own_other), refs = refs[:3], refs[3:]
    direct, refs = refs[: 2 * (X - 1)], refs[2 * (X - 1) :]
    other, refs = refs[: X - 1], refs[X - 1 :]
    results, (held, rows, answer, copied) = refs[:ROUNDS], refs[ROUNDS:]
    offset = offset_ref[0]

    def place_of(span):
        return lax.rem(span - offset + SPANS, SPANS)

    def bring(source, first, m, half):
        for i in range(HALF):
            place = place_of(row_ref[KSPAN + m * ROUNDS + half * HALF + i])
            at = pl.ds(pl.multiple_of(place * SPAN, SPAN), SPAN)
            pltpu.make_async_copy(
                source.at[pl.ds(first + i * SPAN, SPAN)], held.at[at], copied
            ).start()

    @pl.when(row_ref[ACTIVE] == 1)
    def _():
        for half, own in enumerate((own_0, own_1)):

            @pl.when(row_ref[OTHER_OWN] == 0)
            def _():
                bring(own, 0, 0, half)

            @pl.when(row_ref[OTHER_OWN] == 1)
            def _():
                bring(own_other, half * HALF * SPAN, 0, half)

            for m in range(1, X):

                @pl.when(row_ref[OTHER + half] == 0)
                def _():
                    bring(direct[(m - 1) * 2 + half], 0, m, half)

                @pl.when(row_ref[OTHER + half] == 1)
                def _():
                    bring(other[m - 1], 0, m, half)

        for m in range(1, X):
            rows[m] = queries[m][...]

        @pl.when(row_ref[SHARES] == 0)
        def _():
            rows[0] = queries[0][...]

        @pl.when(row_ref[SHARES] == 1)
        def _():
            rows[0] = queries[X][...]

        pltpu.make_async_copy(held, held, copied).wait()

        def scores_of(query, key_rows):
            return lax.dot_general(
                query,
                held[key_rows, :HEAD_DIM],
                (((1,), (1,)), ((), ())),
                preferred_element_type=jnp.float32,
            )

        def chunk_rows(t):
            return pl.ds(pl.multiple_of(t * STEP * SPAN, STEP * SPAN), STEP * SPAN)

        def hidden(place, own):
            return jnp.where(place <= own, 0.0, LARGEST)

        def fixed_step(t, query, shift, owns):
            scores = scores_of(query, chunk_rows(t))
            weights = []
            for u in range(STEP):
                part = scores[:, u * SPAN : (u + 1) * SPAN]
                moved_by = jnp.concatenate(
                    [
                        shift[n * SPAN : (n + 1) * SPAN] + hidden(t * STEP + u, own)
                        for n, own in enumerate(owns)
                    ]
                )
                weights.append(jnp.exp2(part * SCALE - moved_by))
            total = sum(
                w[:, g : g + HEAD_DIM] for w in weights for g in range(0, SPAN, HEAD_DIM)
            )
            summed = jnp.dot(
                jnp.concatenate([w.astype(jnp.bfloat16) for w in weights], axis=1),
                held[chunk_rows(t), HEAD_DIM:],
                preferred_element_type=jnp.float32,
            )
            return total, summed

        def running(query, own):
            def step(t, carry):
                top, total, summed = carry
                key_rows = pl.ds(pl.multiple_of(t * SPAN, SPAN), SPAN)
                scores = scores_of(query, key_rows)
                top_new = jnp.maximum(top, jnp.max(scores, axis=1, keepdims=True))
                weights = jnp.exp2((scores - top_new) * SCALE)
                factor = jnp.exp2((top - top_new) * SCALE)
                total = total * factor + jnp.sum(weights, axis=1, keepdims=True)
                summed = summed * factor + jnp.dot(
                    weights.astype(jnp.bfloat16),
                    held[key_rows, HEAD_DIM:],
                    preferred_element_type=jnp.float32,
                )
                return top_new, total, summed

            start = (
                jnp.full((SPAN, 1), NEGATIVE, jnp.float32),
                jnp.zeros((SPAN, 1), jnp.float32),
                jnp.zeros((SPAN, HEAD_DIM), jnp.float32),
            )
            carry = lax.fori_loop(0, own + 1, step, start)
            return carry[2] / carry[1]

        def span_rows(n):
            return pl.ds(pl.multiple_of(n * SPAN, SPAN), SPAN)

        for m in range(X):
            owns = [place_of(row_ref[QSPAN + 2 * m + n]) for n in range(2)]
            query = rows[m]
            shift = jnp.max(scores_of(query, pl.ds(0, SPAN)), axis=1, keepdims=True) * SCALE

            def both(t, carry):
                total, summed = fixed_step(t, query, shift, owns)
                return carry[0] + total, carry[1] + summed

            empty = jnp.zeros((2 * SPAN, HEAD_DIM), jnp.float32)
            common = lax.div(jnp.minimum(owns[0], owns[1]), STEP) + 1
            total, summed = lax.fori_loop(0, common, both, (empty, empty))
            answer[0], answer[1] = total, summed

            later = (owns[1] > owns[0]).astype(jnp.int32)
            own = jnp.maximum(owns[0], owns[1])
            late = span_rows(later)
            late_query = rows[m, late, :]
            late_shift = jnp.where(later == 1, shift[SPAN:], shift[:SPAN])

            def one(t, carry):
                total, summed = fixed_step(t, late_query, late_shift, [own])
                return carry[0] + total, carry[1] + summed

            total, summed = lax.fori_loop(
                common, lax.div(own, STEP) + 1, one, (answer[0, late, :], answer[1, late, :])
            )
            answer[0, late, :], answer[1, late, :] = total, summed

            total = jnp.sum(answer[0], axis=1, keepdims=True)
            outcome = answer[1] / total
            for n in range(2):
                results[2 * m + n][...] = outcome[n * SPAN : (n + 1) * SPAN].astype(jnp.bfloat16)

            @pl.when(jnp.logical_not(jnp.max(total) < 1e30))
            def _():
                for n in range(2):
                    results[2 * m + n][...] = running(
                        rows[m, n * SPAN : (n + 1) * SPAN, :], owns[n]
                    ).astype(jnp.bfloat16)


def attend(row, offset, queries, sources):
    return pl.pallas_call(
        attend_kernel,
        out_shape=[shape(SPAN, HEAD_DIM)] * ROUNDS,
        in_specs=[in_smem(), in_smem()] + [in_vmem()] * len(queries) + [anywhere()] * len(sources),
        out_specs=[in_vmem()] * ROUNDS,
        scratch_shapes=[
            pltpu.VMEM((SPANS * SPAN, 2 * HEAD_DIM), jnp.bfloat16),
            pltpu.VMEM((X, 2 * SPAN, HEAD_DIM), jnp.bfloat16),
            pltpu.VMEM((2, 2 * SPAN, HEAD_DIM), jnp.float32),
            pltpu.SemaphoreType.DMA,
        ],
        compiler_params=pltpu.CompilerParams(vmem_limit_bytes=VMEM_LIMIT),
        name="attend",
    )(row, offset, *queries, *sources)


def gather_kernel(row_ref, *refs):
    parts, out_ref = refs[:ROUNDS], refs[ROUNDS]
    for i in range(ROUNDS):
        head = row_ref[TAKE + i]

        @pl.when(head >= 0)
        def _():
            columns = pl.ds(pl.multiple_of(head * HEAD_DIM, HEAD_DIM), HEAD_DIM)
            out_ref[:, columns] = parts[i][...]


def gather_heads(row, parts):
    return pl.pallas_call(
        gather_kernel,
        out_shape=shape(SPAN, HERE * HEAD_DIM),
        in_specs=[in_smem()] + [in_vmem()] * ROUNDS,
        out_specs=in_vmem(),
        compiler_params=pltpu.CompilerParams(vmem_limit_bytes=VMEM_LIMIT),
        name="heads",
    )(row, *parts)


def project_kernel(row_ref, rows_ref, weight_ref, out_ref):
    out_ref[0] = jnp.dot(
        rows_ref[...], weight_ref[...], preferred_element_type=jnp.float32
    ).astype(jnp.bfloat16)


def project(row, rows, weight, other):
    wide = weight.shape[1] // (Y * C)

    def weight_at(m, row_ref):
        core = row_ref[CORE]
        core = 1 - core if other else core
        return (0, lax.rem(row_ref[PLACE_Y] + m, Y) * C + core)

    return pl.pallas_call(
        project_kernel,
        out_shape=shape(Y, SPAN, wide),
        grid_spec=pltpu.PrefetchScalarGridSpec(
            num_scalar_prefetch=1,
            grid=(Y,),
            in_specs=[
                pl.BlockSpec((SPAN, HERE * HEAD_DIM), lambda m, row_ref: (0, 0)),
                pl.BlockSpec((HERE * HEAD_DIM, wide), weight_at),
            ],
            out_specs=pl.BlockSpec((1, SPAN, wide), lambda m, row_ref: (m, 0, 0)),
        ),
        compiler_params=pltpu.CompilerParams(vmem_limit_bytes=VMEM_LIMIT),
        name="project",
    )(row, rows, weight)


def body(
    query_rows,
    key_rows,
    value_rows,
    residual_in,
    out_weight,
    time_proj,
    levels,
    timestep_table,
    window_offset,
):
    me = lax.axis_index("tm") * (Y * C) + lax.axis_index("head")
    row = lax.dynamic_slice(jnp.asarray(table()), (me, 0), (1, WIDTH))[0]
    packed = pack(row, query_rows, key_rows, value_rows)

    arrived = [
        packed[i] if shift == 0 else moved(packed[i], plane_pairs(shift))
        for i, shift in enumerate(SHIFTS)
    ]

    wide = 2 * HEAD_DIM
    own = [
        jnp.concatenate([a[:, :wide] for a in arrived[half * HALF : (half + 1) * HALF]])
        for half in range(2)
    ]
    sent = [
        jnp.concatenate([a[:, wide:] for a in arrived[2 * m : 2 * m + 2]]) for m in range(X)
    ]
    queries = [sent[0]] + [moved(sent[m], query_pairs(m)) for m in (1, 2, 3)]
    queries.append(moved(sent[0], query_pairs(0)))
    direct = [
        [moved(own[half], across_pairs(m, half)) for half in range(2)] for m in range(1, X)
    ]
    own_other = moved(jnp.concatenate(own), core_pairs(True))
    first = row[CORE] == 0
    other = [moved(jnp.where(first, pair[0], pair[1]), core_pairs(False)) for pair in direct]
    sources = own + [own_other] + [part for pair in direct for part in pair] + other

    results = attend(row, window_offset, queries, sources)

    parts = [moved(results[i], result_pairs(shift)) for i, shift in enumerate(SHIFTS)]
    next_slot = [
        (device(x, z, y, c), device((x * Z + z + 1) % SPANS // Z, z + 1, y, c)) for x, z, y, c in ALL
    ]
    residual = moved(residual_in, next_slot)
    level = moved(levels, next_slot)[0]

    attention = gather_heads(row, parts)
    swap = [(device(x, z, y, c), device(x, z, y, 1 - c)) for x, z, y, c in ALL]
    from_core = moved(project(row, attention, out_weight, True), swap)
    kept = project(row, attention, out_weight, False)
    both = [kept[m].astype(jnp.float32) + from_core[m].astype(jnp.float32) for m in range(Y)]
    projected = both[0]
    for m in (2, 1, 3):
        pairs = [(device(x, z, y, c), device(x, z, y + m, c)) for x, z, y, c in ALL]
        projected = projected + moved(both[m].astype(jnp.bfloat16), pairs).astype(jnp.float32)

    half_dim = time_proj.shape[0] // 2
    stamp_value = jnp.sum(
        jnp.where(jnp.arange(timestep_table.shape[0], dtype=jnp.int32) == level, timestep_table, 0)
    ).astype(jnp.float32)
    frequency = jnp.exp(-math.log(10000.0) * jnp.arange(half_dim, dtype=jnp.float32) / half_dim)
    angles = stamp_value * frequency
    embedding = jnp.concatenate([jnp.cos(angles), jnp.sin(angles)])[None, :].astype(jnp.bfloat16)
    gate_row = jnp.dot(embedding, time_proj, preferred_element_type=jnp.float32)
    return (residual.astype(jnp.float32) + gate_row * projected).astype(jnp.bfloat16)


def solution(mesh):
    in_specs = (
        P("tm", "head"),
        P("tm", "head"),
        P("tm", "head"),
        P("tm", "head"),
        P("head", None),
        P(None, "head"),
        P("tm"),
        P(),
        P(),
    )
    out_specs = P("tm", "head")
    return jax.shard_map(body, mesh=mesh, in_specs=in_specs, out_specs=out_specs, check_vma=False)
```

```python
import math

import jax
import jax.numpy as jnp
import numpy as np
from jax import lax
from jax.experimental import pallas as pl
from jax.experimental.pallas import tpu as pltpu
from jax.sharding import PartitionSpec as P

HEAD_DIM = 128
SPAN = 256
X, Z, Y, C = 4, 8, 4, 2
HERE = 5
SPANS = X * Z
NEGATIVE = -1e30
SCALE = math.log2(math.e) / math.sqrt(HEAD_DIM)
VMEM_LIMIT = 48 * 1024 * 1024

HOST = ((0, 1, 3, 4, 6), (0, 2, 4, 5, 7))
AXES = ("tm", "head")
PIECE = SPAN // X
HALF = SPAN // 2


def device(x, z, y, c):
    return ((x % X) * Z + z % Z) * (Y * C) + (y % Y) * C + c


ALL = [(x, z, y, c) for x in range(X) for z in range(Z) for y in range(Y) for c in range(C)]
PLANES = [[x * Z + z for z in range(Z)] for x in range(X)]


def across_pairs(m):
    return [(device(x, z, y, c), device(x + m, z, y, c)) for x, z, y, c in ALL if z in HOST[c]]


HEAD, PLANE, ACTIVE, PLACE_X, PLACE_Y, CORE = 0, 8, 13, 14, 15, 16
WIDTH = 32


def table():
    rows = np.zeros((X * Z * Y * C, WIDTH), np.int32)
    for x, z, y, c in ALL:
        row = rows[device(x, z, y, c)]
        for to_z in range(Z):
            row[HEAD + to_z] = HOST[c].index(to_z) if to_z in HOST[c] else -1
        row[PLANE : PLANE + HERE] = HOST[c]
        row[ACTIVE] = int(z in HOST[c])
        row[PLACE_X] = x
        row[PLACE_Y] = y
        row[CORE] = c
    return rows


def moved(block, pairs):
    return lax.ppermute(block, AXES, pairs)


def in_vmem():
    return pl.BlockSpec(memory_space=pltpu.VMEM)


def in_smem():
    return pl.BlockSpec(memory_space=pltpu.SMEM)


def anywhere():
    return pl.BlockSpec(memory_space=pl.ANY)


def shape(*dims, dtype=jnp.bfloat16):
    return jax.ShapeDtypeStruct(dims, dtype)


def pack_kernel(row_ref, query_ref, key_ref, value_ref, first_ref, second_ref, pieces_ref):
    for z in range(Z):
        head = row_ref[HEAD + z]

        @pl.when(head >= 0)
        def _():
            columns = pl.ds(pl.multiple_of(head * HEAD_DIM, HEAD_DIM), HEAD_DIM)
            for half, out in enumerate((first_ref, second_ref)):
                rows = slice(half * HALF, (half + 1) * HALF)
                out[z, :, :HEAD_DIM] = key_ref[rows, columns]
                out[z, :, HEAD_DIM:] = value_ref[rows, columns]
            for x in range(X):
                pieces_ref[x * Z + z] = query_ref[x * PIECE : (x + 1) * PIECE, columns]


def pack(row, query_rows, key_rows, value_rows):
    return pl.pallas_call(
        pack_kernel,
        out_shape=[shape(Z, HALF, 2 * HEAD_DIM)] * 2 + [shape(SPANS, PIECE, HEAD_DIM)],
        in_specs=[in_smem(), in_vmem(), in_vmem(), in_vmem()],
        out_specs=[in_vmem()] * 3,
        compiler_params=pltpu.CompilerParams(vmem_limit_bytes=VMEM_LIMIT),
        name="pack",
    )(row, query_rows, key_rows, value_rows)


STEP = 4
TILE = 8
TILE_ROWS = TILE * PIECE
STEP_KEYS = STEP * SPAN
LARGEST = 1e30


def attend_kernel(row_ref, offset_ref, pieces_ref, *refs):
    sources, (out_ref, held, rows, copied, moved_rows) = refs[: 2 * X], refs[2 * X :]
    offset = offset_ref[0]

    def place_of(span):
        return lax.rem(span - offset + SPANS, SPANS)

    def scores_of(query, key_rows):
        return lax.dot_general(
            query, held[key_rows, :HEAD_DIM], (((1,), (1,)), ((), ())),
            preferred_element_type=jnp.float32,
        )

    def values_of(weights, key_rows):
        return jnp.dot(
            weights.astype(jnp.bfloat16), held[key_rows, HEAD_DIM:],
            preferred_element_type=jnp.float32,
        )

    def lanes(weights):
        parts = [weights[:, g : g + HEAD_DIM] for g in range(0, weights.shape[1], HEAD_DIM)]
        return sum(parts[1:], parts[0])

    def triangle(scores, shift):
        weights = []
        for g in range(STEP):
            at, seen = slice(g * PIECE, (g + 1) * PIECE), (g + 1) * SPAN
            own = jnp.exp2(scores[at, :seen] * SCALE - shift[at])
            if g + 1 < STEP:
                own = jnp.concatenate(
                    [own, jnp.zeros((PIECE, STEP_KEYS - seen), jnp.float32)], axis=1
                )
            weights.append(own)
        return jnp.concatenate(weights, axis=0)

    def running(query, first_place):
        place = first_place + lax.div(
            lax.broadcasted_iota(jnp.int32, (TILE_ROWS, 1), 0), jnp.int32(PIECE)
        )

        def step(t, carry):
            top, total, summed = carry
            key_rows = pl.ds(pl.multiple_of(t * SPAN, SPAN), SPAN)
            scores = jnp.where(place >= t, scores_of(query, key_rows), NEGATIVE)
            top_new = jnp.maximum(top, jnp.max(scores, axis=1, keepdims=True))
            weights = jnp.where(place >= t, jnp.exp2((scores - top_new) * SCALE), 0.0)
            factor = jnp.exp2((top - top_new) * SCALE)
            total = total * factor + jnp.sum(weights, axis=1, keepdims=True)
            return top_new, total, summed * factor + values_of(weights, key_rows)

        start = (
            jnp.full((TILE_ROWS, 1), NEGATIVE, jnp.float32),
            jnp.zeros((TILE_ROWS, 1), jnp.float32),
            jnp.zeros((TILE_ROWS, HEAD_DIM), jnp.float32),
        )
        carry = lax.fori_loop(0, first_place + TILE, step, start)
        return carry[2] / carry[1]

    @pl.when(row_ref[ACTIVE] == 1)
    def _():
        for m in range(X):
            from_x = lax.rem(row_ref[PLACE_X] - m + X, X)
            for z in range(Z):
                place = place_of(from_x * Z + z)
                for half in range(2):
                    at = pl.ds(pl.multiple_of(place * SPAN + half * HALF, HALF), HALF)
                    pltpu.make_async_copy(
                        sources[m * 2 + half].at[z], held.at[at], copied
                    ).start()
        for span in range(SPANS):
            at = pl.ds(pl.multiple_of(place_of(span) * PIECE, PIECE), PIECE)
            pltpu.make_async_copy(pieces_ref.at[span], rows.at[at], moved_rows).start()
        pltpu.make_async_copy(rows, rows, moved_rows).wait()
        pltpu.make_async_copy(held, held, copied).wait()

        for tile in range(SPANS // TILE):
            query = rows[tile * TILE_ROWS : (tile + 1) * TILE_ROWS, :]
            shift = jnp.max(scores_of(query, pl.ds(0, SPAN)), axis=1, keepdims=True) * SCALE

            def step(t, carry):
                key_rows = pl.ds(pl.multiple_of(t * STEP_KEYS, STEP_KEYS), STEP_KEYS)
                weights = jnp.exp2(scores_of(query, key_rows) * SCALE - shift)
                return carry[0] + lanes(weights), carry[1] + values_of(weights, key_rows)

            empty = jnp.zeros((TILE_ROWS, HEAD_DIM), jnp.float32)
            total, summed = lax.fori_loop(0, 2 * tile, step, (empty, empty))

            half = TILE_ROWS // 2
            key_rows = pl.ds(2 * tile * STEP_KEYS, STEP_KEYS)
            scores = scores_of(query, key_rows)
            weights = jnp.concatenate(
                [
                    triangle(scores[:half], shift[:half]),
                    jnp.exp2(scores[half:] * SCALE - shift[half:]),
                ],
                axis=0,
            )
            total, summed = total + lanes(weights), summed + values_of(weights, key_rows)
            key_rows = pl.ds((2 * tile + 1) * STEP_KEYS, STEP_KEYS)
            weights = triangle(scores_of(query[half:], key_rows), shift[half:])
            total = jnp.concatenate([total[:half], total[half:] + lanes(weights)], axis=0)
            summed = jnp.concatenate(
                [summed[:half], summed[half:] + values_of(weights, key_rows)], axis=0
            )
            total = jnp.sum(total, axis=1, keepdims=True)

            def put(answer):
                for n in range(TILE):
                    slot = lax.rem(offset + (tile * TILE + n + 1), SPANS)
                    out_ref[slot] = answer[n * PIECE : (n + 1) * PIECE].astype(jnp.bfloat16)

            put(summed / total)

            @pl.when(jnp.logical_not(jnp.max(total) < LARGEST))
            def _():
                put(running(query, tile * TILE))


def attend(row, offset, pieces, sources):
    return pl.pallas_call(
        attend_kernel,
        out_shape=shape(SPANS, PIECE, HEAD_DIM),
        in_specs=[in_smem(), in_smem(), in_vmem()] + [anywhere()] * len(sources),
        out_specs=in_vmem(),
        scratch_shapes=[
            pltpu.VMEM((SPANS * SPAN, 2 * HEAD_DIM), jnp.bfloat16),
            pltpu.VMEM((SPANS * PIECE, HEAD_DIM), jnp.bfloat16),
            pltpu.SemaphoreType.DMA,
            pltpu.SemaphoreType.DMA,
        ],
        compiler_params=pltpu.CompilerParams(vmem_limit_bytes=VMEM_LIMIT),
        name="attend",
    )(row, offset, pieces, *sources)


def gather_kernel(row_ref, parts_ref, out_ref):
    for head in range(HERE):
        for x in range(X):
            out_ref[x * PIECE : (x + 1) * PIECE, head * HEAD_DIM : (head + 1) * HEAD_DIM] = (
                parts_ref[x * Z + row_ref[PLANE + head]]
            )


def gather_heads(row, parts):
    return pl.pallas_call(
        gather_kernel,
        out_shape=shape(SPAN, HERE * HEAD_DIM),
        in_specs=[in_smem(), in_vmem()],
        out_specs=in_vmem(),
        compiler_params=pltpu.CompilerParams(vmem_limit_bytes=VMEM_LIMIT),
        name="heads",
    )(row, parts)


def project_kernel(row_ref, rows_ref, weight_ref, out_ref):
    out_ref[0] = jnp.dot(
        rows_ref[...], weight_ref[...], preferred_element_type=jnp.float32
    ).astype(jnp.bfloat16)


def project(row, rows, weight, other):
    wide = weight.shape[1] // (Y * C)

    def weight_at(m, row_ref):
        core = row_ref[CORE]
        core = 1 - core if other else core
        return (0, lax.rem(row_ref[PLACE_Y] + m, Y) * C + core)

    return pl.pallas_call(
        project_kernel,
        out_shape=shape(Y, SPAN, wide),
        grid_spec=pltpu.PrefetchScalarGridSpec(
            num_scalar_prefetch=1,
            grid=(Y,),
            in_specs=[
                pl.BlockSpec((SPAN, HERE * HEAD_DIM), lambda m, row_ref: (0, 0)),
                pl.BlockSpec((HERE * HEAD_DIM, wide), weight_at),
            ],
            out_specs=pl.BlockSpec((1, SPAN, wide), lambda m, row_ref: (m, 0, 0)),
        ),
        compiler_params=pltpu.CompilerParams(vmem_limit_bytes=VMEM_LIMIT),
        name="project",
    )(row, rows, weight)


def body(
    query_rows,
    key_rows,
    value_rows,
    residual_in,
    out_weight,
    time_proj,
    levels,
    timestep_table,
    window_offset,
):
    me = lax.axis_index("tm") * (Y * C) + lax.axis_index("head")
    row = lax.dynamic_slice(jnp.asarray(table()), (me, 0), (1, WIDTH))[0]
    first, second, pieces = pack(row, query_rows, key_rows, value_rows)

    arrived = [
        lax.all_to_all(part, "tm", 0, 0, axis_index_groups=PLANES, tiled=True)
        for part in (first, second)
    ]
    sources = []
    for m in range(X):
        sources += [moved(part, across_pairs(m)) if m else part for part in arrived]
    pieces = lax.all_to_all(pieces, "tm", 0, 0, tiled=True)
    answers = attend(row, window_offset, pieces, sources)
    answers = lax.all_to_all(answers, "tm", 0, 0, tiled=True)
    attention = gather_heads(row, answers)

    next_slot = [
        (device(x, z, y, c), device((x * Z + z + 1) % SPANS // Z, z + 1, y, c)) for x, z, y, c in ALL
    ]
    residual = moved(residual_in, next_slot)
    level = moved(levels, next_slot)[0]

    swap = [(device(x, z, y, c), device(x, z, y, 1 - c)) for x, z, y, c in ALL]
    from_core = moved(project(row, attention, out_weight, True), swap)
    kept = project(row, attention, out_weight, False)
    both = [kept[m].astype(jnp.float32) + from_core[m].astype(jnp.float32) for m in range(Y)]
    projected = both[0]
    for m in (2, 1, 3):
        pairs = [(device(x, z, y, c), device(x, z, y + m, c)) for x, z, y, c in ALL]
        projected = projected + moved(both[m].astype(jnp.bfloat16), pairs).astype(jnp.float32)

    half_dim = time_proj.shape[0] // 2
    stamp_value = jnp.sum(
        jnp.where(jnp.arange(timestep_table.shape[0], dtype=jnp.int32) == level, timestep_table, 0)
    ).astype(jnp.float32)
    frequency = jnp.exp(-math.log(10000.0) * jnp.arange(half_dim, dtype=jnp.float32) / half_dim)
    angles = stamp_value * frequency
    embedding = jnp.concatenate([jnp.cos(angles), jnp.sin(angles)])[None, :].astype(jnp.bfloat16)
    gate_row = jnp.dot(embedding, time_proj, preferred_element_type=jnp.float32)
    return (residual.astype(jnp.float32) + gate_row * projected).astype(jnp.bfloat16)


def solution(mesh):
    in_specs = (
        P("tm", "head"),
        P("tm", "head"),
        P("tm", "head"),
        P("tm", "head"),
        P("head", None),
        P(None, "head"),
        P("tm"),
        P(),
        P(),
    )
    out_specs = P("tm", "head")
    return jax.shard_map(body, mesh=mesh, in_specs=in_specs, out_specs=out_specs, check_vma=False)
```

```python
import functools
import math

import jax
import jax.numpy as jnp
import numpy as np
from jax import lax
from jax.experimental import pallas as pl
from jax.experimental.pallas import tpu as pltpu
from jax.sharding import PartitionSpec as P

HEAD_DIM = 128
SPAN = 256
X, Z, Y, C = 4, 8, 4, 2
HERE = 5
SPANS = X * Z
NEGATIVE = -1e30
SCALE = math.log2(math.e) / math.sqrt(HEAD_DIM)
VMEM_LIMIT = 48 * 1024 * 1024

HOST = ((0, 1, 3, 4, 6), (0, 2, 4, 5, 7))
AXES = ("tm", "head")
PIECE = SPAN // X


def device(x, z, y, c):
    return ((x % X) * Z + z % Z) * (Y * C) + (y % Y) * C + c


ALL = [(x, z, y, c) for x in range(X) for z in range(Z) for y in range(Y) for c in range(C)]
PLANES = [[x * Z + z for z in range(Z)] for x in range(X)]


def across_pairs(m):
    return [(device(x, z, y, c), device(x + m, z, y, c)) for x, z, y, c in ALL if z in HOST[c]]


HEAD, PLANE, ACTIVE, PLACE_X, PLACE_Y, CORE = 0, 8, 13, 14, 15, 16
WIDTH = 32


def table():
    rows = np.zeros((X * Z * Y * C, WIDTH), np.int32)
    for x, z, y, c in ALL:
        row = rows[device(x, z, y, c)]
        for to_z in range(Z):
            row[HEAD + to_z] = HOST[c].index(to_z) if to_z in HOST[c] else -1
        row[PLANE : PLANE + HERE] = HOST[c]
        row[ACTIVE] = int(z in HOST[c])
        row[PLACE_X] = x
        row[PLACE_Y] = y
        row[CORE] = c
    return rows


def moved(block, pairs):
    return lax.ppermute(block, AXES, pairs)


def in_vmem():
    return pl.BlockSpec(memory_space=pltpu.VMEM)


def in_smem():
    return pl.BlockSpec(memory_space=pltpu.SMEM)


def anywhere():
    return pl.BlockSpec(memory_space=pl.ANY)


def shape(*dims, dtype=jnp.bfloat16):
    return jax.ShapeDtypeStruct(dims, dtype)


def pack_kernel(row_ref, query_ref, key_ref, value_ref, keys_ref, pieces_ref):
    for z in range(Z):
        head = row_ref[HEAD + z]

        @pl.when(head >= 0)
        def _():
            columns = pl.ds(pl.multiple_of(head * HEAD_DIM, HEAD_DIM), HEAD_DIM)
            keys_ref[z, :, :HEAD_DIM] = key_ref[:, columns]
            keys_ref[z, :, HEAD_DIM:] = value_ref[:, columns]
            for x in range(X):
                pieces_ref[x * Z + z] = query_ref[x * PIECE : (x + 1) * PIECE, columns]


def pack(row, query_rows, key_rows, value_rows):
    return pl.pallas_call(
        pack_kernel,
        out_shape=[shape(Z, SPAN, 2 * HEAD_DIM), shape(SPANS, PIECE, HEAD_DIM)],
        in_specs=[in_smem(), in_vmem(), in_vmem(), in_vmem()],
        out_specs=[in_vmem()] * 2,
        compiler_params=pltpu.CompilerParams(vmem_limit_bytes=VMEM_LIMIT),
        name="pack",
    )(row, query_rows, key_rows, value_rows)


STEP = Z // 2
STEP_KEYS = STEP * SPAN
STEPS = 2 * X
TILE = 8
TILES = SPANS // TILE
TILE_ROWS = TILE * PIECE
ROWS = SPANS * PIECE
SMALLEST, LARGEST = 1e-18, 1e30


def attend_kernel(places, ends, row_ref, offset_ref, pieces_ref, *refs):
    sources, refs = refs[: len(places)], refs[len(places) :]
    if ends:
        (total_in, summed_in, shift_ref), refs = refs[:3], refs[3:]
        later_steps, refs = refs[: STEPS - len(places)], refs[STEPS - len(places) :]
        refs = refs[len(refs) - 6 :]
        out_ref, held, rows, total_ref, summed_ref, copied = refs
    else:
        total_ref, summed_ref, shift_ref, held, rows, copied = refs
    offset = offset_ref[0]

    def place_of(span):
        return lax.rem(span - offset + SPANS, SPANS)

    def first_place(at):
        m, half = at
        return place_of(lax.rem(row_ref[PLACE_X] - m + X, X) * Z + half * STEP)

    def pick(values, i):
        found = values[0]
        for n, value in enumerate(values[1:], 1):
            found = jnp.where(i == n, value, found)
        return found

    def scores_of(query, keys):
        return lax.dot_general(
            query, keys, (((1,), (1,)), ((), ())), preferred_element_type=jnp.float32
        )

    def values_of(weights, values):
        return jnp.dot(
            weights.astype(jnp.bfloat16), values, preferred_element_type=jnp.float32
        )

    def lanes(weights):
        parts = [weights[:, g : g + HEAD_DIM] for g in range(0, weights.shape[1], HEAD_DIM)]
        return sum(parts[1:], parts[0])

    def tile_rows(tile):
        return pl.ds(pl.multiple_of(tile * TILE_ROWS, TILE_ROWS), TILE_ROWS)

    def row_places(tile):
        return tile * TILE + lax.div(
            lax.broadcasted_iota(jnp.int32, (TILE_ROWS, 1), 0), jnp.int32(PIECE)
        )

    def running(tile, firsts):
        query, own = rows[tile_rows(tile), :], row_places(tile)

        def step(t, carry):
            top, total, summed = carry
            key_rows = pl.ds(pl.multiple_of(lax.rem(t, STEP) * SPAN, SPAN), SPAN)
            at = lax.div(t, STEP)
            seen = own >= lax.rem(pick(firsts, at) + lax.rem(t, STEP), SPANS)
            scores = jnp.where(seen, scores_of(query, held[at, key_rows, :HEAD_DIM]), NEGATIVE)
            top_new = jnp.maximum(top, jnp.max(scores, axis=1, keepdims=True))
            weights = jnp.where(seen, jnp.exp2((scores - top_new) * SCALE), 0.0)
            factor = jnp.exp2((top - top_new) * SCALE)
            total = total * factor + jnp.sum(weights, axis=1, keepdims=True)
            summed = summed * factor + values_of(weights, held[at, key_rows, HEAD_DIM:])
            return top_new, total, summed

        start = (
            jnp.full((TILE_ROWS, 1), NEGATIVE, jnp.float32),
            jnp.zeros((TILE_ROWS, 1), jnp.float32),
            jnp.zeros((TILE_ROWS, HEAD_DIM), jnp.float32),
        )
        carry = lax.fori_loop(0, SPANS, step, start)
        return carry[2] / carry[1]

    @pl.when(row_ref[ACTIVE] == 1)
    def _():
        steps = len(places)
        for i, source in enumerate(sources):
            pltpu.make_async_copy(source, held.at[i], copied).start()
        for span in range(SPANS):
            at = pl.ds(pl.multiple_of(place_of(span) * PIECE, PIECE), PIECE)
            rows[at, :] = pieces_ref[span]
        firsts = [first_place(at) for at in places]
        if ends:
            total_ref[...] = total_in[...]
            summed_ref[...] = summed_in[...]
        else:
            total_ref[...] = jnp.zeros_like(total_ref)
            summed_ref[...] = jnp.zeros_like(summed_ref)
        brought = held.at[pl.ds(0, steps)]
        pltpu.make_async_copy(brought, brought, copied).wait()

        if not ends:
            for tile in range(TILES):
                at = slice(tile * TILE_ROWS, (tile + 1) * TILE_ROWS)
                top = jnp.max(
                    scores_of(rows[at, :], held[0, :HEAD_DIM, :HEAD_DIM]), axis=1, keepdims=True
                )
                shift_ref[at, :] = jnp.broadcast_to(top * SCALE, (TILE_ROWS, HEAD_DIM))

        def add(tile, i, masked, first):
            at = tile_rows(tile)
            scores = scores_of(rows[at, :], held[i, :, :HEAD_DIM])
            shift = shift_ref[at, :1]
            if masked:
                own = row_places(tile)
                weights = []
                for u in range(STEP):
                    hidden = own < lax.rem(first + u, SPANS)
                    part = scores[:, u * SPAN : (u + 1) * SPAN] * SCALE
                    weights.append(jnp.exp2(part - jnp.where(hidden, LARGEST, shift)))
                weights = jnp.concatenate(weights, axis=1)
            else:
                weights = jnp.exp2(scores * SCALE - shift)
            total_ref[at, :] += lanes(weights)
            summed_ref[at, :] += values_of(weights, held[i, :, HEAD_DIM:])

        def one(n, unused):
            tile, i = lax.div(n, steps), lax.rem(n, steps)
            first = pick(firsts, i)
            wraps = first > SPANS - STEP
            lowest = jnp.where(wraps, 0, first)
            highest = jnp.where(wraps, SPANS - 1, first + STEP - 1)
            whole = highest <= tile * TILE

            @pl.when(whole)
            def _():
                add(tile, i, False, first)

            @pl.when(jnp.logical_not(whole) & (lowest < (tile + 1) * TILE))
            def _():
                add(tile, i, True, first)

            return unused

        lax.fori_loop(0, TILES * steps, one, 0)

        if ends:

            def put(tile, answer):
                for n in range(TILE):
                    slot = lax.rem(offset + (tile * TILE + n + 1), SPANS)
                    out_ref[slot] = answer[n * PIECE : (n + 1) * PIECE].astype(jnp.bfloat16)

            total = jnp.sum(total_ref[...], axis=1, keepdims=True)
            for tile in range(TILES):
                at = slice(tile * TILE_ROWS, (tile + 1) * TILE_ROWS)
                put(tile, summed_ref[at, :] / total[at])

            safe = (jnp.max(total) < LARGEST) & (jnp.min(total) > SMALLEST)

            @pl.when(jnp.logical_not(safe))
            def _():
                for i, source in enumerate(later_steps):
                    pltpu.make_async_copy(source, held.at[steps + i], copied).start()
                brought = held.at[pl.ds(steps, STEPS - steps)]
                pltpu.make_async_copy(brought, brought, copied).wait()
                all_firsts = firsts + [first_place(at) for at in NEAR]
                for tile in range(TILES):
                    put(tile, running(tile, all_firsts))


NEAR = ((0, 0), (0, 1), (1, 0), (1, 1), (3, 0), (3, 1))
FAR = ((2, 0), (2, 1))


def attend_near(row, offset, pieces, near):
    held = shape(ROWS, HEAD_DIM, dtype=jnp.float32)
    return pl.pallas_call(
        functools.partial(attend_kernel, NEAR, False),
        out_shape=[held] * 3,
        in_specs=[in_smem(), in_smem(), in_vmem()] + [anywhere()] * len(near),
        out_specs=[in_vmem()] * 3,
        scratch_shapes=[
            pltpu.VMEM((len(near), STEP_KEYS, 2 * HEAD_DIM), jnp.bfloat16),
            pltpu.VMEM((ROWS, HEAD_DIM), jnp.bfloat16),
            pltpu.SemaphoreType.DMA,
        ],
        compiler_params=pltpu.CompilerParams(vmem_limit_bytes=VMEM_LIMIT),
        name="near",
    )(row, offset, pieces, *near)


def attend_far(row, offset, pieces, far, state, near, others):
    return pl.pallas_call(
        functools.partial(attend_kernel, FAR, True),
        out_shape=shape(SPANS, PIECE, HEAD_DIM),
        in_specs=[in_smem(), in_smem(), in_vmem()]
        + [anywhere()] * len(far)
        + [in_vmem()] * len(state)
        + [anywhere()] * (len(near) + len(others)),
        out_specs=in_vmem(),
        scratch_shapes=[
            pltpu.VMEM((STEPS, STEP_KEYS, 2 * HEAD_DIM), jnp.bfloat16),
            pltpu.VMEM((ROWS, HEAD_DIM), jnp.bfloat16),
            pltpu.VMEM((ROWS, HEAD_DIM), jnp.float32),
            pltpu.VMEM((ROWS, HEAD_DIM), jnp.float32),
            pltpu.SemaphoreType.DMA,
        ],
        compiler_params=pltpu.CompilerParams(vmem_limit_bytes=VMEM_LIMIT),
        name="far",
    )(row, offset, pieces, *far, *state, *near, *others)


def gather_kernel(row_ref, parts_ref, out_ref):
    for head in range(HERE):
        for x in range(X):
            out_ref[x * PIECE : (x + 1) * PIECE, head * HEAD_DIM : (head + 1) * HEAD_DIM] = (
                parts_ref[x * Z + row_ref[PLANE + head]]
            )


def gather_heads(row, parts):
    return pl.pallas_call(
        gather_kernel,
        out_shape=shape(SPAN, HERE * HEAD_DIM),
        in_specs=[in_smem(), in_vmem()],
        out_specs=in_vmem(),
        compiler_params=pltpu.CompilerParams(vmem_limit_bytes=VMEM_LIMIT),
        name="heads",
    )(row, parts)


def project_kernel(row_ref, rows_ref, weight_ref, out_ref):
    out_ref[0] = jnp.dot(
        rows_ref[...], weight_ref[...], preferred_element_type=jnp.float32
    ).astype(jnp.bfloat16)


def project(row, rows, weight, other):
    wide = weight.shape[1] // (Y * C)

    def weight_at(m, row_ref):
        core = row_ref[CORE]
        core = 1 - core if other else core
        return (0, lax.rem(row_ref[PLACE_Y] + m, Y) * C + core)

    return pl.pallas_call(
        project_kernel,
        out_shape=shape(Y, SPAN, wide),
        grid_spec=pltpu.PrefetchScalarGridSpec(
            num_scalar_prefetch=1,
            grid=(Y,),
            in_specs=[
                pl.BlockSpec((SPAN, HERE * HEAD_DIM), lambda m, row_ref: (0, 0)),
                pl.BlockSpec((HERE * HEAD_DIM, wide), weight_at),
            ],
            out_specs=pl.BlockSpec((1, SPAN, wide), lambda m, row_ref: (m, 0, 0)),
        ),
        compiler_params=pltpu.CompilerParams(vmem_limit_bytes=VMEM_LIMIT),
        name="project",
    )(row, rows, weight)


def body(
    query_rows,
    key_rows,
    value_rows,
    residual_in,
    out_weight,
    time_proj,
    levels,
    timestep_table,
    window_offset,
):
    me = lax.axis_index("tm") * (Y * C) + lax.axis_index("head")
    row = lax.dynamic_slice(jnp.asarray(table()), (me, 0), (1, WIDTH))[0]
    keys, pieces = pack(row, query_rows, key_rows, value_rows)

    keys = lax.all_to_all(keys, "tm", 0, 0, axis_index_groups=PLANES, tiled=True)
    pieces = lax.all_to_all(pieces, "tm", 0, 0, tiled=True)

    own = [keys[half * STEP : (half + 1) * STEP].reshape(STEP_KEYS, -1) for half in range(2)]
    back = [moved(part, across_pairs(1)) for part in own]
    ahead = [moved(part, across_pairs(-1)) for part in own]
    far = [moved(ahead[0], across_pairs(-1)), moved(back[1], across_pairs(1))]
    near = own + back + ahead

    next_slot = [
        (device(x, z, y, c), device((x * Z + z + 1) % SPANS // Z, z + 1, y, c)) for x, z, y, c in ALL
    ]
    residual = moved(residual_in, next_slot)
    level = moved(levels, next_slot)

    state = attend_near(row, window_offset, pieces, near)
    answers = attend_far(row, window_offset, pieces, far, state, near, [residual, level])
    answers = lax.all_to_all(answers, "tm", 0, 0, tiled=True)
    attention = gather_heads(row, answers)

    swap = [(device(x, z, y, c), device(x, z, y, 1 - c)) for x, z, y, c in ALL]
    from_core = moved(project(row, attention, out_weight, True), swap)
    kept = project(row, attention, out_weight, False)
    both = [kept[m].astype(jnp.float32) + from_core[m].astype(jnp.float32) for m in range(Y)]
    projected = both[0]
    for m in (2, 1, 3):
        pairs = [(device(x, z, y, c), device(x, z, y + m, c)) for x, z, y, c in ALL]
        projected = projected + moved(both[m].astype(jnp.bfloat16), pairs).astype(jnp.float32)

    half_dim = time_proj.shape[0] // 2
    stamp_value = jnp.sum(
        jnp.where(jnp.arange(timestep_table.shape[0], dtype=jnp.int32) == level[0], timestep_table, 0)
    ).astype(jnp.float32)
    frequency = jnp.exp(-math.log(10000.0) * jnp.arange(half_dim, dtype=jnp.float32) / half_dim)
    angles = stamp_value * frequency
    embedding = jnp.concatenate([jnp.cos(angles), jnp.sin(angles)])[None, :].astype(jnp.bfloat16)
    gate_row = jnp.dot(embedding, time_proj, preferred_element_type=jnp.float32)
    return (residual.astype(jnp.float32) + gate_row * projected).astype(jnp.bfloat16)


def solution(mesh):
    in_specs = (
        P("tm", "head"),
        P("tm", "head"),
        P("tm", "head"),
        P("tm", "head"),
        P("head", None),
        P(None, "head"),
        P("tm"),
        P(),
        P(),
    )
    out_specs = P("tm", "head")
    return jax.shard_map(body, mesh=mesh, in_specs=in_specs, out_specs=out_specs, check_vma=False)
```

```python
import functools
import math

import jax
import jax.numpy as jnp
import numpy as np
from jax import lax
from jax.experimental import pallas as pl
from jax.experimental.pallas import tpu as pltpu
from jax.sharding import PartitionSpec as P

HEAD_DIM = 128
SPAN = 256
X, Z, Y, C = 4, 8, 4, 2
HERE = 5
SPANS = X * Z
NEGATIVE = -1e30
SCALE = math.log2(math.e) / math.sqrt(HEAD_DIM)
VMEM_LIMIT = 48 * 1024 * 1024

HOST = ((0, 1, 3, 4, 6), (0, 2, 4, 5, 7))
SHIFTS = (0, 4, 1, 7, 3, 5, 2, 6)
AXES = ("tm", "head")
PIECE = SPAN // X


def device(x, z, y, c):
    return ((x % X) * Z + z % Z) * (Y * C) + (y % Y) * C + c


ALL = [(x, z, y, c) for x in range(X) for z in range(Z) for y in range(Y) for c in range(C)]


def plane_pairs(shift):
    return [
        (device(x, z, y, c), device(x, z + shift, y, c))
        for x, z, y, c in ALL
        if (z + shift) % Z in HOST[c]
    ]


def across_pairs(m):
    return [(device(x, z, y, c), device(x + m, z, y, c)) for x, z, y, c in ALL if z in HOST[c]]


HEAD, PLANE, ACTIVE, PLACE_X, PLACE_Y, CORE, SEND, FROM = 0, 8, 13, 14, 15, 16, 17, 25
WIDTH = 64


def table():
    rows = np.zeros((X * Z * Y * C, WIDTH), np.int32)
    for x, z, y, c in ALL:
        row = rows[device(x, z, y, c)]
        for to_z in range(Z):
            row[HEAD + to_z] = HOST[c].index(to_z) if to_z in HOST[c] else -1
        row[PLANE : PLANE + HERE] = HOST[c]
        row[ACTIVE] = int(z in HOST[c])
        row[PLACE_X] = x
        row[PLACE_Y] = y
        row[CORE] = c
        for i, shift in enumerate(SHIFTS):
            row[SEND + i] = row[HEAD + (z + shift) % Z]
            row[FROM + i] = (z - shift) % Z
    return rows


def moved(block, pairs):
    return lax.ppermute(block, AXES, pairs)


def in_vmem():
    return pl.BlockSpec(memory_space=pltpu.VMEM)


def in_smem():
    return pl.BlockSpec(memory_space=pltpu.SMEM)


def anywhere():
    return pl.BlockSpec(memory_space=pl.ANY)


def shape(*dims, dtype=jnp.bfloat16):
    return jax.ShapeDtypeStruct(dims, dtype)


def pack_kernel(row_ref, query_ref, key_ref, value_ref, *outs):
    pieces_ref = outs[-1]
    for i in range(Z):
        head = row_ref[SEND + i]

        @pl.when(head >= 0)
        def _():
            columns = pl.ds(pl.multiple_of(head * HEAD_DIM, HEAD_DIM), HEAD_DIM)
            outs[i][:, :HEAD_DIM] = key_ref[:, columns]
            outs[i][:, HEAD_DIM:] = value_ref[:, columns]

    for z in range(Z):
        head = row_ref[HEAD + z]

        @pl.when(head >= 0)
        def _():
            columns = pl.ds(pl.multiple_of(head * HEAD_DIM, HEAD_DIM), HEAD_DIM)
            for x in range(X):
                pieces_ref[x * Z + z] = query_ref[x * PIECE : (x + 1) * PIECE, columns]


def pack(row, query_rows, key_rows, value_rows):
    outs = pl.pallas_call(
        pack_kernel,
        out_shape=[shape(SPAN, 2 * HEAD_DIM)] * Z + [shape(SPANS, PIECE, HEAD_DIM)],
        in_specs=[in_smem(), in_vmem(), in_vmem(), in_vmem()],
        out_specs=[in_vmem()] * (Z + 1),
        compiler_params=pltpu.CompilerParams(vmem_limit_bytes=VMEM_LIMIT),
        name="pack",
    )(row, query_rows, key_rows, value_rows)
    return outs[:Z], outs[Z]


STEP = Z // 2
STEP_KEYS = STEP * SPAN
STEPS = 2 * X
TILE = 8
TILES = SPANS // TILE
TILE_ROWS = TILE * PIECE
ROWS = SPANS * PIECE
SMALLEST, LARGEST = 1e-18, 1e30


def attend_kernel(places, ends, row_ref, offset_ref, pieces_ref, *refs):
    sources, refs = refs[: len(places)], refs[len(places) :]
    if ends:
        (total_in, summed_in, shift_ref), refs = refs[:3], refs[3:]
        later_steps, refs = refs[: STEPS - len(places)], refs[STEPS - len(places) :]
        refs = refs[len(refs) - 7 :]
        out_ref, held, rows, total_ref, summed_ref, keys_at, copied = refs
    else:
        total_ref, summed_ref, shift_ref, held, rows, keys_at, copied = refs
    offset = offset_ref[0]

    def place_of(span):
        return lax.rem(span - offset + SPANS, SPANS)

    def note_places(first, found):
        for i, (m, half) in enumerate(found):
            from_x = lax.rem(row_ref[PLACE_X] - m + X, X)
            for u in range(STEP):
                keys_at[first + i, u] = place_of(from_x * Z + row_ref[FROM + half * STEP + u])

    def scores_of(query, keys):
        return lax.dot_general(
            query, keys, (((1,), (1,)), ((), ())), preferred_element_type=jnp.float32
        )

    def values_of(weights, values):
        return jnp.dot(
            weights.astype(jnp.bfloat16), values, preferred_element_type=jnp.float32
        )

    def lanes(weights):
        parts = [weights[:, g : g + HEAD_DIM] for g in range(0, weights.shape[1], HEAD_DIM)]
        return sum(parts[1:], parts[0])

    def tile_rows(tile):
        return pl.ds(pl.multiple_of(tile * TILE_ROWS, TILE_ROWS), TILE_ROWS)

    def row_places(tile):
        return tile * TILE + lax.div(
            lax.broadcasted_iota(jnp.int32, (TILE_ROWS, 1), 0), jnp.int32(PIECE)
        )

    def running(tile):
        query, own = rows[tile_rows(tile), :], row_places(tile)

        def step(t, carry):
            top, total, summed = carry
            key_rows = pl.ds(pl.multiple_of(lax.rem(t, STEP) * SPAN, SPAN), SPAN)
            at = lax.div(t, STEP)
            seen = own >= keys_at[at, lax.rem(t, STEP)]
            scores = jnp.where(seen, scores_of(query, held[at, key_rows, :HEAD_DIM]), NEGATIVE)
            top_new = jnp.maximum(top, jnp.max(scores, axis=1, keepdims=True))
            weights = jnp.where(seen, jnp.exp2((scores - top_new) * SCALE), 0.0)
            factor = jnp.exp2((top - top_new) * SCALE)
            total = total * factor + jnp.sum(weights, axis=1, keepdims=True)
            summed = summed * factor + values_of(weights, held[at, key_rows, HEAD_DIM:])
            return top_new, total, summed

        start = (
            jnp.full((TILE_ROWS, 1), NEGATIVE, jnp.float32),
            jnp.zeros((TILE_ROWS, 1), jnp.float32),
            jnp.zeros((TILE_ROWS, HEAD_DIM), jnp.float32),
        )
        carry = lax.fori_loop(0, SPANS, step, start)
        return carry[2] / carry[1]

    @pl.when(row_ref[ACTIVE] == 1)
    def _():
        steps = len(places)
        for i, source in enumerate(sources):
            pltpu.make_async_copy(source, held.at[i], copied).start()
        for span in range(SPANS):
            at = pl.ds(pl.multiple_of(place_of(span) * PIECE, PIECE), PIECE)
            rows[at, :] = pieces_ref[span]
        note_places(0, places)
        if ends:
            total_ref[...] = total_in[...]
            summed_ref[...] = summed_in[...]
        else:
            total_ref[...] = jnp.zeros_like(total_ref)
            summed_ref[...] = jnp.zeros_like(summed_ref)
        brought = held.at[pl.ds(0, steps)]
        pltpu.make_async_copy(brought, brought, copied).wait()

        if not ends:
            for tile in range(TILES):
                at = slice(tile * TILE_ROWS, (tile + 1) * TILE_ROWS)
                top = jnp.max(
                    scores_of(rows[at, :], held[0, :HEAD_DIM, :HEAD_DIM]), axis=1, keepdims=True
                )
                shift_ref[at, :] = jnp.broadcast_to(top * SCALE, (TILE_ROWS, HEAD_DIM))

        def add(tile, i, masked):
            at = tile_rows(tile)
            scores = scores_of(rows[at, :], held[i, :, :HEAD_DIM])
            shift = shift_ref[at, :1]
            if masked:
                own = row_places(tile)
                weights = []
                for u in range(STEP):
                    hidden = own < keys_at[i, u]
                    part = scores[:, u * SPAN : (u + 1) * SPAN] * SCALE
                    weights.append(jnp.exp2(part - jnp.where(hidden, LARGEST, shift)))
                weights = jnp.concatenate(weights, axis=1)
            else:
                weights = jnp.exp2(scores * SCALE - shift)
            total_ref[at, :] += lanes(weights)
            summed_ref[at, :] += values_of(weights, held[i, :, HEAD_DIM:])

        def one(n, unused):
            tile, i = lax.div(n, steps), lax.rem(n, steps)
            found = [keys_at[i, u] for u in range(STEP)]
            lowest = functools.reduce(jnp.minimum, found)
            highest = functools.reduce(jnp.maximum, found)
            whole = highest <= tile * TILE

            @pl.when(whole)
            def _():
                add(tile, i, False)

            @pl.when(jnp.logical_not(whole) & (lowest < (tile + 1) * TILE))
            def _():
                add(tile, i, True)

            return unused

        lax.fori_loop(0, TILES * steps, one, 0)

        if ends:

            def put(tile, answer):
                for n in range(TILE):
                    slot = lax.rem(offset + (tile * TILE + n + 1), SPANS)
                    out_ref[slot] = answer[n * PIECE : (n + 1) * PIECE].astype(jnp.bfloat16)

            total = jnp.sum(total_ref[...], axis=1, keepdims=True)
            for tile in range(TILES):
                at = slice(tile * TILE_ROWS, (tile + 1) * TILE_ROWS)
                put(tile, summed_ref[at, :] / total[at])

            safe = (jnp.max(total) < LARGEST) & (jnp.min(total) > SMALLEST)

            @pl.when(jnp.logical_not(safe))
            def _():
                for i, source in enumerate(later_steps):
                    pltpu.make_async_copy(source, held.at[steps + i], copied).start()
                brought = held.at[pl.ds(steps, STEPS - steps)]
                pltpu.make_async_copy(brought, brought, copied).wait()
                note_places(steps, NEAR)
                for tile in range(TILES):
                    put(tile, running(tile))


NEAR = ((0, 0), (0, 1), (1, 0), (1, 1), (3, 0), (3, 1))
FAR = ((2, 0), (2, 1))


def attend_near(row, offset, pieces, near):
    held = shape(ROWS, HEAD_DIM, dtype=jnp.float32)
    return pl.pallas_call(
        functools.partial(attend_kernel, NEAR, False),
        out_shape=[held] * 3,
        in_specs=[in_smem(), in_smem(), in_vmem()] + [anywhere()] * len(near),
        out_specs=[in_vmem()] * 3,
        scratch_shapes=[
            pltpu.VMEM((len(near), STEP_KEYS, 2 * HEAD_DIM), jnp.bfloat16),
            pltpu.VMEM((ROWS, HEAD_DIM), jnp.bfloat16),
            pltpu.SMEM((STEPS, STEP), jnp.int32),
            pltpu.SemaphoreType.DMA,
        ],
        compiler_params=pltpu.CompilerParams(vmem_limit_bytes=VMEM_LIMIT),
        name="near",
    )(row, offset, pieces, *near)


def attend_far(row, offset, pieces, far, state, near, others):
    return pl.pallas_call(
        functools.partial(attend_kernel, FAR, True),
        out_shape=shape(SPANS, PIECE, HEAD_DIM),
        in_specs=[in_smem(), in_smem(), in_vmem()]
        + [anywhere()] * len(far)
        + [in_vmem()] * len(state)
        + [anywhere()] * (len(near) + len(others)),
        out_specs=in_vmem(),
        scratch_shapes=[
            pltpu.VMEM((STEPS, STEP_KEYS, 2 * HEAD_DIM), jnp.bfloat16),
            pltpu.VMEM((ROWS, HEAD_DIM), jnp.bfloat16),
            pltpu.VMEM((ROWS, HEAD_DIM), jnp.float32),
            pltpu.VMEM((ROWS, HEAD_DIM), jnp.float32),
            pltpu.SMEM((STEPS, STEP), jnp.int32),
            pltpu.SemaphoreType.DMA,
        ],
        compiler_params=pltpu.CompilerParams(vmem_limit_bytes=VMEM_LIMIT),
        name="far",
    )(row, offset, pieces, *far, *state, *near, *others)


def gather_kernel(row_ref, parts_ref, out_ref):
    for head in range(HERE):
        for x in range(X):
            out_ref[x * PIECE : (x + 1) * PIECE, head * HEAD_DIM : (head + 1) * HEAD_DIM] = (
                parts_ref[x * Z + row_ref[PLANE + head]]
            )


def gather_heads(row, parts):
    return pl.pallas_call(
        gather_kernel,
        out_shape=shape(SPAN, HERE * HEAD_DIM),
        in_specs=[in_smem(), in_vmem()],
        out_specs=in_vmem(),
        compiler_params=pltpu.CompilerParams(vmem_limit_bytes=VMEM_LIMIT),
        name="heads",
    )(row, parts)


def project_kernel(row_ref, rows_ref, weight_ref, out_ref):
    out_ref[0] = jnp.dot(
        rows_ref[...], weight_ref[...], preferred_element_type=jnp.float32
    ).astype(jnp.bfloat16)


def project(row, rows, weight, other):
    wide = weight.shape[1] // (Y * C)

    def weight_at(m, row_ref):
        core = row_ref[CORE]
        core = 1 - core if other else core
        return (0, lax.rem(row_ref[PLACE_Y] + m, Y) * C + core)

    return pl.pallas_call(
        project_kernel,
        out_shape=shape(Y, SPAN, wide),
        grid_spec=pltpu.PrefetchScalarGridSpec(
            num_scalar_prefetch=1,
            grid=(Y,),
            in_specs=[
                pl.BlockSpec((SPAN, HERE * HEAD_DIM), lambda m, row_ref: (0, 0)),
                pl.BlockSpec((HERE * HEAD_DIM, wide), weight_at),
            ],
            out_specs=pl.BlockSpec((1, SPAN, wide), lambda m, row_ref: (m, 0, 0)),
        ),
        compiler_params=pltpu.CompilerParams(vmem_limit_bytes=VMEM_LIMIT),
        name="project",
    )(row, rows, weight)


def body(
    query_rows,
    key_rows,
    value_rows,
    residual_in,
    out_weight,
    time_proj,
    levels,
    timestep_table,
    window_offset,
):
    me = lax.axis_index("tm") * (Y * C) + lax.axis_index("head")
    row = lax.dynamic_slice(jnp.asarray(table()), (me, 0), (1, WIDTH))[0]
    packed, pieces = pack(row, query_rows, key_rows, value_rows)

    arrived = [
        moved(part, plane_pairs(shift)) if shift else part for part, shift in zip(packed, SHIFTS)
    ]
    pieces = lax.all_to_all(pieces, "tm", 0, 0, tiled=True)

    own = [jnp.concatenate(arrived[half * STEP : (half + 1) * STEP]) for half in range(2)]
    back = [moved(part, across_pairs(1)) for part in own]
    ahead = [moved(part, across_pairs(-1)) for part in own]
    far = [moved(ahead[0], across_pairs(-1)), moved(back[1], across_pairs(1))]
    near = own + back + ahead

    next_slot = [
        (device(x, z, y, c), device((x * Z + z + 1) % SPANS // Z, z + 1, y, c)) for x, z, y, c in ALL
    ]
    residual = moved(residual_in, next_slot)
    level = moved(levels, next_slot)

    state = attend_near(row, window_offset, pieces, near)
    answers = attend_far(row, window_offset, pieces, far, state, near, [residual, level])
    answers = lax.all_to_all(answers, "tm", 0, 0, tiled=True)
    attention = gather_heads(row, answers)

    swap = [(device(x, z, y, c), device(x, z, y, 1 - c)) for x, z, y, c in ALL]
    from_core = moved(project(row, attention, out_weight, True), swap)
    kept = project(row, attention, out_weight, False)
    both = [kept[m].astype(jnp.float32) + from_core[m].astype(jnp.float32) for m in range(Y)]
    projected = both[0]
    for m in (2, 1, 3):
        pairs = [(device(x, z, y, c), device(x, z, y + m, c)) for x, z, y, c in ALL]
        projected = projected + moved(both[m].astype(jnp.bfloat16), pairs).astype(jnp.float32)

    half_dim = time_proj.shape[0] // 2
    stamp_value = jnp.sum(
        jnp.where(jnp.arange(timestep_table.shape[0], dtype=jnp.int32) == level[0], timestep_table, 0)
    ).astype(jnp.float32)
    frequency = jnp.exp(-math.log(10000.0) * jnp.arange(half_dim, dtype=jnp.float32) / half_dim)
    angles = stamp_value * frequency
    embedding = jnp.concatenate([jnp.cos(angles), jnp.sin(angles)])[None, :].astype(jnp.bfloat16)
    gate_row = jnp.dot(embedding, time_proj, preferred_element_type=jnp.float32)
    return (residual.astype(jnp.float32) + gate_row * projected).astype(jnp.bfloat16)


def solution(mesh):
    in_specs = (
        P("tm", "head"),
        P("tm", "head"),
        P("tm", "head"),
        P("tm", "head"),
        P("head", None),
        P(None, "head"),
        P("tm"),
        P(),
        P(),
    )
    out_specs = P("tm", "head")
    return jax.shard_map(body, mesh=mesh, in_specs=in_specs, out_specs=out_specs, check_vma=False)
```

```python
import functools
import math

import jax
import jax.numpy as jnp
import numpy as np
from jax import lax
from jax.experimental import pallas as pl
from jax.experimental.pallas import tpu as pltpu
from jax.sharding import PartitionSpec as P

HEAD_DIM = 128
SPAN = 256
X, Z, Y, C = 4, 8, 4, 2
HERE = 5
SPANS = X * Z
NEGATIVE = -1e30
SCALE = math.log2(math.e) / math.sqrt(HEAD_DIM)
MIB = 1024 * 1024

HOST = ((0, 1, 3, 4, 6), (0, 2, 4, 5, 7))
SHIFTS = (0, 4, 1, 7, 3, 5, 2, 6)
AXES = ("tm", "head")
PIECE = SPAN // X


def device(x, z, y, c):
    return ((x % X) * Z + z % Z) * (Y * C) + (y % Y) * C + c


ALL = [(x, z, y, c) for x in range(X) for z in range(Z) for y in range(Y) for c in range(C)]


def plane_pairs(shift):
    return [
        (device(x, z, y, c), device(x, z + shift, y, c))
        for x, z, y, c in ALL
        if (z + shift) % Z in HOST[c]
    ]


def across_pairs(m):
    return [(device(x, z, y, c), device(x + m, z, y, c)) for x, z, y, c in ALL if z in HOST[c]]


HEAD, PLANE, ACTIVE, PLACE_X, PLACE_Y, CORE, SEND, FROM = 0, 8, 13, 14, 15, 16, 17, 25
WIDTH = 64


def table():
    rows = np.zeros((X * Z * Y * C, WIDTH), np.int32)
    for x, z, y, c in ALL:
        row = rows[device(x, z, y, c)]
        for to_z in range(Z):
            row[HEAD + to_z] = HOST[c].index(to_z) if to_z in HOST[c] else -1
        row[PLANE : PLANE + HERE] = HOST[c]
        row[ACTIVE] = int(z in HOST[c])
        row[PLACE_X] = x
        row[PLACE_Y] = y
        row[CORE] = c
        for i, shift in enumerate(SHIFTS):
            row[SEND + i] = row[HEAD + (z + shift) % Z]
            row[FROM + i] = (z - shift) % Z
    return rows


def moved(block, pairs):
    return lax.ppermute(block, AXES, pairs)


def in_vmem():
    return pl.BlockSpec(memory_space=pltpu.VMEM)


def in_smem():
    return pl.BlockSpec(memory_space=pltpu.SMEM)


def anywhere():
    return pl.BlockSpec(memory_space=pl.ANY)


def shape(*dims, dtype=jnp.bfloat16):
    return jax.ShapeDtypeStruct(dims, dtype)


def pack_kernel(rounds, row_ref, key_ref, value_ref, *refs):
    outs = refs[len(refs) - len(rounds) :]
    for i, out in zip(rounds, outs):
        head = row_ref[SEND + i]

        @pl.when(head >= 0)
        def _():
            columns = pl.ds(pl.multiple_of(head * HEAD_DIM, HEAD_DIM), HEAD_DIM)
            out[:, :HEAD_DIM] = key_ref[:, columns]
            out[:, HEAD_DIM:] = value_ref[:, columns]


def pack(row, key_rows, value_rows, rounds, after=()):
    return pl.pallas_call(
        functools.partial(pack_kernel, rounds),
        out_shape=[shape(SPAN, 2 * HEAD_DIM)] * len(rounds),
        in_specs=[in_smem(), in_vmem(), in_vmem()] + [anywhere()] * len(after),
        out_specs=[in_vmem()] * len(rounds),
        compiler_params=pltpu.CompilerParams(vmem_limit_bytes=8 * MIB),
        name="pack",
    )(row, key_rows, value_rows, *after)


def pieces_kernel(row_ref, query_ref, residual_ref, unused_ref, pieces_ref, copy_ref):
    copy_ref[...] = residual_ref[...]
    for z in range(Z):
        head = row_ref[HEAD + z]

        @pl.when(head >= 0)
        def _():
            columns = pl.ds(pl.multiple_of(head * HEAD_DIM, HEAD_DIM), HEAD_DIM)
            for x in range(X):
                pieces_ref[x * Z + z] = query_ref[x * PIECE : (x + 1) * PIECE, columns]


def cut_queries(row, query_rows, residual, after):
    return pl.pallas_call(
        pieces_kernel,
        out_shape=[shape(SPANS, PIECE, HEAD_DIM), shape(*residual.shape)],
        in_specs=[in_smem(), in_vmem(), in_vmem(), anywhere()],
        out_specs=[in_vmem()] * 2,
        compiler_params=pltpu.CompilerParams(vmem_limit_bytes=8 * MIB),
        name="pieces",
    )(row, query_rows, residual, after)


STEP = Z // 2
STEP_KEYS = STEP * SPAN
STEPS = 2 * X
TILE = 8
TILES = SPANS // TILE
TILE_ROWS = TILE * PIECE
ROWS = SPANS * PIECE
SMALLEST, LARGEST = 1e-18, 1e30


def attend_kernel(places, ends, row_ref, offset_ref, pieces_ref, *refs):
    sources, refs = refs[: len(places)], refs[len(places) :]
    if ends:
        (total_in, summed_in, shift_ref), refs = refs[:3], refs[3:]
        later_steps, refs = refs[: STEPS - len(places)], refs[STEPS - len(places) :]
        refs = refs[len(refs) - 7 :]
        out_ref, held, rows, total_ref, summed_ref, keys_at, copied = refs
    else:
        total_ref, summed_ref, shift_ref, held, rows, keys_at, copied = refs
    offset = offset_ref[0]

    def place_of(span):
        return lax.rem(span - offset + SPANS, SPANS)

    def note_places(first, found):
        for i, (m, half) in enumerate(found):
            from_x = lax.rem(row_ref[PLACE_X] - m + X, X)
            for u in range(STEP):
                keys_at[first + i, u] = place_of(from_x * Z + row_ref[FROM + half * STEP + u])

    def scores_of(query, keys):
        return lax.dot_general(
            query, keys, (((1,), (1,)), ((), ())), preferred_element_type=jnp.float32
        )

    def values_of(weights, values):
        return jnp.dot(
            weights.astype(jnp.bfloat16), values, preferred_element_type=jnp.float32
        )

    def lanes(weights):
        parts = [weights[:, g : g + HEAD_DIM] for g in range(0, weights.shape[1], HEAD_DIM)]
        return sum(parts[1:], parts[0])

    def tile_rows(tile):
        return pl.ds(pl.multiple_of(tile * TILE_ROWS, TILE_ROWS), TILE_ROWS)

    def row_places(tile):
        return tile * TILE + lax.div(
            lax.broadcasted_iota(jnp.int32, (TILE_ROWS, 1), 0), jnp.int32(PIECE)
        )

    def running(tile):
        query, own = rows[tile_rows(tile), :], row_places(tile)

        def step(t, carry):
            top, total, summed = carry
            key_rows = pl.ds(pl.multiple_of(lax.rem(t, STEP) * SPAN, SPAN), SPAN)
            at = lax.div(t, STEP)
            seen = own >= keys_at[at, lax.rem(t, STEP)]
            scores = jnp.where(seen, scores_of(query, held[at, key_rows, :HEAD_DIM]), NEGATIVE)
            top_new = jnp.maximum(top, jnp.max(scores, axis=1, keepdims=True))
            weights = jnp.where(seen, jnp.exp2((scores - top_new) * SCALE), 0.0)
            factor = jnp.exp2((top - top_new) * SCALE)
            total = total * factor + jnp.sum(weights, axis=1, keepdims=True)
            summed = summed * factor + values_of(weights, held[at, key_rows, HEAD_DIM:])
            return top_new, total, summed

        start = (
            jnp.full((TILE_ROWS, 1), NEGATIVE, jnp.float32),
            jnp.zeros((TILE_ROWS, 1), jnp.float32),
            jnp.zeros((TILE_ROWS, HEAD_DIM), jnp.float32),
        )
        carry = lax.fori_loop(0, SPANS, step, start)
        return carry[2] / carry[1]

    @pl.when(row_ref[ACTIVE] == 1)
    def _():
        steps = len(places)
        for i, source in enumerate(sources):
            pltpu.make_async_copy(source, held.at[i], copied).start()
        for span in range(SPANS):
            at = pl.ds(pl.multiple_of(place_of(span) * PIECE, PIECE), PIECE)
            rows[at, :] = pieces_ref[span]
        note_places(0, places)
        if ends:
            total_ref[...] = total_in[...]
            summed_ref[...] = summed_in[...]
        else:
            total_ref[...] = jnp.zeros_like(total_ref)
            summed_ref[...] = jnp.zeros_like(summed_ref)
        brought = held.at[pl.ds(0, steps)]
        pltpu.make_async_copy(brought, brought, copied).wait()

        if not ends:
            for tile in range(TILES):
                at = slice(tile * TILE_ROWS, (tile + 1) * TILE_ROWS)
                top = jnp.max(
                    scores_of(rows[at, :], held[0, :HEAD_DIM, :HEAD_DIM]), axis=1, keepdims=True
                )
                shift_ref[at, :] = jnp.broadcast_to(top * SCALE, (TILE_ROWS, HEAD_DIM))

        def add(tile, i, masked):
            at = tile_rows(tile)
            scores = scores_of(rows[at, :], held[i, :, :HEAD_DIM])
            shift = shift_ref[at, :1]
            if masked:
                own = row_places(tile)
                weights = []
                for u in range(STEP):
                    hidden = own < keys_at[i, u]
                    part = scores[:, u * SPAN : (u + 1) * SPAN] * SCALE
                    weights.append(jnp.exp2(part - jnp.where(hidden, LARGEST, shift)))
                weights = jnp.concatenate(weights, axis=1)
            else:
                weights = jnp.exp2(scores * SCALE - shift)
            total_ref[at, :] += lanes(weights)
            summed_ref[at, :] += values_of(weights, held[i, :, HEAD_DIM:])

        def one(n, unused):
            tile, i = lax.div(n, steps), lax.rem(n, steps)
            found = [keys_at[i, u] for u in range(STEP)]
            lowest = functools.reduce(jnp.minimum, found)
            highest = functools.reduce(jnp.maximum, found)
            whole = highest <= tile * TILE

            @pl.when(whole)
            def _():
                add(tile, i, False)

            @pl.when(jnp.logical_not(whole) & (lowest < (tile + 1) * TILE))
            def _():
                add(tile, i, True)

            return unused

        lax.fori_loop(0, TILES * steps, one, 0)

        if ends:

            def put(tile, answer):
                for n in range(TILE):
                    slot = lax.rem(offset + (tile * TILE + n + 1), SPANS)
                    out_ref[slot] = answer[n * PIECE : (n + 1) * PIECE].astype(jnp.bfloat16)

            total = jnp.sum(total_ref[...], axis=1, keepdims=True)
            for tile in range(TILES):
                at = slice(tile * TILE_ROWS, (tile + 1) * TILE_ROWS)
                put(tile, summed_ref[at, :] / total[at])

            safe = (jnp.max(total) < LARGEST) & (jnp.min(total) > SMALLEST)

            @pl.when(jnp.logical_not(safe))
            def _():
                for i, source in enumerate(later_steps):
                    pltpu.make_async_copy(source, held.at[steps + i], copied).start()
                brought = held.at[pl.ds(steps, STEPS - steps)]
                pltpu.make_async_copy(brought, brought, copied).wait()
                note_places(steps, NEAR)
                for tile in range(TILES):
                    put(tile, running(tile))


NEAR = ((0, 0), (0, 1), (1, 0), (1, 1), (3, 0), (3, 1))
FAR = ((2, 0), (2, 1))


def attend_near(row, offset, pieces, near):
    held = shape(ROWS, HEAD_DIM, dtype=jnp.float32)
    return pl.pallas_call(
        functools.partial(attend_kernel, NEAR, False),
        out_shape=[held] * 3,
        in_specs=[in_smem(), in_smem(), in_vmem()] + [anywhere()] * len(near),
        out_specs=[in_vmem()] * 3,
        scratch_shapes=[
            pltpu.VMEM((len(near), STEP_KEYS, 2 * HEAD_DIM), jnp.bfloat16),
            pltpu.VMEM((ROWS, HEAD_DIM), jnp.bfloat16),
            pltpu.SMEM((STEPS, STEP), jnp.int32),
            pltpu.SemaphoreType.DMA,
        ],
        compiler_params=pltpu.CompilerParams(vmem_limit_bytes=28 * MIB),
        name="near",
    )(row, offset, pieces, *near)


def attend_far(row, offset, pieces, far, state, near, others):
    return pl.pallas_call(
        functools.partial(attend_kernel, FAR, True),
        out_shape=shape(SPANS, PIECE, HEAD_DIM),
        in_specs=[in_smem(), in_smem(), in_vmem()]
        + [anywhere()] * len(far)
        + [in_vmem()] * len(state)
        + [anywhere()] * (len(near) + len(others)),
        out_specs=in_vmem(),
        scratch_shapes=[
            pltpu.VMEM((STEPS, STEP_KEYS, 2 * HEAD_DIM), jnp.bfloat16),
            pltpu.VMEM((ROWS, HEAD_DIM), jnp.bfloat16),
            pltpu.VMEM((ROWS, HEAD_DIM), jnp.float32),
            pltpu.VMEM((ROWS, HEAD_DIM), jnp.float32),
            pltpu.SMEM((STEPS, STEP), jnp.int32),
            pltpu.SemaphoreType.DMA,
        ],
        compiler_params=pltpu.CompilerParams(vmem_limit_bytes=28 * MIB),
        name="far",
    )(row, offset, pieces, *far, *state, *near, *others)


def project_kernel(other, row_ref, parts_ref, weight_ref, out_ref, *refs):
    wide = out_ref.shape[2]
    if other:
        rows_ref, held, copied = refs
    else:
        held, copied = refs
    core = 1 - row_ref[CORE] if other else row_ref[CORE]
    copies = []
    for m in range(Y):
        block = lax.rem(row_ref[PLACE_Y] + m, Y) * C + core
        columns = pl.ds(pl.multiple_of(block * wide, wide), wide)
        for k in range(HERE):
            at = pl.ds(k * HEAD_DIM, HEAD_DIM)
            copies.append(
                pltpu.make_async_copy(weight_ref.at[at, columns], held.at[m, at], copied.at[m, k])
            )
            copies[-1].start()
    if other:
        for head in range(HERE):
            for x in range(X):
                rows_ref[x * PIECE : (x + 1) * PIECE, head * HEAD_DIM : (head + 1) * HEAD_DIM] = (
                    parts_ref[x * Z + row_ref[PLANE + head]]
                )
        rows = rows_ref[...]
    else:
        rows = parts_ref[...]
    for m in range(Y):
        for copy in copies[m * HERE : (m + 1) * HERE]:
            copy.wait()
        out_ref[m] = jnp.dot(rows, held[m], preferred_element_type=jnp.float32).astype(jnp.bfloat16)


def project(row, parts, weight, other):
    wide = weight.shape[1] // (Y * C)
    out = shape(Y, SPAN, wide)
    rows = shape(SPAN, HERE * HEAD_DIM)
    return pl.pallas_call(
        functools.partial(project_kernel, other),
        out_shape=[out, rows] if other else out,
        in_specs=[in_smem(), in_vmem(), anywhere()],
        out_specs=[in_vmem(), in_vmem()] if other else in_vmem(),
        scratch_shapes=[
            pltpu.VMEM((Y, HERE * HEAD_DIM, wide), jnp.bfloat16),
            pltpu.SemaphoreType.DMA((Y, HERE)),
        ],
        compiler_params=pltpu.CompilerParams(vmem_limit_bytes=16 * MIB),
        name="project",
    )(row, parts, weight)


def gate_of(level, time_proj, timestep_table):
    half_dim = time_proj.shape[0] // 2
    stamp_value = jnp.sum(
        jnp.where(
            jnp.arange(timestep_table.shape[0], dtype=jnp.int32) == level, timestep_table, 0
        )
    ).astype(jnp.float32)
    frequency = jnp.exp(-math.log(10000.0) * jnp.arange(half_dim, dtype=jnp.float32) / half_dim)
    angles = stamp_value * frequency
    embedding = jnp.concatenate([jnp.cos(angles), jnp.sin(angles)])[None, :].astype(jnp.bfloat16)
    return jnp.dot(embedding, time_proj, preferred_element_type=jnp.float32)


def body(
    query_rows,
    key_rows,
    value_rows,
    residual_in,
    out_weight,
    time_proj,
    levels,
    timestep_table,
    window_offset,
):
    me = lax.axis_index("tm") * (Y * C) + lax.axis_index("head")
    row = lax.dynamic_slice(jnp.asarray(table()), (me, 0), (1, WIDTH))[0]
    first, second = range(STEP), range(STEP, Z)
    packed = pack(row, key_rows, value_rows, first)
    early = [packed[0]] + [moved(packed[i], plane_pairs(SHIFTS[i])) for i in first[1:]]
    packed = pack(row, key_rows, value_rows, second, early[1:])
    late = [moved(part, plane_pairs(SHIFTS[i])) for part, i in zip(packed, second)]
    pieces, residual = cut_queries(row, query_rows, residual_in, packed[0])
    pieces = lax.all_to_all(pieces, "tm", 0, 0, tiled=True)

    own = [jnp.concatenate(early), jnp.concatenate(late)]
    back = [moved(part, across_pairs(1)) for part in own]
    ahead = [moved(part, across_pairs(-1)) for part in own]
    far = [moved(ahead[0], across_pairs(-1)), moved(back[1], across_pairs(1))]
    near = own + back + ahead

    next_slot = [
        (device(x, z, y, c), device((x * Z + z + 1) % SPANS // Z, z + 1, y, c)) for x, z, y, c in ALL
    ]
    residual = moved(residual, next_slot)
    gate_row = gate_of(moved(levels, next_slot)[0], time_proj, timestep_table)

    state = attend_near(row, window_offset, pieces, near)
    answers = attend_far(row, window_offset, pieces, far, state, near, [residual, gate_row])
    answers = lax.all_to_all(answers, "tm", 0, 0, tiled=True)

    swap = [(device(x, z, y, c), device(x, z, y, 1 - c)) for x, z, y, c in ALL]
    leaving, attention = project(row, answers, out_weight, True)
    from_core = moved(leaving, swap)
    kept = project(row, attention, out_weight, False)
    both = [kept[m].astype(jnp.float32) + from_core[m].astype(jnp.float32) for m in range(Y)]
    projected = both[0]
    for m in (2, 1, 3):
        pairs = [(device(x, z, y, c), device(x, z, y + m, c)) for x, z, y, c in ALL]
        projected = projected + moved(both[m].astype(jnp.bfloat16), pairs).astype(jnp.float32)
    return (residual.astype(jnp.float32) + gate_row * projected).astype(jnp.bfloat16)


def solution(mesh):
    in_specs = (
        P("tm", "head"),
        P("tm", "head"),
        P("tm", "head"),
        P("tm", "head"),
        P("head", None),
        P(None, "head"),
        P("tm"),
        P(),
        P(),
    )
    out_specs = P("tm", "head")
    return jax.shard_map(body, mesh=mesh, in_specs=in_specs, out_specs=out_specs, check_vma=False)
```

```python
import functools
import math

import jax
import jax.numpy as jnp
import numpy as np
from jax import lax
from jax.experimental import pallas as pl
from jax.experimental.pallas import tpu as pltpu
from jax.sharding import PartitionSpec as P

HEAD_DIM = 128
SPAN = 256
X, Z, Y, C = 4, 8, 4, 2
HERE = 5
SPANS = X * Z
NEGATIVE = -1e30
SCALE = math.log2(math.e) / math.sqrt(HEAD_DIM)
MIB = 1024 * 1024

HOST = ((0, 1, 3, 4, 6), (0, 2, 4, 5, 7))
SHIFTS = (0, 4, 1, 7, 3, 5, 2, 6)
AXES = ("tm", "head")
PIECE = SPAN // X


def device(x, z, y, c):
    return ((x % X) * Z + z % Z) * (Y * C) + (y % Y) * C + c


ALL = [(x, z, y, c) for x in range(X) for z in range(Z) for y in range(Y) for c in range(C)]


def plane_pairs(shift):
    return [
        (device(x, z, y, c), device(x, z + shift, y, c))
        for x, z, y, c in ALL
        if (z + shift) % Z in HOST[c]
    ]


def across_pairs(m):
    return [(device(x, z, y, c), device(x + m, z, y, c)) for x, z, y, c in ALL if z in HOST[c]]


HEAD, PLANE, ACTIVE, PLACE_X, PLACE_Y, CORE, SEND, FROM = 0, 8, 13, 14, 15, 16, 17, 25
WIDTH = 64


def table():
    rows = np.zeros((X * Z * Y * C, WIDTH), np.int32)
    for x, z, y, c in ALL:
        row = rows[device(x, z, y, c)]
        for to_z in range(Z):
            row[HEAD + to_z] = HOST[c].index(to_z) if to_z in HOST[c] else -1
        row[PLANE : PLANE + HERE] = HOST[c]
        row[ACTIVE] = int(z in HOST[c])
        row[PLACE_X] = x
        row[PLACE_Y] = y
        row[CORE] = c
        for i, shift in enumerate(SHIFTS):
            row[SEND + i] = row[HEAD + (z + shift) % Z]
            row[FROM + i] = (z - shift) % Z
    return rows


def moved(block, pairs):
    return lax.ppermute(block, AXES, pairs)


def in_vmem():
    return pl.BlockSpec(memory_space=pltpu.VMEM)


def in_smem():
    return pl.BlockSpec(memory_space=pltpu.SMEM)


def anywhere():
    return pl.BlockSpec(memory_space=pl.ANY)


def shape(*dims, dtype=jnp.bfloat16):
    return jax.ShapeDtypeStruct(dims, dtype)


def pack_kernel(row_ref, key_ref, value_ref, *refs):
    outs, copied = refs[:Z], refs[Z]

    def copies(i):
        columns = pl.ds(pl.multiple_of(row_ref[SEND + i] * HEAD_DIM, HEAD_DIM), HEAD_DIM)
        return [
            pltpu.make_async_copy(
                ref.at[:, columns], outs[i].at[:, pl.ds(n * HEAD_DIM, HEAD_DIM)], copied.at[i, n]
            )
            for n, ref in enumerate((key_ref, value_ref))
        ]

    for i in range(Z):

        @pl.when(row_ref[SEND + i] >= 0)
        def _():
            for copy in copies(i):
                copy.start()

    for i in range(Z):

        @pl.when(row_ref[SEND + i] >= 0)
        def _():
            for copy in copies(i):
                copy.wait()


def pack(row, key_rows, value_rows):
    return pl.pallas_call(
        pack_kernel,
        out_shape=[shape(SPAN, 2 * HEAD_DIM)] * Z,
        in_specs=[in_smem()] + [pl.BlockSpec(memory_space=pltpu.HBM)] * 2,
        out_specs=[in_vmem()] * Z,
        scratch_shapes=[pltpu.SemaphoreType.DMA((Z, 2))],
        compiler_params=pltpu.CompilerParams(vmem_limit_bytes=8 * MIB),
        name="pack",
    )(row, key_rows, value_rows)


def pieces_kernel(row_ref, query_ref, residual_ref, unused_ref, pieces_ref, copy_ref):
    copy_ref[...] = residual_ref[...]
    for z in range(Z):
        head = row_ref[HEAD + z]

        @pl.when(head >= 0)
        def _():
            columns = pl.ds(pl.multiple_of(head * HEAD_DIM, HEAD_DIM), HEAD_DIM)
            for x in range(X):
                pieces_ref[x * Z + z] = query_ref[x * PIECE : (x + 1) * PIECE, columns]


def cut_queries(row, query_rows, residual, after):
    return pl.pallas_call(
        pieces_kernel,
        out_shape=[shape(SPANS, PIECE, HEAD_DIM), shape(*residual.shape)],
        in_specs=[in_smem(), in_vmem(), in_vmem(), anywhere()],
        out_specs=[in_vmem()] * 2,
        compiler_params=pltpu.CompilerParams(vmem_limit_bytes=8 * MIB),
        name="pieces",
    )(row, query_rows, residual, after)


STEP = Z // 2
STEP_KEYS = STEP * SPAN
STEPS = 2 * X
TILE = 8
TILES = SPANS // TILE
TILE_ROWS = TILE * PIECE
ROWS = SPANS * PIECE
SMALLEST, LARGEST = 1e-18, 1e30


def attend_kernel(places, begins, ends, row_ref, offset_ref, pieces_ref, *refs):
    sources, refs = refs[: len(places)], refs[len(places) :]
    if not begins:
        (total_in, summed_in, shift_ref), refs = refs[:3], refs[3:]
    if ends:
        later_steps, refs = refs[: STEPS - len(places)], refs[STEPS - len(places) :]
        refs = refs[len(refs) - 7 :]
        out_ref, held, rows, total_ref, summed_ref, keys_at, copied = refs
    elif begins:
        total_ref, summed_ref, shift_ref, held, rows, keys_at, copied = refs
    else:
        total_ref, summed_ref, held, rows, keys_at, copied = refs
    offset = offset_ref[0]

    def place_of(span):
        return lax.rem(span - offset + SPANS, SPANS)

    def note_places(first, found):
        for i, (m, half) in enumerate(found):
            from_x = lax.rem(row_ref[PLACE_X] - m + X, X)
            for u in range(STEP):
                keys_at[first + i, u] = place_of(from_x * Z + row_ref[FROM + half * STEP + u])

    def scores_of(query, keys):
        return lax.dot_general(
            query, keys, (((1,), (1,)), ((), ())), preferred_element_type=jnp.float32
        )

    def values_of(weights, values):
        return jnp.dot(
            weights.astype(jnp.bfloat16), values, preferred_element_type=jnp.float32
        )

    def lanes(weights):
        parts = [weights[:, g : g + HEAD_DIM] for g in range(0, weights.shape[1], HEAD_DIM)]
        return sum(parts[1:], parts[0])

    def tile_rows(tile):
        return pl.ds(pl.multiple_of(tile * TILE_ROWS, TILE_ROWS), TILE_ROWS)

    def row_places(tile):
        return tile * TILE + lax.div(
            lax.broadcasted_iota(jnp.int32, (TILE_ROWS, 1), 0), jnp.int32(PIECE)
        )

    def running(tile):
        query, own = rows[tile_rows(tile), :], row_places(tile)

        def step(t, carry):
            top, total, summed = carry
            key_rows = pl.ds(pl.multiple_of(lax.rem(t, STEP) * SPAN, SPAN), SPAN)
            at = lax.div(t, STEP)
            seen = own >= keys_at[at, lax.rem(t, STEP)]
            scores = jnp.where(seen, scores_of(query, held[at, key_rows, :HEAD_DIM]), NEGATIVE)
            top_new = jnp.maximum(top, jnp.max(scores, axis=1, keepdims=True))
            weights = jnp.where(seen, jnp.exp2((scores - top_new) * SCALE), 0.0)
            factor = jnp.exp2((top - top_new) * SCALE)
            total = total * factor + jnp.sum(weights, axis=1, keepdims=True)
            summed = summed * factor + values_of(weights, held[at, key_rows, HEAD_DIM:])
            return top_new, total, summed

        start = (
            jnp.full((TILE_ROWS, 1), NEGATIVE, jnp.float32),
            jnp.zeros((TILE_ROWS, 1), jnp.float32),
            jnp.zeros((TILE_ROWS, HEAD_DIM), jnp.float32),
        )
        carry = lax.fori_loop(0, SPANS, step, start)
        return carry[2] / carry[1]

    @pl.when(row_ref[ACTIVE] == 1)
    def _():
        steps = len(places)
        for i, source in enumerate(sources):
            pltpu.make_async_copy(source, held.at[i], copied).start()
        for span in range(SPANS):
            at = pl.ds(pl.multiple_of(place_of(span) * PIECE, PIECE), PIECE)
            rows[at, :] = pieces_ref[span]
        note_places(0, places)
        if begins:
            total_ref[...] = jnp.zeros_like(total_ref)
            summed_ref[...] = jnp.zeros_like(summed_ref)
        else:
            total_ref[...] = total_in[...]
            summed_ref[...] = summed_in[...]
        brought = held.at[pl.ds(0, steps)]
        pltpu.make_async_copy(brought, brought, copied).wait()

        if begins:
            for tile in range(TILES):
                at = slice(tile * TILE_ROWS, (tile + 1) * TILE_ROWS)
                top = jnp.max(
                    scores_of(rows[at, :], held[0, :HEAD_DIM, :HEAD_DIM]), axis=1, keepdims=True
                )
                shift_ref[at, :] = jnp.broadcast_to(top * SCALE, (TILE_ROWS, HEAD_DIM))

        def add(tile, i, masked):
            at = tile_rows(tile)
            scores = scores_of(rows[at, :], held[i, :, :HEAD_DIM])
            shift = shift_ref[at, :1]
            if masked:
                own = row_places(tile)
                weights = []
                for u in range(STEP):
                    hidden = own < keys_at[i, u]
                    part = scores[:, u * SPAN : (u + 1) * SPAN] * SCALE
                    weights.append(jnp.exp2(part - jnp.where(hidden, LARGEST, shift)))
                weights = jnp.concatenate(weights, axis=1)
            else:
                weights = jnp.exp2(scores * SCALE - shift)
            total_ref[at, :] += lanes(weights)
            summed_ref[at, :] += values_of(weights, held[i, :, HEAD_DIM:])

        def one(n, unused):
            tile, i = lax.div(n, steps), lax.rem(n, steps)
            found = [keys_at[i, u] for u in range(STEP)]
            lowest = functools.reduce(jnp.minimum, found)
            highest = functools.reduce(jnp.maximum, found)
            whole = highest <= tile * TILE

            @pl.when(whole)
            def _():
                add(tile, i, False)

            @pl.when(jnp.logical_not(whole) & (lowest < (tile + 1) * TILE))
            def _():
                add(tile, i, True)

            return unused

        lax.fori_loop(0, TILES * steps, one, 0)

        if ends:

            def put(tile, answer):
                for n in range(TILE):
                    slot = lax.rem(offset + (tile * TILE + n + 1), SPANS)
                    out_ref[slot] = answer[n * PIECE : (n + 1) * PIECE].astype(jnp.bfloat16)

            total = jnp.sum(total_ref[...], axis=1, keepdims=True)
            for tile in range(TILES):
                at = slice(tile * TILE_ROWS, (tile + 1) * TILE_ROWS)
                put(tile, summed_ref[at, :] / total[at])

            safe = (jnp.max(total) < LARGEST) & (jnp.min(total) > SMALLEST)

            @pl.when(jnp.logical_not(safe))
            def _():
                for i, source in enumerate(later_steps):
                    pltpu.make_async_copy(source, held.at[steps + i], copied).start()
                brought = held.at[pl.ds(steps, STEPS - steps)]
                pltpu.make_async_copy(brought, brought, copied).wait()
                note_places(steps, BEHIND + AHEAD)
                for tile in range(TILES):
                    put(tile, running(tile))


BEHIND = ((0, 0), (0, 1), (1, 0), (1, 1))
AHEAD = ((3, 0), (3, 1))
FAR = ((2, 0), (2, 1))


def attend_part(places, row, offset, pieces, sources, state=()):
    held = shape(ROWS, HEAD_DIM, dtype=jnp.float32)
    found = pl.pallas_call(
        functools.partial(attend_kernel, places, not state, False),
        out_shape=[held] * (2 if state else 3),
        in_specs=[in_smem(), in_smem(), in_vmem()]
        + [anywhere()] * len(sources)
        + [in_vmem()] * len(state),
        out_specs=[in_vmem()] * (2 if state else 3),
        scratch_shapes=[
            pltpu.VMEM((len(sources), STEP_KEYS, 2 * HEAD_DIM), jnp.bfloat16),
            pltpu.VMEM((ROWS, HEAD_DIM), jnp.bfloat16),
            pltpu.SMEM((STEPS, STEP), jnp.int32),
            pltpu.SemaphoreType.DMA,
        ],
        compiler_params=pltpu.CompilerParams(vmem_limit_bytes=28 * MIB),
        name="part",
    )(row, offset, pieces, *sources, *state)
    return [*found, state[2]] if state else found


def attend_far(row, offset, pieces, far, state, near, others):
    return pl.pallas_call(
        functools.partial(attend_kernel, FAR, False, True),
        out_shape=shape(SPANS, PIECE, HEAD_DIM),
        in_specs=[in_smem(), in_smem(), in_vmem()]
        + [anywhere()] * len(far)
        + [in_vmem()] * len(state)
        + [anywhere()] * (len(near) + len(others)),
        out_specs=in_vmem(),
        scratch_shapes=[
            pltpu.VMEM((STEPS, STEP_KEYS, 2 * HEAD_DIM), jnp.bfloat16),
            pltpu.VMEM((ROWS, HEAD_DIM), jnp.bfloat16),
            pltpu.VMEM((ROWS, HEAD_DIM), jnp.float32),
            pltpu.VMEM((ROWS, HEAD_DIM), jnp.float32),
            pltpu.SMEM((STEPS, STEP), jnp.int32),
            pltpu.SemaphoreType.DMA,
        ],
        compiler_params=pltpu.CompilerParams(vmem_limit_bytes=28 * MIB),
        name="far",
    )(row, offset, pieces, *far, *state, *near, *others)


def project_kernel(other, places, waits, row_ref, parts_ref, weight_ref, *refs):
    refs = refs[waits:]
    out_ref = refs[0]
    wide = out_ref.shape[2]
    if len(refs) > 1:
        rows_ref = refs[1]
        for head in range(HERE):
            for x in range(X):
                rows_ref[x * PIECE : (x + 1) * PIECE, head * HEAD_DIM : (head + 1) * HEAD_DIM] = (
                    parts_ref[x * Z + row_ref[PLANE + head]]
                )
        rows = rows_ref[...]
    else:
        rows = parts_ref[...]
    core = 1 - row_ref[CORE] if other else row_ref[CORE]
    for n, m in enumerate(places):
        block = lax.rem(row_ref[PLACE_Y] + m, Y) * C + core
        columns = pl.ds(pl.multiple_of(block * wide, HEAD_DIM), wide)
        out_ref[n] = jnp.dot(
            rows, weight_ref[:, columns], preferred_element_type=jnp.float32
        ).astype(jnp.bfloat16)


def project(row, parts, weight, other, places, after=()):
    wide = weight.shape[1] // (Y * C)
    out = shape(len(places), SPAN, wide)
    rows = shape(SPAN, HERE * HEAD_DIM)
    whole = parts.ndim == 3
    return pl.pallas_call(
        functools.partial(project_kernel, other, places, len(after)),
        out_shape=[out, rows] if whole else out,
        in_specs=[in_smem(), in_vmem(), in_vmem()] + [anywhere()] * len(after),
        out_specs=[in_vmem(), in_vmem()] if whole else in_vmem(),
        compiler_params=pltpu.CompilerParams(vmem_limit_bytes=16 * MIB),
        name="project",
    )(row, parts, weight, *after)


def gate_of(level, time_proj, timestep_table):
    half_dim = time_proj.shape[0] // 2
    stamp_value = jnp.sum(
        jnp.where(
            jnp.arange(timestep_table.shape[0], dtype=jnp.int32) == level, timestep_table, 0
        )
    ).astype(jnp.float32)
    frequency = jnp.exp(-math.log(10000.0) * jnp.arange(half_dim, dtype=jnp.float32) / half_dim)
    angles = stamp_value * frequency
    embedding = jnp.concatenate([jnp.cos(angles), jnp.sin(angles)])[None, :].astype(jnp.bfloat16)
    return jnp.dot(embedding, time_proj, preferred_element_type=jnp.float32)


def body(
    query_rows,
    key_rows,
    value_rows,
    residual_in,
    out_weight,
    time_proj,
    levels,
    timestep_table,
    window_offset,
):
    me = lax.axis_index("tm") * (Y * C) + lax.axis_index("head")
    row = lax.dynamic_slice(jnp.asarray(table()), (me, 0), (1, WIDTH))[0]
    packed = pack(row, key_rows, value_rows)
    arrived = [
        moved(part, plane_pairs(shift)) if shift else part for part, shift in zip(packed, SHIFTS)
    ]
    pieces, residual = cut_queries(row, query_rows, residual_in, packed[0])
    pieces = lax.all_to_all(pieces, "tm", 0, 0, tiled=True)

    own = [jnp.concatenate(arrived[half * STEP : (half + 1) * STEP]) for half in range(2)]
    back = [moved(part, across_pairs(1)) for part in own]
    ahead = [moved(part, across_pairs(-1)) for part in own]
    far = [moved(ahead[0], across_pairs(-1)), moved(back[1], across_pairs(1))]

    next_slot = [
        (device(x, z, y, c), device((x * Z + z + 1) % SPANS // Z, z + 1, y, c)) for x, z, y, c in ALL
    ]
    residual = moved(residual, next_slot)
    gate_row = gate_of(moved(levels, next_slot)[0], time_proj, timestep_table)

    state = attend_part(BEHIND, row, window_offset, pieces, own + back)
    state = attend_part(AHEAD, row, window_offset, pieces, ahead, state)
    near = own + back + ahead
    answers = attend_far(row, window_offset, pieces, far, state, near, [residual, gate_row])
    answers = lax.all_to_all(answers, "tm", 0, 0, tiled=True)

    swap = [(device(x, z, y, c), device(x, z, y, 1 - c)) for x, z, y, c in ALL]
    along_y = {m: [(device(x, z, y, c), device(x, z, y + m, c)) for x, z, y, c in ALL] for m in (1, -1)}

    def over_cores(leaving, places, after=()):
        from_core = moved(leaving, swap)
        kept = project(row, attention, out_weight, False, places, after)
        return [
            kept[n].astype(jnp.float32) + from_core[n].astype(jnp.float32)
            for n in range(len(places))
        ]

    leaving, attention = project(row, answers, out_weight, True, (2,))
    (opposite,) = over_cores(leaving, (2,))
    opposite = opposite.astype(jnp.bfloat16)
    half = SPAN // 2
    forward = moved(opposite[:half], along_y[1])
    backward = moved(opposite[half:], along_y[-1])
    leaving = project(row, attention, out_weight, True, (1, 3, 0), [opposite])
    following, preceding, projected = over_cores(leaving, (1, 3, 0), [forward, backward])
    following = jnp.concatenate([following[:half] + forward.astype(jnp.float32), following[half:]])
    preceding = jnp.concatenate([preceding[:half], preceding[half:] + backward.astype(jnp.float32)])
    for share, m in ((following, 1), (preceding, -1)):
        projected = projected + moved(share.astype(jnp.bfloat16), along_y[m]).astype(jnp.float32)
    return (residual.astype(jnp.float32) + gate_row * projected).astype(jnp.bfloat16)


def solution(mesh):
    in_specs = (
        P("tm", "head"),
        P("tm", "head"),
        P("tm", "head"),
        P("tm", "head"),
        P("head", None),
        P(None, "head"),
        P("tm"),
        P(),
        P(),
    )
    out_specs = P("tm", "head")
    return jax.shard_map(body, mesh=mesh, in_specs=in_specs, out_specs=out_specs, check_vma=False)
```

```python
import functools
import math

import jax
import jax.numpy as jnp
import numpy as np
from jax import lax
from jax.experimental import pallas as pl
from jax.experimental.pallas import tpu as pltpu
from jax.sharding import PartitionSpec as P

HEAD_DIM = 128
SPAN = 256
X, Z, Y, C = 4, 8, 4, 2
HERE = 5
SPANS = X * Z
NEGATIVE = -1e30
SCALE = math.log2(math.e) / math.sqrt(HEAD_DIM)
MIB = 1024 * 1024

HOST = ((0, 1, 3, 4, 6), (0, 2, 4, 5, 7))
SHIFTS = (0, 4, 1, 7, 3, 5, 2, 6)
AXES = ("tm", "head")
PIECE = SPAN // X


def device(x, z, y, c):
    return ((x % X) * Z + z % Z) * (Y * C) + (y % Y) * C + c


ALL = [(x, z, y, c) for x in range(X) for z in range(Z) for y in range(Y) for c in range(C)]


def plane_pairs(shift):
    return [
        (device(x, z, y, c), device(x, z + shift, y, c))
        for x, z, y, c in ALL
        if (z + shift) % Z in HOST[c]
    ]


def across_pairs(m):
    return [(device(x, z, y, c), device(x + m, z, y, c)) for x, z, y, c in ALL if z in HOST[c]]


HEAD, PLANE, ACTIVE, PLACE_X, PLACE_Y, CORE, SEND, FROM = 0, 8, 13, 14, 15, 16, 17, 25
WIDTH = 64


def table():
    rows = np.zeros((X * Z * Y * C, WIDTH), np.int32)
    for x, z, y, c in ALL:
        row = rows[device(x, z, y, c)]
        for to_z in range(Z):
            row[HEAD + to_z] = HOST[c].index(to_z) if to_z in HOST[c] else -1
        row[PLANE : PLANE + HERE] = HOST[c]
        row[ACTIVE] = int(z in HOST[c])
        row[PLACE_X] = x
        row[PLACE_Y] = y
        row[CORE] = c
        for i, shift in enumerate(SHIFTS):
            row[SEND + i] = row[HEAD + (z + shift) % Z]
            row[FROM + i] = (z - shift) % Z
    return rows


def moved(block, pairs):
    return lax.ppermute(block, AXES, pairs)


def in_vmem():
    return pl.BlockSpec(memory_space=pltpu.VMEM)


def in_smem():
    return pl.BlockSpec(memory_space=pltpu.SMEM)


def anywhere():
    return pl.BlockSpec(memory_space=pl.ANY)


def shape(*dims, dtype=jnp.bfloat16):
    return jax.ShapeDtypeStruct(dims, dtype)


def pack_kernel(row_ref, key_ref, value_ref, *refs):
    outs, copied = refs[:Z], refs[Z]

    def copies(i):
        columns = pl.ds(pl.multiple_of(row_ref[SEND + i] * HEAD_DIM, HEAD_DIM), HEAD_DIM)
        return [
            pltpu.make_async_copy(
                ref.at[:, columns], outs[i].at[:, pl.ds(n * HEAD_DIM, HEAD_DIM)], copied.at[i, n]
            )
            for n, ref in enumerate((key_ref, value_ref))
        ]

    for i in range(Z):

        @pl.when(row_ref[SEND + i] >= 0)
        def _():
            for copy in copies(i):
                copy.start()

    for i in range(Z):

        @pl.when(row_ref[SEND + i] >= 0)
        def _():
            for copy in copies(i):
                copy.wait()


def pack(row, key_rows, value_rows):
    return pl.pallas_call(
        pack_kernel,
        out_shape=[shape(SPAN, 2 * HEAD_DIM)] * Z,
        in_specs=[in_smem()] + [pl.BlockSpec(memory_space=pltpu.HBM)] * 2,
        out_specs=[in_vmem()] * Z,
        scratch_shapes=[pltpu.SemaphoreType.DMA((Z, 2))],
        compiler_params=pltpu.CompilerParams(vmem_limit_bytes=8 * MIB),
        name="pack",
    )(row, key_rows, value_rows)


def pieces_kernel(row_ref, query_ref, unused_ref, pieces_ref):
    for z in range(Z):
        head = row_ref[HEAD + z]

        @pl.when(head >= 0)
        def _():
            columns = pl.ds(pl.multiple_of(head * HEAD_DIM, HEAD_DIM), HEAD_DIM)
            for x in range(X):
                pieces_ref[x * Z + z] = query_ref[x * PIECE : (x + 1) * PIECE, columns]


def cut_queries(row, query_rows, after):
    return pl.pallas_call(
        pieces_kernel,
        out_shape=shape(SPANS, PIECE, HEAD_DIM),
        in_specs=[in_smem(), in_vmem(), anywhere()],
        out_specs=in_vmem(),
        compiler_params=pltpu.CompilerParams(vmem_limit_bytes=8 * MIB),
        name="pieces",
    )(row, query_rows, after)


STEP = Z // 2
STEP_KEYS = STEP * SPAN
STEPS = 2 * X
TILE = 8
TILES = SPANS // TILE
TILE_ROWS = TILE * PIECE
ROWS = SPANS * PIECE
SMALLEST, LARGEST = 1e-18, 1e30


def attend_kernel(places, begins, ends, row_ref, offset_ref, pieces_ref, *refs):
    sources, refs = refs[: len(places)], refs[len(places) :]
    if not begins:
        (total_in, summed_in, shift_ref), refs = refs[:3], refs[3:]
    if ends:
        later_steps, refs = refs[: STEPS - len(places)], refs[STEPS - len(places) :]
        refs = refs[len(refs) - 7 :]
        out_ref, held, rows, total_ref, summed_ref, keys_at, copied = refs
    elif begins:
        passed, refs = refs[0], refs[1:]
        total_ref, summed_ref, shift_ref, passed_on, held, rows, keys_at, copied, passing = refs
        pass_on = pltpu.make_async_copy(passed, passed_on, passing)
        pass_on.start()
    else:
        total_ref, summed_ref, held, rows, keys_at, copied = refs
    offset = offset_ref[0]

    def place_of(span):
        return lax.rem(span - offset + SPANS, SPANS)

    def note_places(first, found):
        for i, (m, half) in enumerate(found):
            from_x = lax.rem(row_ref[PLACE_X] - m + X, X)
            for u in range(STEP):
                keys_at[first + i, u] = place_of(from_x * Z + row_ref[FROM + half * STEP + u])

    def scores_of(query, keys):
        return lax.dot_general(
            query, keys, (((1,), (1,)), ((), ())), preferred_element_type=jnp.float32
        )

    def values_of(weights, values):
        return jnp.dot(
            weights.astype(jnp.bfloat16), values, preferred_element_type=jnp.float32
        )

    def lanes(weights):
        parts = [weights[:, g : g + HEAD_DIM] for g in range(0, weights.shape[1], HEAD_DIM)]
        return sum(parts[1:], parts[0])

    def tile_rows(tile):
        return pl.ds(pl.multiple_of(tile * TILE_ROWS, TILE_ROWS), TILE_ROWS)

    def row_places(tile):
        return tile * TILE + lax.div(
            lax.broadcasted_iota(jnp.int32, (TILE_ROWS, 1), 0), jnp.int32(PIECE)
        )

    def running(tile):
        query, own = rows[tile_rows(tile), :], row_places(tile)

        def step(t, carry):
            top, total, summed = carry
            key_rows = pl.ds(pl.multiple_of(lax.rem(t, STEP) * SPAN, SPAN), SPAN)
            at = lax.div(t, STEP)
            seen = own >= keys_at[at, lax.rem(t, STEP)]
            scores = jnp.where(seen, scores_of(query, held[at, key_rows, :HEAD_DIM]), NEGATIVE)
            top_new = jnp.maximum(top, jnp.max(scores, axis=1, keepdims=True))
            weights = jnp.where(seen, jnp.exp2((scores - top_new) * SCALE), 0.0)
            factor = jnp.exp2((top - top_new) * SCALE)
            total = total * factor + jnp.sum(weights, axis=1, keepdims=True)
            summed = summed * factor + values_of(weights, held[at, key_rows, HEAD_DIM:])
            return top_new, total, summed

        start = (
            jnp.full((TILE_ROWS, 1), NEGATIVE, jnp.float32),
            jnp.zeros((TILE_ROWS, 1), jnp.float32),
            jnp.zeros((TILE_ROWS, HEAD_DIM), jnp.float32),
        )
        carry = lax.fori_loop(0, SPANS, step, start)
        return carry[2] / carry[1]

    @pl.when(row_ref[ACTIVE] == 1)
    def _():
        steps = len(places)
        for i, source in enumerate(sources):
            pltpu.make_async_copy(source, held.at[i], copied).start()
        for span in range(SPANS):
            at = pl.ds(pl.multiple_of(place_of(span) * PIECE, PIECE), PIECE)
            rows[at, :] = pieces_ref[span]
        note_places(0, places)
        if begins:
            total_ref[...] = jnp.zeros_like(total_ref)
            summed_ref[...] = jnp.zeros_like(summed_ref)
        else:
            total_ref[...] = total_in[...]
            summed_ref[...] = summed_in[...]
        brought = held.at[pl.ds(0, steps)]
        pltpu.make_async_copy(brought, brought, copied).wait()

        if begins:
            for tile in range(TILES):
                at = slice(tile * TILE_ROWS, (tile + 1) * TILE_ROWS)
                top = jnp.max(
                    scores_of(rows[at, :], held[0, :HEAD_DIM, :HEAD_DIM]), axis=1, keepdims=True
                )
                shift_ref[at, :] = jnp.broadcast_to(top * SCALE, (TILE_ROWS, HEAD_DIM))

        def add(tile, i, masked):
            at = tile_rows(tile)
            scores = scores_of(rows[at, :], held[i, :, :HEAD_DIM])
            shift = shift_ref[at, :1]
            if masked:
                own = row_places(tile)
                weights = []
                for u in range(STEP):
                    hidden = own < keys_at[i, u]
                    part = scores[:, u * SPAN : (u + 1) * SPAN] * SCALE
                    weights.append(jnp.exp2(part - jnp.where(hidden, LARGEST, shift)))
                weights = jnp.concatenate(weights, axis=1)
            else:
                weights = jnp.exp2(scores * SCALE - shift)
            total_ref[at, :] += lanes(weights)
            summed_ref[at, :] += values_of(weights, held[i, :, HEAD_DIM:])

        def one(n, unused):
            tile, i = lax.div(n, steps), lax.rem(n, steps)
            found = [keys_at[i, u] for u in range(STEP)]
            lowest = functools.reduce(jnp.minimum, found)
            highest = functools.reduce(jnp.maximum, found)
            whole = highest <= tile * TILE

            @pl.when(whole)
            def _():
                add(tile, i, False)

            @pl.when(jnp.logical_not(whole) & (lowest < (tile + 1) * TILE))
            def _():
                add(tile, i, True)

            return unused

        lax.fori_loop(0, TILES * steps, one, 0)

        if ends:

            def put(tile, answer):
                for n in range(TILE):
                    slot = lax.rem(offset + (tile * TILE + n + 1), SPANS)
                    out_ref[slot] = answer[n * PIECE : (n + 1) * PIECE].astype(jnp.bfloat16)

            total = jnp.sum(total_ref[...], axis=1, keepdims=True)
            for tile in range(TILES):
                at = slice(tile * TILE_ROWS, (tile + 1) * TILE_ROWS)
                put(tile, summed_ref[at, :] / total[at])

            safe = (jnp.max(total) < LARGEST) & (jnp.min(total) > SMALLEST)

            @pl.when(jnp.logical_not(safe))
            def _():
                for i, source in enumerate(later_steps):
                    pltpu.make_async_copy(source, held.at[steps + i], copied).start()
                brought = held.at[pl.ds(steps, STEPS - steps)]
                pltpu.make_async_copy(brought, brought, copied).wait()
                note_places(steps, BEHIND + AHEAD)
                for tile in range(TILES):
                    put(tile, running(tile))

    if begins:
        pass_on.wait()


BEHIND = ((0, 0), (0, 1), (1, 0), (1, 1))
AHEAD = ((3, 0), (3, 1))
FAR = ((2, 0), (2, 1))


def attend_part(places, row, offset, pieces, sources, state=(), passed=None):
    held = shape(ROWS, HEAD_DIM, dtype=jnp.float32)
    begins = not state
    out_specs, outs = [in_vmem()] * 2, [held] * 2
    if begins:
        out_specs, outs = out_specs + [in_vmem(), anywhere()], outs + [held, shape(*passed.shape)]
    found = pl.pallas_call(
        functools.partial(attend_kernel, places, begins, False),
        out_shape=outs,
        in_specs=[in_smem(), in_smem(), in_vmem()]
        + [anywhere()] * len(sources)
        + ([anywhere()] if begins else [in_vmem()] * len(state)),
        out_specs=out_specs,
        scratch_shapes=[
            pltpu.VMEM((len(sources), STEP_KEYS, 2 * HEAD_DIM), jnp.bfloat16),
            pltpu.VMEM((ROWS, HEAD_DIM), jnp.bfloat16),
            pltpu.SMEM((STEPS, STEP), jnp.int32),
            pltpu.SemaphoreType.DMA,
        ]
        + [pltpu.SemaphoreType.DMA] * begins,
        compiler_params=pltpu.CompilerParams(vmem_limit_bytes=28 * MIB),
        name="part",
    )(row, offset, pieces, *sources, *((passed,) if begins else state))
    return found if begins else [*found, state[2]]


def attend_far(row, offset, pieces, far, state, near, others):
    return pl.pallas_call(
        functools.partial(attend_kernel, FAR, False, True),
        out_shape=shape(SPANS, PIECE, HEAD_DIM),
        in_specs=[in_smem(), in_smem(), in_vmem()]
        + [anywhere()] * len(far)
        + [in_vmem()] * len(state)
        + [anywhere()] * (len(near) + len(others)),
        out_specs=in_vmem(),
        scratch_shapes=[
            pltpu.VMEM((STEPS, STEP_KEYS, 2 * HEAD_DIM), jnp.bfloat16),
            pltpu.VMEM((ROWS, HEAD_DIM), jnp.bfloat16),
            pltpu.VMEM((ROWS, HEAD_DIM), jnp.float32),
            pltpu.VMEM((ROWS, HEAD_DIM), jnp.float32),
            pltpu.SMEM((STEPS, STEP), jnp.int32),
            pltpu.SemaphoreType.DMA,
        ],
        compiler_params=pltpu.CompilerParams(vmem_limit_bytes=28 * MIB),
        name="far",
    )(row, offset, pieces, *far, *state, *near, *others)


def project_kernel(other, places, waits, row_ref, parts_ref, weight_ref, *refs):
    refs = refs[waits:]
    out_ref = refs[0]
    wide = out_ref.shape[2]
    if len(refs) > 1:
        rows_ref = refs[1]
        for head in range(HERE):
            for x in range(X):
                rows_ref[x * PIECE : (x + 1) * PIECE, head * HEAD_DIM : (head + 1) * HEAD_DIM] = (
                    parts_ref[x * Z + row_ref[PLANE + head]]
                )
        rows = rows_ref[...]
    else:
        rows = parts_ref[...]
    core = 1 - row_ref[CORE] if other else row_ref[CORE]
    for n, m in enumerate(places):
        block = lax.rem(row_ref[PLACE_Y] + m, Y) * C + core
        columns = pl.ds(pl.multiple_of(block * wide, HEAD_DIM), wide)
        out_ref[n] = jnp.dot(
            rows, weight_ref[:, columns], preferred_element_type=jnp.float32
        ).astype(jnp.bfloat16)


def project(row, parts, weight, other, places, after=()):
    wide = weight.shape[1] // (Y * C)
    out = shape(len(places), SPAN, wide)
    rows = shape(SPAN, HERE * HEAD_DIM)
    whole = parts.ndim == 3
    return pl.pallas_call(
        functools.partial(project_kernel, other, places, len(after)),
        out_shape=[out, rows] if whole else out,
        in_specs=[in_smem(), in_vmem(), in_vmem()] + [anywhere()] * len(after),
        out_specs=[in_vmem(), in_vmem()] if whole else in_vmem(),
        compiler_params=pltpu.CompilerParams(vmem_limit_bytes=16 * MIB),
        name="project",
    )(row, parts, weight, *after)


def embedding_of(level, timestep_table, half_dim):
    stamp_value = jnp.sum(
        jnp.where(
            jnp.arange(timestep_table.shape[0], dtype=jnp.int32) == level, timestep_table, 0
        )
    ).astype(jnp.float32)
    frequency = jnp.exp(-math.log(10000.0) * jnp.arange(half_dim, dtype=jnp.float32) / half_dim)
    angles = stamp_value * frequency
    return jnp.concatenate([jnp.cos(angles), jnp.sin(angles)])[None, :].astype(jnp.bfloat16)


def body(
    query_rows,
    key_rows,
    value_rows,
    residual_in,
    out_weight,
    time_proj,
    levels,
    timestep_table,
    window_offset,
):
    me = lax.axis_index("tm") * (Y * C) + lax.axis_index("head")
    row = lax.dynamic_slice(jnp.asarray(table()), (me, 0), (1, WIDTH))[0]
    packed = pack(row, key_rows, value_rows)
    arrived = [
        moved(part, plane_pairs(shift)) if shift else part for part, shift in zip(packed, SHIFTS)
    ]

    own = [jnp.concatenate(arrived[half * STEP : (half + 1) * STEP]) for half in range(2)]
    back = [moved(part, across_pairs(1)) for part in own]
    ahead = [moved(part, across_pairs(-1)) for part in own]
    pieces = cut_queries(row, query_rows, own[1])
    pieces = lax.all_to_all(pieces, "tm", 0, 0, tiled=True)
    far = [moved(ahead[0], across_pairs(-1)), moved(back[1], across_pairs(1))]

    freq_dim = time_proj.shape[0]
    embedding = embedding_of(levels[0], timestep_table, freq_dim // 2)
    below = jnp.pad(embedding, ((0, 15), (0, residual_in.shape[1] - freq_dim)))
    passed = jnp.concatenate([residual_in, below])
    next_slot = [
        (device(x, z, y, c), device((x * Z + z + 1) % SPANS // Z, z + 1, y, c)) for x, z, y, c in ALL
    ]
    *state, passed = attend_part(BEHIND, row, window_offset, pieces, own + back, passed=passed)
    passed = moved(passed, next_slot)
    residual, embedding = passed[:SPAN], passed[SPAN : SPAN + 1, :freq_dim]
    gate_row = jnp.dot(embedding, time_proj, preferred_element_type=jnp.float32)

    state = attend_part(AHEAD, row, window_offset, pieces, ahead, state)
    near = own + back + ahead
    answers = attend_far(row, window_offset, pieces, far, state, near, [passed])
    answers = lax.all_to_all(answers, "tm", 0, 0, tiled=True)

    swap = [(device(x, z, y, c), device(x, z, y, 1 - c)) for x, z, y, c in ALL]
    along_y = {m: [(device(x, z, y, c), device(x, z, y + m, c)) for x, z, y, c in ALL] for m in (1, -1)}

    def over_cores(leaving, places, after=()):
        from_core = moved(leaving, swap)
        kept = project(row, attention, out_weight, False, places, after)
        return [
            kept[n].astype(jnp.float32) + from_core[n].astype(jnp.float32)
            for n in range(len(places))
        ]

    leaving, attention = project(row, answers, out_weight, True, (2,))
    (opposite,) = over_cores(leaving, (2,))
    opposite = opposite.astype(jnp.bfloat16)
    half = SPAN // 2
    forward = moved(opposite[:half], along_y[1])
    backward = moved(opposite[half:], along_y[-1])
    leaving = project(row, attention, out_weight, True, (1, 3, 0), [opposite])
    following, preceding, projected = over_cores(leaving, (1, 3, 0), [forward, backward])
    following = jnp.concatenate([following[:half] + forward.astype(jnp.float32), following[half:]])
    preceding = jnp.concatenate([preceding[:half], preceding[half:] + backward.astype(jnp.float32)])
    for share, m in ((following, 1), (preceding, -1)):
        projected = projected + moved(share.astype(jnp.bfloat16), along_y[m]).astype(jnp.float32)
    return (residual.astype(jnp.float32) + gate_row * projected).astype(jnp.bfloat16)


def solution(mesh):
    in_specs = (
        P("tm", "head"),
        P("tm", "head"),
        P("tm", "head"),
        P("tm", "head"),
        P("head", None),
        P(None, "head"),
        P("tm"),
        P(),
        P(),
    )
    out_specs = P("tm", "head")
    return jax.shard_map(body, mesh=mesh, in_specs=in_specs, out_specs=out_specs, check_vma=False)
```

```python
import functools
import math

import jax
import jax.numpy as jnp
import numpy as np
from jax import lax
from jax.experimental import pallas as pl
from jax.experimental.pallas import tpu as pltpu
from jax.sharding import PartitionSpec as P

HEAD_DIM = 128
SPAN = 256
X, Z, Y, C = 4, 8, 4, 2
HERE = 5
SPANS = X * Z
NEGATIVE = -1e30
SCALE = math.log2(math.e) / math.sqrt(HEAD_DIM)
MIB = 1024 * 1024

HOST = ((0, 1, 3, 4, 6), (0, 2, 4, 5, 7))
SHIFTS = (0, 4, 1, 7, 3, 5, 2, 6)
AXES = ("tm", "head")
PIECE = SPAN // X


def device(x, z, y, c):
    return ((x % X) * Z + z % Z) * (Y * C) + (y % Y) * C + c


ALL = [(x, z, y, c) for x in range(X) for z in range(Z) for y in range(Y) for c in range(C)]


def plane_pairs(shift):
    return [
        (device(x, z, y, c), device(x, z + shift, y, c))
        for x, z, y, c in ALL
        if (z + shift) % Z in HOST[c]
    ]


def across_pairs(m):
    return [(device(x, z, y, c), device(x + m, z, y, c)) for x, z, y, c in ALL if z in HOST[c]]


HEAD, PLANE, ACTIVE, PLACE_X, PLACE_Y, CORE, SEND, FROM = 0, 8, 13, 14, 15, 16, 17, 25
WIDTH = 64


def table():
    rows = np.zeros((X * Z * Y * C, WIDTH), np.int32)
    for x, z, y, c in ALL:
        row = rows[device(x, z, y, c)]
        for to_z in range(Z):
            row[HEAD + to_z] = HOST[c].index(to_z) if to_z in HOST[c] else -1
        row[PLANE : PLANE + HERE] = HOST[c]
        row[ACTIVE] = int(z in HOST[c])
        row[PLACE_X] = x
        row[PLACE_Y] = y
        row[CORE] = c
        for i, shift in enumerate(SHIFTS):
            row[SEND + i] = row[HEAD + (z + shift) % Z]
            row[FROM + i] = (z - shift) % Z
    return rows


def moved(block, pairs):
    return lax.ppermute(block, AXES, pairs)


def in_vmem():
    return pl.BlockSpec(memory_space=pltpu.VMEM)


def in_smem():
    return pl.BlockSpec(memory_space=pltpu.SMEM)


def anywhere():
    return pl.BlockSpec(memory_space=pl.ANY)


def shape(*dims, dtype=jnp.bfloat16):
    return jax.ShapeDtypeStruct(dims, dtype)


def pack_kernel(key_ref, value_ref, *refs):
    outs, copied = refs[:Z], refs[Z]
    z = lax.rem(lax.axis_index("tm"), Z)
    core = lax.rem(lax.axis_index("head"), C)

    hosted = [sum((HOST[c].index(to_z) + 8) << (4 * to_z) for to_z in HOST[c]) for c in range(C)]
    hosted = [have - (1 << 32) if have >= 1 << 31 else have for have in hosted]
    hosted = jnp.where(core == 0, jnp.int32(hosted[0]), jnp.int32(hosted[1]))
    heads = [
        lax.shift_right_logical(hosted, 4 * lax.rem(z + shift, Z)) & 15 for shift in SHIFTS
    ]

    def copies(i):
        columns = pl.ds(pl.multiple_of((heads[i] & 7) * HEAD_DIM, HEAD_DIM), HEAD_DIM)
        return [
            pltpu.make_async_copy(
                ref.at[:, columns], outs[i].at[:, pl.ds(n * HEAD_DIM, HEAD_DIM)], copied.at[i, n]
            )
            for n, ref in enumerate((key_ref, value_ref))
        ]

    for i in range(Z):

        @pl.when(heads[i] >= 8)
        def _():
            for copy in copies(i):
                copy.start()

    for i in range(Z):

        @pl.when(heads[i] >= 8)
        def _():
            for copy in copies(i):
                copy.wait()


def pack(key_rows, value_rows):
    return pl.pallas_call(
        pack_kernel,
        out_shape=[shape(SPAN, 2 * HEAD_DIM)] * Z,
        in_specs=[anywhere()] * 2,
        out_specs=[in_vmem()] * Z,
        scratch_shapes=[pltpu.SemaphoreType.DMA((Z, 2))],
        compiler_params=pltpu.CompilerParams(vmem_limit_bytes=8 * MIB),
        name="pack",
    )(key_rows, value_rows)


def pieces_kernel(row_ref, query_ref, unused_ref, pieces_ref):
    for z in range(Z):
        head = row_ref[HEAD + z]

        @pl.when(head >= 0)
        def _():
            columns = pl.ds(pl.multiple_of(head * HEAD_DIM, HEAD_DIM), HEAD_DIM)
            for x in range(X):
                pieces_ref[x * Z + z] = query_ref[x * PIECE : (x + 1) * PIECE, columns]


def cut_queries(row, query_rows, after):
    return pl.pallas_call(
        pieces_kernel,
        out_shape=shape(SPANS, PIECE, HEAD_DIM),
        in_specs=[in_smem(), in_vmem(), anywhere()],
        out_specs=in_vmem(),
        compiler_params=pltpu.CompilerParams(vmem_limit_bytes=8 * MIB),
        name="pieces",
    )(row, query_rows, after)


STEP = Z // 2
STEP_KEYS = STEP * SPAN
STEPS = 2 * X
TILE = 8
TILES = SPANS // TILE
TILE_ROWS = TILE * PIECE
ROWS = SPANS * PIECE
SMALLEST, LARGEST = 1e-18, 1e30
HALF_FREQ = 128
BELOW = 16


def attend_kernel(places, begins, ends, row_ref, offset_ref, pieces_ref, *refs):
    sources, refs = refs[: len(places)], refs[len(places) :]
    if not begins:
        (total_in, summed_in, shift_ref), refs = refs[:3], refs[3:]
    if ends:
        later_steps, refs = refs[: STEPS - len(places)], refs[STEPS - len(places) :]
        refs = refs[len(refs) - 7 :]
        out_ref, held, rows, total_ref, summed_ref, keys_at, copied = refs
    elif begins:
        (residual_ref, level_ref, table_ref), refs = refs[:3], refs[3:]
        total_ref, summed_ref, shift_ref, passed_on, held, rows, keys_at, copied = refs[:8]
        below, passing = refs[8:]
        pass_on = [
            pltpu.make_async_copy(residual_ref, passed_on.at[pl.ds(0, SPAN)], passing.at[0]),
            pltpu.make_async_copy(below, passed_on.at[pl.ds(SPAN, BELOW)], passing.at[1]),
        ]
        pass_on[0].start()
        steps_of = lax.broadcasted_iota(jnp.int32, (BELOW, HEAD_DIM), 1).astype(jnp.float32)
        stamp = table_ref[level_ref[0]].astype(jnp.float32)
        angles = stamp * jnp.exp(-math.log(10000.0) * steps_of / HALF_FREQ)
        below[:, :HALF_FREQ] = jnp.cos(angles).astype(jnp.bfloat16)
        below[:, HALF_FREQ : 2 * HALF_FREQ] = jnp.sin(angles).astype(jnp.bfloat16)
        below[:, 2 * HALF_FREQ :] = jnp.zeros_like(below[:, 2 * HALF_FREQ :])
        pass_on[1].start()
    else:
        total_ref, summed_ref, held, rows, keys_at, copied = refs
    offset = offset_ref[0]

    def place_of(span):
        return lax.rem(span - offset + SPANS, SPANS)

    def note_places(first, found):
        for i, (m, half) in enumerate(found):
            from_x = lax.rem(row_ref[PLACE_X] - m + X, X)
            for u in range(STEP):
                keys_at[first + i, u] = place_of(from_x * Z + row_ref[FROM + half * STEP + u])

    def scores_of(query, keys):
        return lax.dot_general(
            query, keys, (((1,), (1,)), ((), ())), preferred_element_type=jnp.float32
        )

    def values_of(weights, values):
        return jnp.dot(
            weights.astype(jnp.bfloat16), values, preferred_element_type=jnp.float32
        )

    def lanes(weights):
        parts = [weights[:, g : g + HEAD_DIM] for g in range(0, weights.shape[1], HEAD_DIM)]
        return sum(parts[1:], parts[0])

    def tile_rows(tile):
        return pl.ds(pl.multiple_of(tile * TILE_ROWS, TILE_ROWS), TILE_ROWS)

    def row_places(tile):
        return tile * TILE + lax.div(
            lax.broadcasted_iota(jnp.int32, (TILE_ROWS, 1), 0), jnp.int32(PIECE)
        )

    def running(tile):
        query, own = rows[tile_rows(tile), :], row_places(tile)

        def step(t, carry):
            top, total, summed = carry
            key_rows = pl.ds(pl.multiple_of(lax.rem(t, STEP) * SPAN, SPAN), SPAN)
            at = lax.div(t, STEP)
            seen = own >= keys_at[at, lax.rem(t, STEP)]
            scores = jnp.where(seen, scores_of(query, held[at, key_rows, :HEAD_DIM]), NEGATIVE)
            top_new = jnp.maximum(top, jnp.max(scores, axis=1, keepdims=True))
            weights = jnp.where(seen, jnp.exp2((scores - top_new) * SCALE), 0.0)
            factor = jnp.exp2((top - top_new) * SCALE)
            total = total * factor + jnp.sum(weights, axis=1, keepdims=True)
            summed = summed * factor + values_of(weights, held[at, key_rows, HEAD_DIM:])
            return top_new, total, summed

        start = (
            jnp.full((TILE_ROWS, 1), NEGATIVE, jnp.float32),
            jnp.zeros((TILE_ROWS, 1), jnp.float32),
            jnp.zeros((TILE_ROWS, HEAD_DIM), jnp.float32),
        )
        carry = lax.fori_loop(0, SPANS, step, start)
        return carry[2] / carry[1]

    @pl.when(row_ref[ACTIVE] == 1)
    def _():
        steps = len(places)
        for i, source in enumerate(sources):
            pltpu.make_async_copy(source, held.at[i], copied.at[i]).start()
        for span in range(SPANS):
            at = pl.ds(pl.multiple_of(place_of(span) * PIECE, PIECE), PIECE)
            rows[at, :] = pieces_ref[span]
        note_places(0, places)
        if begins:
            total_ref[...] = jnp.zeros_like(total_ref)
            summed_ref[...] = jnp.zeros_like(summed_ref)
        else:
            total_ref[...] = total_in[...]
            summed_ref[...] = summed_in[...]

        def wait_for(i):
            pltpu.make_async_copy(held.at[i], held.at[i], copied.at[i]).wait()

        if begins:
            wait_for(0)
            for tile in range(TILES):
                at = slice(tile * TILE_ROWS, (tile + 1) * TILE_ROWS)
                top = jnp.max(
                    scores_of(rows[at, :], held[0, :HEAD_DIM, :HEAD_DIM]), axis=1, keepdims=True
                )
                shift_ref[at, :] = jnp.broadcast_to(top * SCALE, (TILE_ROWS, HEAD_DIM))

        def add(tile, i, masked):
            at = tile_rows(tile)
            scores = scores_of(rows[at, :], held[i, :, :HEAD_DIM])
            shift = shift_ref[at, :1]
            if masked:
                own = row_places(tile)
                weights = []
                for u in range(STEP):
                    hidden = own < keys_at[i, u]
                    part = scores[:, u * SPAN : (u + 1) * SPAN] * SCALE
                    weights.append(jnp.exp2(part - jnp.where(hidden, LARGEST, shift)))
                weights = jnp.concatenate(weights, axis=1)
            else:
                weights = jnp.exp2(scores * SCALE - shift)
            total_ref[at, :] += lanes(weights)
            summed_ref[at, :] += values_of(weights, held[i, :, HEAD_DIM:])

        def one(n, unused):
            i, tile = lax.div(n, TILES), lax.rem(n, TILES)

            @pl.when((tile == 0) & (i >= int(begins)))
            def _():
                wait_for(i)

            found = [keys_at[i, u] for u in range(STEP)]
            lowest = functools.reduce(jnp.minimum, found)
            highest = functools.reduce(jnp.maximum, found)
            whole = highest <= tile * TILE

            @pl.when(whole)
            def _():
                add(tile, i, False)

            @pl.when(jnp.logical_not(whole) & (lowest < (tile + 1) * TILE))
            def _():
                add(tile, i, True)

            return unused

        lax.fori_loop(0, TILES * steps, one, 0)

        if ends:

            def put(tile, answer):
                for n in range(TILE):
                    slot = lax.rem(offset + (tile * TILE + n + 1), SPANS)
                    out_ref[slot] = answer[n * PIECE : (n + 1) * PIECE].astype(jnp.bfloat16)

            total = jnp.sum(total_ref[...], axis=1, keepdims=True)
            for tile in range(TILES):
                at = slice(tile * TILE_ROWS, (tile + 1) * TILE_ROWS)
                put(tile, summed_ref[at, :] / total[at])

            safe = (jnp.max(total) < LARGEST) & (jnp.min(total) > SMALLEST)

            @pl.when(jnp.logical_not(safe))
            def _():
                for i, source in enumerate(later_steps, steps):
                    pltpu.make_async_copy(source, held.at[i], copied.at[i]).start()
                for i in range(steps, STEPS):
                    wait_for(i)
                note_places(steps, BEHIND + AHEAD)
                for tile in range(TILES):
                    put(tile, running(tile))

    if begins:
        for copy in pass_on:
            copy.wait()


BEHIND = ((0, 0), (0, 1), (1, 0), (1, 1))
AHEAD = ((3, 0), (3, 1))
FAR = ((2, 0), (2, 1))


def attend_part(places, row, offset, pieces, sources, state=(), residual=None, level=None, table=None):
    held = shape(ROWS, HEAD_DIM, dtype=jnp.float32)
    begins = not state
    out_specs, outs = [in_vmem()] * 2, [held] * 2
    scratch = [
        pltpu.VMEM((len(sources), STEP_KEYS, 2 * HEAD_DIM), jnp.bfloat16),
        pltpu.VMEM((ROWS, HEAD_DIM), jnp.bfloat16),
        pltpu.SMEM((STEPS, STEP), jnp.int32),
        pltpu.SemaphoreType.DMA((STEPS,)),
    ]
    if begins:
        wide = residual.shape[1]
        out_specs = out_specs + [in_vmem(), anywhere()]
        outs = outs + [held, shape(SPAN + BELOW, wide)]
        scratch += [pltpu.VMEM((BELOW, wide), jnp.bfloat16), pltpu.SemaphoreType.DMA((2,))]
    found = pl.pallas_call(
        functools.partial(attend_kernel, places, begins, False),
        out_shape=outs,
        in_specs=[in_smem(), in_smem(), in_vmem()]
        + [anywhere()] * len(sources)
        + ([anywhere(), in_smem(), in_smem()] if begins else [in_vmem()] * len(state)),
        out_specs=out_specs,
        scratch_shapes=scratch,
        compiler_params=pltpu.CompilerParams(vmem_limit_bytes=28 * MIB),
        name="part",
    )(row, offset, pieces, *sources, *((residual, level, table) if begins else state))
    return found if begins else [*found, state[2]]


def attend_far(row, offset, pieces, far, state, near):
    return pl.pallas_call(
        functools.partial(attend_kernel, FAR, False, True),
        out_shape=shape(SPANS, PIECE, HEAD_DIM),
        in_specs=[in_smem(), in_smem(), in_vmem()]
        + [anywhere()] * len(far)
        + [in_vmem()] * len(state)
        + [anywhere()] * len(near),
        out_specs=in_vmem(),
        scratch_shapes=[
            pltpu.VMEM((STEPS, STEP_KEYS, 2 * HEAD_DIM), jnp.bfloat16),
            pltpu.VMEM((ROWS, HEAD_DIM), jnp.bfloat16),
            pltpu.VMEM((ROWS, HEAD_DIM), jnp.float32),
            pltpu.VMEM((ROWS, HEAD_DIM), jnp.float32),
            pltpu.SMEM((STEPS, STEP), jnp.int32),
            pltpu.SemaphoreType.DMA((STEPS,)),
        ],
        compiler_params=pltpu.CompilerParams(vmem_limit_bytes=28 * MIB),
        name="far",
    )(row, offset, pieces, *far, *state, *near)


def share_of(row_ref, rows, weight_ref, out_ref, other, places):
    wide = out_ref.shape[2]
    core = 1 - row_ref[CORE] if other else row_ref[CORE]
    for n, m in enumerate(places):
        block = lax.rem(row_ref[PLACE_Y] + m, Y) * C + core
        columns = pl.ds(pl.multiple_of(block * wide, HEAD_DIM), wide)
        out_ref[n] = jnp.dot(
            rows, weight_ref[:, columns], preferred_element_type=jnp.float32
        ).astype(jnp.bfloat16)


def first_kernel(row_ref, parts_ref, weight_ref, passed_ref, out_ref, rows_ref, passed_on, passing):
    pass_on = pltpu.make_async_copy(passed_ref, passed_on, passing)
    pass_on.start()
    for head in range(HERE):
        for x in range(X):
            rows_ref[x * PIECE : (x + 1) * PIECE, head * HEAD_DIM : (head + 1) * HEAD_DIM] = (
                parts_ref[x * Z + row_ref[PLANE + head]]
            )
    share_of(row_ref, rows_ref[...], weight_ref, out_ref, True, (2,))
    pass_on.wait()


def project_first(row, parts, weight, passed):
    wide = weight.shape[1] // (Y * C)
    return pl.pallas_call(
        first_kernel,
        out_shape=[shape(1, SPAN, wide), shape(SPAN, HERE * HEAD_DIM), shape(*passed.shape)],
        in_specs=[in_smem(), in_vmem(), in_vmem(), in_vmem()],
        out_specs=[in_vmem()] * 3,
        scratch_shapes=[pltpu.SemaphoreType.DMA],
        compiler_params=pltpu.CompilerParams(vmem_limit_bytes=16 * MIB),
        name="first",
    )(row, parts, weight, passed)


def project_kernel(other, places, waits, row_ref, rows_ref, weight_ref, *refs):
    share_of(row_ref, rows_ref[...], weight_ref, refs[waits], other, places)


def project(row, rows, weight, other, places, after=()):
    return pl.pallas_call(
        functools.partial(project_kernel, other, places, len(after)),
        out_shape=shape(len(places), SPAN, weight.shape[1] // (Y * C)),
        in_specs=[in_smem(), in_vmem(), in_vmem()] + [anywhere()] * len(after),
        out_specs=in_vmem(),
        compiler_params=pltpu.CompilerParams(vmem_limit_bytes=16 * MIB),
        name="project",
    )(row, rows, weight, *after)


def body(
    query_rows,
    key_rows,
    value_rows,
    residual_in,
    out_weight,
    time_proj,
    levels,
    timestep_table,
    window_offset,
):
    me = lax.axis_index("tm") * (Y * C) + lax.axis_index("head")
    row = lax.dynamic_slice(jnp.asarray(table()), (me, 0), (1, WIDTH))[0]
    packed = pack(key_rows, value_rows)
    arrived = [
        moved(part, plane_pairs(shift)) if shift else part for part, shift in zip(packed, SHIFTS)
    ]

    own = [jnp.concatenate(arrived[half * STEP : (half + 1) * STEP]) for half in range(2)]
    back = [moved(part, across_pairs(1)) for part in own]
    ahead = [moved(part, across_pairs(-1)) for part in own]
    pieces = cut_queries(row, query_rows, own[1])
    pieces = lax.all_to_all(pieces, "tm", 0, 0, tiled=True)
    far = [moved(ahead[0], across_pairs(-1)), moved(back[1], across_pairs(1))]

    *state, passed = attend_part(
        BEHIND, row, window_offset, pieces, own + back, (), residual_in, levels, timestep_table
    )
    state = attend_part(AHEAD, row, window_offset, pieces, ahead, state)
    near = own + back + ahead
    answers = attend_far(row, window_offset, pieces, far, state, near)
    answers = lax.all_to_all(answers, "tm", 0, 0, tiled=True)

    swap = [(device(x, z, y, c), device(x, z, y, 1 - c)) for x, z, y, c in ALL]
    along_y = {m: [(device(x, z, y, c), device(x, z, y + m, c)) for x, z, y, c in ALL] for m in (1, -1)}

    def over_cores(leaving, places, after=()):
        from_core = moved(leaving, swap)
        kept = project(row, attention, out_weight, False, places, after)
        return [
            kept[n].astype(jnp.float32) + from_core[n].astype(jnp.float32)
            for n in range(len(places))
        ]

    leaving, attention, passed = project_first(row, answers, out_weight, passed)
    next_slot = [
        (device(x, z, y, c), device((x * Z + z + 1) % SPANS // Z, z + 1, y, c)) for x, z, y, c in ALL
    ]
    passed = moved(passed, next_slot)
    residual, embedding = passed[:SPAN], passed[SPAN : SPAN + 1, : time_proj.shape[0]]
    gate_row = jnp.dot(embedding, time_proj, preferred_element_type=jnp.float32)

    (opposite,) = over_cores(leaving, (2,))
    opposite = opposite.astype(jnp.bfloat16)
    half = SPAN // 2
    forward = moved(opposite[:half], along_y[1])
    backward = moved(opposite[half:], along_y[-1])
    leaving = project(row, attention, out_weight, True, (1, 3, 0), [opposite])
    following, preceding, projected = over_cores(leaving, (1, 3, 0), [forward, backward])
    following = jnp.concatenate([following[:half] + forward.astype(jnp.float32), following[half:]])
    preceding = jnp.concatenate([preceding[:half], preceding[half:] + backward.astype(jnp.float32)])
    for share, m in ((following, 1), (preceding, -1)):
        projected = projected + moved(share.astype(jnp.bfloat16), along_y[m]).astype(jnp.float32)
    return (residual.astype(jnp.float32) + gate_row * projected).astype(jnp.bfloat16)


def solution(mesh):
    in_specs = (
        P("tm", "head"),
        P("tm", "head"),
        P("tm", "head"),
        P("tm", "head"),
        P("head", None),
        P(None, "head"),
        P("tm"),
        P(),
        P(),
    )
    out_specs = P("tm", "head")
    return jax.shard_map(body, mesh=mesh, in_specs=in_specs, out_specs=out_specs, check_vma=False)
```

```python
import functools
import math

import jax
import jax.numpy as jnp
import numpy as np
from jax import lax
from jax.experimental import pallas as pl
from jax.experimental.pallas import tpu as pltpu
from jax.sharding import PartitionSpec as P

HEAD_DIM = 128
SPAN = 256
X, Z, Y, C = 4, 8, 4, 2
HERE = 5
SPANS = X * Z
NEGATIVE = -1e30
SCALE = math.log2(math.e) / math.sqrt(HEAD_DIM)
MIB = 1024 * 1024

HOST = ((0, 1, 3, 4, 6), (0, 2, 4, 5, 7))
SHIFTS = (0, 4, 1, 7, 3, 5, 2, 6)
AXES = ("tm", "head")
PIECE = SPAN // X


def device(x, z, y, c):
    return ((x % X) * Z + z % Z) * (Y * C) + (y % Y) * C + c


ALL = [(x, z, y, c) for x in range(X) for z in range(Z) for y in range(Y) for c in range(C)]


def plane_pairs(shift):
    return [
        (device(x, z, y, c), device(x, z + shift, y, c))
        for x, z, y, c in ALL
        if (z + shift) % Z in HOST[c]
    ]


def across_pairs(m):
    return [(device(x, z, y, c), device(x + m, z, y, c)) for x, z, y, c in ALL if z in HOST[c]]


HEAD, PLANE, ACTIVE, PLACE_X, PLACE_Y, CORE, SEND, FROM = 0, 8, 13, 14, 15, 16, 17, 25
WIDTH = 64


def table():
    rows = np.zeros((X * Z * Y * C, WIDTH), np.int32)
    for x, z, y, c in ALL:
        row = rows[device(x, z, y, c)]
        for to_z in range(Z):
            row[HEAD + to_z] = HOST[c].index(to_z) if to_z in HOST[c] else -1
        row[PLANE : PLANE + HERE] = HOST[c]
        row[ACTIVE] = int(z in HOST[c])
        row[PLACE_X] = x
        row[PLACE_Y] = y
        row[CORE] = c
        for i, shift in enumerate(SHIFTS):
            row[SEND + i] = row[HEAD + (z + shift) % Z]
            row[FROM + i] = (z - shift) % Z
    return rows


def moved(block, pairs):
    return lax.ppermute(block, AXES, pairs)


def in_vmem():
    return pl.BlockSpec(memory_space=pltpu.VMEM)


def in_smem():
    return pl.BlockSpec(memory_space=pltpu.SMEM)


def anywhere():
    return pl.BlockSpec(memory_space=pl.ANY)


def shape(*dims, dtype=jnp.bfloat16):
    return jax.ShapeDtypeStruct(dims, dtype)


def pack_kernel(key_ref, value_ref, *refs):
    outs, copied = refs[:Z], refs[Z]
    z = lax.rem(lax.axis_index("tm"), Z)
    core = lax.rem(lax.axis_index("head"), C)

    hosted = [sum((HOST[c].index(to_z) + 8) << (4 * to_z) for to_z in HOST[c]) for c in range(C)]
    hosted = [have - (1 << 32) if have >= 1 << 31 else have for have in hosted]
    hosted = jnp.where(core == 0, jnp.int32(hosted[0]), jnp.int32(hosted[1]))
    heads = [
        lax.shift_right_logical(hosted, 4 * lax.rem(z + shift, Z)) & 15 for shift in SHIFTS
    ]

    def copies(i):
        columns = pl.ds(pl.multiple_of((heads[i] & 7) * HEAD_DIM, HEAD_DIM), HEAD_DIM)
        return [
            pltpu.make_async_copy(
                ref.at[:, columns], outs[i].at[:, pl.ds(n * HEAD_DIM, HEAD_DIM)], copied.at[i, n]
            )
            for n, ref in enumerate((key_ref, value_ref))
        ]

    for i in range(Z):

        @pl.when(heads[i] >= 8)
        def _():
            for copy in copies(i):
                copy.start()

    for i in range(Z):

        @pl.when(heads[i] >= 8)
        def _():
            for copy in copies(i):
                copy.wait()


def pack(key_rows, value_rows):
    return pl.pallas_call(
        pack_kernel,
        out_shape=[shape(SPAN, 2 * HEAD_DIM)] * Z,
        in_specs=[anywhere()] * 2,
        out_specs=[in_vmem()] * Z,
        scratch_shapes=[pltpu.SemaphoreType.DMA((Z, 2))],
        compiler_params=pltpu.CompilerParams(vmem_limit_bytes=8 * MIB),
        name="pack",
    )(key_rows, value_rows)


def pieces_kernel(row_ref, query_ref, unused_ref, pieces_ref):
    for z in range(Z):
        head = row_ref[HEAD + z]

        @pl.when(head >= 0)
        def _():
            columns = pl.ds(pl.multiple_of(head * HEAD_DIM, HEAD_DIM), HEAD_DIM)
            for x in range(X):
                pieces_ref[x * Z + z] = query_ref[x * PIECE : (x + 1) * PIECE, columns]


def cut_queries(row, query_rows, after):
    return pl.pallas_call(
        pieces_kernel,
        out_shape=shape(SPANS, PIECE, HEAD_DIM),
        in_specs=[in_smem(), in_vmem(), anywhere()],
        out_specs=in_vmem(),
        compiler_params=pltpu.CompilerParams(vmem_limit_bytes=8 * MIB),
        name="pieces",
    )(row, query_rows, after)


STEP = Z // 2
STEP_KEYS = STEP * SPAN
STEPS = 2 * X
TILE = 8
TILES = SPANS // TILE
TILE_ROWS = TILE * PIECE
ROWS = SPANS * PIECE
SMALLEST, LARGEST = 1e-18, 1e30
HALF_FREQ = 128
BELOW = 16


def attend_kernel(places, begins, ends, row_ref, offset_ref, pieces_ref, *refs):
    sources, refs = refs[: len(places)], refs[len(places) :]
    if not begins:
        (total_in, summed_in, shift_ref), refs = refs[:3], refs[3:]
    if ends:
        later_steps, refs = refs[: STEPS - len(places)], refs[STEPS - len(places) :]
        refs = refs[len(refs) - 7 :]
        out_ref, held, rows, total_ref, summed_ref, keys_at, copied = refs
    elif begins:
        (residual_ref, level_ref, table_ref), refs = refs[:3], refs[3:]
        total_ref, summed_ref, shift_ref, passed_on, held, rows, keys_at, copied = refs[:8]
        below, passing = refs[8:]
        pass_on = [
            pltpu.make_async_copy(residual_ref, passed_on.at[pl.ds(0, SPAN)], passing.at[0]),
            pltpu.make_async_copy(below, passed_on.at[pl.ds(SPAN, BELOW)], passing.at[1]),
        ]
        pass_on[0].start()
        steps_of = lax.broadcasted_iota(jnp.int32, (BELOW, HEAD_DIM), 1).astype(jnp.float32)
        stamp = table_ref[level_ref[0]].astype(jnp.float32)
        angles = stamp * jnp.exp(-math.log(10000.0) * steps_of / HALF_FREQ)
        below[:, :HALF_FREQ] = jnp.cos(angles).astype(jnp.bfloat16)
        below[:, HALF_FREQ : 2 * HALF_FREQ] = jnp.sin(angles).astype(jnp.bfloat16)
        below[:, 2 * HALF_FREQ :] = jnp.zeros_like(below[:, 2 * HALF_FREQ :])
        pass_on[1].start()
    else:
        total_ref, summed_ref, held, rows, keys_at, copied = refs
    offset = offset_ref[0]

    def place_of(span):
        return lax.rem(span - offset + SPANS, SPANS)

    def note_places(first, found):
        for i, (m, half) in enumerate(found):
            from_x = lax.rem(row_ref[PLACE_X] - m + X, X)
            for u in range(STEP):
                keys_at[first + i, u] = place_of(from_x * Z + row_ref[FROM + half * STEP + u])

    def scores_of(query, keys):
        return lax.dot_general(
            query, keys, (((1,), (1,)), ((), ())), preferred_element_type=jnp.float32
        )

    def values_of(weights, values):
        return jnp.dot(
            weights.astype(jnp.bfloat16), values, preferred_element_type=jnp.float32
        )

    def lanes(weights):
        parts = [weights[:, g : g + HEAD_DIM] for g in range(0, weights.shape[1], HEAD_DIM)]
        return sum(parts[1:], parts[0])

    def tile_rows(tile):
        return pl.ds(pl.multiple_of(tile * TILE_ROWS, TILE_ROWS), TILE_ROWS)

    def row_places(tile):
        return tile * TILE + lax.div(
            lax.broadcasted_iota(jnp.int32, (TILE_ROWS, 1), 0), jnp.int32(PIECE)
        )

    def running(tile):
        query, own = rows[tile_rows(tile), :], row_places(tile)

        def step(t, carry):
            top, total, summed = carry
            key_rows = pl.ds(pl.multiple_of(lax.rem(t, STEP) * SPAN, SPAN), SPAN)
            at = lax.div(t, STEP)
            seen = own >= keys_at[at, lax.rem(t, STEP)]
            scores = jnp.where(seen, scores_of(query, held[at, key_rows, :HEAD_DIM]), NEGATIVE)
            top_new = jnp.maximum(top, jnp.max(scores, axis=1, keepdims=True))
            weights = jnp.where(seen, jnp.exp2((scores - top_new) * SCALE), 0.0)
            factor = jnp.exp2((top - top_new) * SCALE)
            total = total * factor + jnp.sum(weights, axis=1, keepdims=True)
            summed = summed * factor + values_of(weights, held[at, key_rows, HEAD_DIM:])
            return top_new, total, summed

        start = (
            jnp.full((TILE_ROWS, 1), NEGATIVE, jnp.float32),
            jnp.zeros((TILE_ROWS, 1), jnp.float32),
            jnp.zeros((TILE_ROWS, HEAD_DIM), jnp.float32),
        )
        carry = lax.fori_loop(0, SPANS, step, start)
        return carry[2] / carry[1]

    @pl.when(row_ref[ACTIVE] == 1)
    def _():
        steps = len(places)
        for i, source in enumerate(sources):
            pltpu.make_async_copy(source, held.at[i], copied.at[i]).start()
        for span in range(SPANS):
            at = pl.ds(pl.multiple_of(place_of(span) * PIECE, PIECE), PIECE)
            rows[at, :] = pieces_ref[span]
        note_places(0, places)
        if begins:
            total_ref[...] = jnp.zeros_like(total_ref)
            summed_ref[...] = jnp.zeros_like(summed_ref)
        else:
            total_ref[...] = total_in[...]
            summed_ref[...] = summed_in[...]

        def wait_for(i):
            pltpu.make_async_copy(held.at[i], held.at[i], copied.at[i]).wait()

        if begins:
            wait_for(0)
            for tile in range(TILES):
                at = slice(tile * TILE_ROWS, (tile + 1) * TILE_ROWS)
                top = jnp.max(
                    scores_of(rows[at, :], held[0, :HEAD_DIM, :HEAD_DIM]), axis=1, keepdims=True
                )
                shift_ref[at, :] = jnp.broadcast_to(top * SCALE, (TILE_ROWS, HEAD_DIM))

        def add(tile, i, masked):
            at = tile_rows(tile)
            scores = scores_of(rows[at, :], held[i, :, :HEAD_DIM])
            shift = shift_ref[at, :1]
            if masked:
                own = row_places(tile)
                weights = []
                for u in range(STEP):
                    hidden = own < keys_at[i, u]
                    part = scores[:, u * SPAN : (u + 1) * SPAN] * SCALE
                    weights.append(jnp.exp2(part - jnp.where(hidden, LARGEST, shift)))
                weights = jnp.concatenate(weights, axis=1)
            else:
                weights = jnp.exp2(scores * SCALE - shift)
            total_ref[at, :] += lanes(weights)
            summed_ref[at, :] += values_of(weights, held[i, :, HEAD_DIM:])

        def one(n, unused):
            i, tile = lax.div(n, TILES), lax.rem(n, TILES)

            @pl.when((tile == 0) & (i >= int(begins)))
            def _():
                wait_for(i)

            found = [keys_at[i, u] for u in range(STEP)]
            lowest = functools.reduce(jnp.minimum, found)
            highest = functools.reduce(jnp.maximum, found)
            whole = highest <= tile * TILE

            @pl.when(whole)
            def _():
                add(tile, i, False)

            @pl.when(jnp.logical_not(whole) & (lowest < (tile + 1) * TILE))
            def _():
                add(tile, i, True)

            return unused

        lax.fori_loop(0, TILES * steps, one, 0)

        if ends:

            def put(tile, answer):
                for n in range(TILE):
                    slot = lax.rem(offset + (tile * TILE + n + 1), SPANS)
                    out_ref[slot] = answer[n * PIECE : (n + 1) * PIECE].astype(jnp.bfloat16)

            total = jnp.sum(total_ref[...], axis=1, keepdims=True)
            for tile in range(TILES):
                at = slice(tile * TILE_ROWS, (tile + 1) * TILE_ROWS)
                put(tile, summed_ref[at, :] / total[at])

            safe = (jnp.max(total) < LARGEST) & (jnp.min(total) > SMALLEST)

            @pl.when(jnp.logical_not(safe))
            def _():
                for i, source in enumerate(later_steps, steps):
                    pltpu.make_async_copy(source, held.at[i], copied.at[i]).start()
                for i in range(steps, STEPS):
                    wait_for(i)
                note_places(steps, OWN + BEHIND + AHEAD)
                for tile in range(TILES):
                    put(tile, running(tile))

    if begins:
        for copy in pass_on:
            copy.wait()


OWN = ((0, 0), (0, 1))
BEHIND = ((1, 0), (1, 1))
AHEAD = ((3, 0), (3, 1))
FAR = ((2, 0), (2, 1))


def attend_part(places, row, offset, pieces, sources, state=(), residual=None, level=None, table=None):
    held = shape(ROWS, HEAD_DIM, dtype=jnp.float32)
    begins = not state
    out_specs, outs = [in_vmem()] * 2, [held] * 2
    scratch = [
        pltpu.VMEM((len(sources), STEP_KEYS, 2 * HEAD_DIM), jnp.bfloat16),
        pltpu.VMEM((ROWS, HEAD_DIM), jnp.bfloat16),
        pltpu.SMEM((STEPS, STEP), jnp.int32),
        pltpu.SemaphoreType.DMA((STEPS,)),
    ]
    if begins:
        wide = residual.shape[1]
        out_specs = out_specs + [in_vmem(), anywhere()]
        outs = outs + [held, shape(SPAN + BELOW, wide)]
        scratch += [pltpu.VMEM((BELOW, wide), jnp.bfloat16), pltpu.SemaphoreType.DMA((2,))]
    found = pl.pallas_call(
        functools.partial(attend_kernel, places, begins, False),
        out_shape=outs,
        in_specs=[in_smem(), in_smem(), in_vmem()]
        + [anywhere()] * len(sources)
        + ([anywhere(), in_smem(), in_smem()] if begins else [in_vmem()] * len(state)),
        out_specs=out_specs,
        scratch_shapes=scratch,
        compiler_params=pltpu.CompilerParams(vmem_limit_bytes=28 * MIB),
        name="part",
    )(row, offset, pieces, *sources, *((residual, level, table) if begins else state))
    return found if begins else [*found, state[2]]


def attend_far(row, offset, pieces, far, state, near):
    return pl.pallas_call(
        functools.partial(attend_kernel, FAR, False, True),
        out_shape=shape(SPANS, PIECE, HEAD_DIM),
        in_specs=[in_smem(), in_smem(), in_vmem()]
        + [anywhere()] * len(far)
        + [in_vmem()] * len(state)
        + [anywhere()] * len(near),
        out_specs=in_vmem(),
        scratch_shapes=[
            pltpu.VMEM((STEPS, STEP_KEYS, 2 * HEAD_DIM), jnp.bfloat16),
            pltpu.VMEM((ROWS, HEAD_DIM), jnp.bfloat16),
            pltpu.VMEM((ROWS, HEAD_DIM), jnp.float32),
            pltpu.VMEM((ROWS, HEAD_DIM), jnp.float32),
            pltpu.SMEM((STEPS, STEP), jnp.int32),
            pltpu.SemaphoreType.DMA((STEPS,)),
        ],
        compiler_params=pltpu.CompilerParams(vmem_limit_bytes=28 * MIB),
        name="far",
    )(row, offset, pieces, *far, *state, *near)


def share_of(row_ref, rows, weight_ref, out_ref, other, places):
    wide = out_ref.shape[2]
    core = 1 - row_ref[CORE] if other else row_ref[CORE]
    for n, m in enumerate(places):
        block = lax.rem(row_ref[PLACE_Y] + m, Y) * C + core
        columns = pl.ds(pl.multiple_of(block * wide, HEAD_DIM), wide)
        out_ref[n] = jnp.dot(
            rows, weight_ref[:, columns], preferred_element_type=jnp.float32
        ).astype(jnp.bfloat16)


def first_kernel(row_ref, parts_ref, weight_ref, passed_ref, out_ref, rows_ref, passed_on, passing):
    pass_on = pltpu.make_async_copy(passed_ref, passed_on, passing)
    pass_on.start()
    for head in range(HERE):
        for x in range(X):
            rows_ref[x * PIECE : (x + 1) * PIECE, head * HEAD_DIM : (head + 1) * HEAD_DIM] = (
                parts_ref[x * Z + row_ref[PLANE + head]]
            )
    share_of(row_ref, rows_ref[...], weight_ref, out_ref, True, (2,))
    pass_on.wait()


def project_first(row, parts, weight, passed):
    wide = weight.shape[1] // (Y * C)
    return pl.pallas_call(
        first_kernel,
        out_shape=[shape(1, SPAN, wide), shape(SPAN, HERE * HEAD_DIM), shape(*passed.shape)],
        in_specs=[in_smem(), in_vmem(), in_vmem(), in_vmem()],
        out_specs=[in_vmem()] * 3,
        scratch_shapes=[pltpu.SemaphoreType.DMA],
        compiler_params=pltpu.CompilerParams(vmem_limit_bytes=16 * MIB),
        name="first",
    )(row, parts, weight, passed)


def project_kernel(other, places, waits, row_ref, rows_ref, weight_ref, *refs):
    share_of(row_ref, rows_ref[...], weight_ref, refs[waits], other, places)


def project(row, rows, weight, other, places, after=()):
    return pl.pallas_call(
        functools.partial(project_kernel, other, places, len(after)),
        out_shape=shape(len(places), SPAN, weight.shape[1] // (Y * C)),
        in_specs=[in_smem(), in_vmem(), in_vmem()] + [anywhere()] * len(after),
        out_specs=in_vmem(),
        compiler_params=pltpu.CompilerParams(vmem_limit_bytes=16 * MIB),
        name="project",
    )(row, rows, weight, *after)


def body(
    query_rows,
    key_rows,
    value_rows,
    residual_in,
    out_weight,
    time_proj,
    levels,
    timestep_table,
    window_offset,
):
    me = lax.axis_index("tm") * (Y * C) + lax.axis_index("head")
    row = lax.dynamic_slice(jnp.asarray(table()), (me, 0), (1, WIDTH))[0]
    packed = pack(key_rows, value_rows)
    arrived = [
        moved(part, plane_pairs(shift)) if shift else part for part, shift in zip(packed, SHIFTS)
    ]

    own = [jnp.concatenate(arrived[half * STEP : (half + 1) * STEP]) for half in range(2)]
    back = [moved(part, across_pairs(1)) for part in own]
    ahead = [moved(part, across_pairs(-1)) for part in own]
    pieces = cut_queries(row, query_rows, own[1])
    pieces = lax.all_to_all(pieces, "tm", 0, 0, tiled=True)
    far = [moved(ahead[0], across_pairs(-1)), moved(back[1], across_pairs(1))]

    *state, passed = attend_part(
        OWN, row, window_offset, pieces, own, (), residual_in, levels, timestep_table
    )
    state = attend_part(BEHIND, row, window_offset, pieces, back, state)
    state = attend_part(AHEAD, row, window_offset, pieces, ahead, state)
    near = own + back + ahead
    answers = attend_far(row, window_offset, pieces, far, state, near)
    answers = lax.all_to_all(answers, "tm", 0, 0, tiled=True)

    swap = [(device(x, z, y, c), device(x, z, y, 1 - c)) for x, z, y, c in ALL]
    along_y = {m: [(device(x, z, y, c), device(x, z, y + m, c)) for x, z, y, c in ALL] for m in (1, -1)}

    def over_cores(leaving, places, after=()):
        from_core = moved(leaving, swap)
        kept = project(row, attention, out_weight, False, places, after)
        return [
            kept[n].astype(jnp.float32) + from_core[n].astype(jnp.float32)
            for n in range(len(places))
        ]

    leaving, attention, passed = project_first(row, answers, out_weight, passed)
    next_slot = [
        (device(x, z, y, c), device((x * Z + z + 1) % SPANS // Z, z + 1, y, c)) for x, z, y, c in ALL
    ]
    passed = moved(passed, next_slot)
    residual, embedding = passed[:SPAN], passed[SPAN : SPAN + 1, : time_proj.shape[0]]
    gate_row = jnp.dot(embedding, time_proj, preferred_element_type=jnp.float32)

    (opposite,) = over_cores(leaving, (2,))
    opposite = opposite.astype(jnp.bfloat16)
    half = SPAN // 2
    forward = moved(opposite[:half], along_y[1])
    backward = moved(opposite[half:], along_y[-1])
    leaving = project(row, attention, out_weight, True, (1, 3, 0), [opposite])
    following, preceding, projected = over_cores(leaving, (1, 3, 0), [forward, backward])
    following = jnp.concatenate([following[:half] + forward.astype(jnp.float32), following[half:]])
    preceding = jnp.concatenate([preceding[:half], preceding[half:] + backward.astype(jnp.float32)])
    for share, m in ((following, 1), (preceding, -1)):
        projected = projected + moved(share.astype(jnp.bfloat16), along_y[m]).astype(jnp.float32)
    return (residual.astype(jnp.float32) + gate_row * projected).astype(jnp.bfloat16)


def solution(mesh):
    in_specs = (
        P("tm", "head"),
        P("tm", "head"),
        P("tm", "head"),
        P("tm", "head"),
        P("head", None),
        P(None, "head"),
        P("tm"),
        P(),
        P(),
    )
    out_specs = P("tm", "head")
    return jax.shard_map(body, mesh=mesh, in_specs=in_specs, out_specs=out_specs, check_vma=False)
```

```python
import functools
import math

import jax
import jax.numpy as jnp
import numpy as np
from jax import lax
from jax.experimental import pallas as pl
from jax.experimental.pallas import tpu as pltpu
from jax.sharding import PartitionSpec as P

HEAD_DIM = 128
SPAN = 256
X, Z, Y, C = 4, 8, 4, 2
HERE = 5
SPANS = X * Z
NEGATIVE = -1e30
SCALE = math.log2(math.e) / math.sqrt(HEAD_DIM)
MIB = 1024 * 1024

HOST = ((0, 1, 3, 4, 6), (0, 2, 4, 5, 7))
SHIFTS = (0, 4, 1, 7, 3, 5, 2, 6)
AXES = ("tm", "head")
PIECE = SPAN // X


def device(x, z, y, c):
    return ((x % X) * Z + z % Z) * (Y * C) + (y % Y) * C + c


ALL = [(x, z, y, c) for x in range(X) for z in range(Z) for y in range(Y) for c in range(C)]


def plane_pairs(shift):
    return [
        (device(x, z, y, c), device(x, z + shift, y, c))
        for x, z, y, c in ALL
        if (z + shift) % Z in HOST[c]
    ]


def across_pairs(m):
    return [(device(x, z, y, c), device(x + m, z, y, c)) for x, z, y, c in ALL if z in HOST[c]]


HEAD, PLANE, ACTIVE, PLACE_X, PLACE_Y, CORE, SEND, FROM = 0, 8, 13, 14, 15, 16, 17, 25
WIDTH = 64


def table():
    rows = np.zeros((X * Z * Y * C, WIDTH), np.int32)
    for x, z, y, c in ALL:
        row = rows[device(x, z, y, c)]
        for to_z in range(Z):
            row[HEAD + to_z] = HOST[c].index(to_z) if to_z in HOST[c] else -1
        row[PLANE : PLANE + HERE] = HOST[c]
        row[ACTIVE] = int(z in HOST[c])
        row[PLACE_X] = x
        row[PLACE_Y] = y
        row[CORE] = c
        for i, shift in enumerate(SHIFTS):
            row[SEND + i] = row[HEAD + (z + shift) % Z]
            row[FROM + i] = (z - shift) % Z
    return rows


def moved(block, pairs):
    return lax.ppermute(block, AXES, pairs)


def in_vmem():
    return pl.BlockSpec(memory_space=pltpu.VMEM)


def in_smem():
    return pl.BlockSpec(memory_space=pltpu.SMEM)


def anywhere():
    return pl.BlockSpec(memory_space=pl.ANY)


def shape(*dims, dtype=jnp.bfloat16):
    return jax.ShapeDtypeStruct(dims, dtype)


def pack_kernel(key_ref, value_ref, *refs):
    outs, copied = refs[:Z], refs[Z]
    z = lax.rem(lax.axis_index("tm"), Z)
    core = lax.rem(lax.axis_index("head"), C)

    hosted = [sum((HOST[c].index(to_z) + 8) << (4 * to_z) for to_z in HOST[c]) for c in range(C)]
    hosted = [have - (1 << 32) if have >= 1 << 31 else have for have in hosted]
    hosted = jnp.where(core == 0, jnp.int32(hosted[0]), jnp.int32(hosted[1]))
    heads = [
        lax.shift_right_logical(hosted, 4 * lax.rem(z + shift, Z)) & 15 for shift in SHIFTS
    ]

    def copies(i):
        columns = pl.ds(pl.multiple_of((heads[i] & 7) * HEAD_DIM, HEAD_DIM), HEAD_DIM)
        return [
            pltpu.make_async_copy(
                ref.at[:, columns], outs[i].at[:, pl.ds(n * HEAD_DIM, HEAD_DIM)], copied.at[i, n]
            )
            for n, ref in enumerate((key_ref, value_ref))
        ]

    for i in range(Z):

        @pl.when(heads[i] >= 8)
        def _():
            for copy in copies(i):
                copy.start()

    for i in range(Z):

        @pl.when(heads[i] >= 8)
        def _():
            for copy in copies(i):
                copy.wait()


def pack(key_rows, value_rows):
    return pl.pallas_call(
        pack_kernel,
        out_shape=[shape(SPAN, 2 * HEAD_DIM)] * Z,
        in_specs=[anywhere()] * 2,
        out_specs=[in_vmem()] * Z,
        scratch_shapes=[pltpu.SemaphoreType.DMA((Z, 2))],
        compiler_params=pltpu.CompilerParams(vmem_limit_bytes=8 * MIB),
        name="pack",
    )(key_rows, value_rows)


def pieces_kernel(row_ref, query_ref, unused_ref, pieces_ref):
    for z in range(Z):
        head = row_ref[HEAD + z]

        @pl.when(head >= 0)
        def _():
            columns = pl.ds(pl.multiple_of(head * HEAD_DIM, HEAD_DIM), HEAD_DIM)
            for x in range(X):
                pieces_ref[x * Z + z] = query_ref[x * PIECE : (x + 1) * PIECE, columns]


def cut_queries(row, query_rows, after):
    return pl.pallas_call(
        pieces_kernel,
        out_shape=shape(SPANS, PIECE, HEAD_DIM),
        in_specs=[in_smem(), in_vmem(), anywhere()],
        out_specs=in_vmem(),
        compiler_params=pltpu.CompilerParams(vmem_limit_bytes=8 * MIB),
        name="pieces",
    )(row, query_rows, after)


STEP = Z // 2
STEP_KEYS = STEP * SPAN
STEPS = 2 * X
TILE = 8
TILES = SPANS // TILE
TILE_ROWS = TILE * PIECE
ROWS = SPANS * PIECE
SMALLEST, LARGEST = 1e-18, 1e30
HALF_FREQ = 128
BELOW = 16


def attend_kernel(places, begins, ends, row_ref, offset_ref, pieces_ref, *refs):
    sources, refs = refs[: len(places)], refs[len(places) :]
    if not begins:
        (total_in, summed_in, shift_ref), refs = refs[:3], refs[3:]
    if ends:
        later_steps, refs = refs[: STEPS - len(places)], refs[STEPS - len(places) :]
        refs = refs[len(refs) - 7 :]
        out_ref, held, rows, total_ref, summed_ref, keys_at, copied = refs
    elif begins:
        (residual_ref, level_ref, table_ref), refs = refs[:3], refs[3:]
        total_ref, summed_ref, shift_ref, passed_on, held, rows, keys_at, copied = refs[:8]
        below, passing = refs[8:]
        pass_on = [
            pltpu.make_async_copy(residual_ref, passed_on.at[pl.ds(0, SPAN)], passing.at[0]),
            pltpu.make_async_copy(below, passed_on.at[pl.ds(SPAN, BELOW)], passing.at[1]),
        ]
        pass_on[0].start()
        steps_of = lax.broadcasted_iota(jnp.int32, (BELOW, HEAD_DIM), 1).astype(jnp.float32)
        stamp = table_ref[level_ref[0]].astype(jnp.float32)
        angles = stamp * jnp.exp(-math.log(10000.0) * steps_of / HALF_FREQ)
        below[:, :HALF_FREQ] = jnp.cos(angles).astype(jnp.bfloat16)
        below[:, HALF_FREQ : 2 * HALF_FREQ] = jnp.sin(angles).astype(jnp.bfloat16)
        below[:, 2 * HALF_FREQ :] = jnp.zeros_like(below[:, 2 * HALF_FREQ :])
        pass_on[1].start()
    else:
        total_ref, summed_ref, held, rows, keys_at, copied = refs
    offset = offset_ref[0]

    def place_of(span):
        return lax.rem(span - offset + SPANS, SPANS)

    def note_places(first, found):
        for i, (m, half) in enumerate(found):
            from_x = lax.rem(row_ref[PLACE_X] - m + X, X)
            for u in range(STEP):
                keys_at[first + i, u] = place_of(from_x * Z + row_ref[FROM + half * STEP + u])

    def scores_of(query, keys):
        return lax.dot_general(
            query, keys, (((1,), (1,)), ((), ())), preferred_element_type=jnp.float32
        )

    def values_of(weights, values):
        return jnp.dot(
            weights.astype(jnp.bfloat16), values, preferred_element_type=jnp.float32
        )

    def lanes(weights):
        parts = [weights[:, g : g + HEAD_DIM] for g in range(0, weights.shape[1], HEAD_DIM)]
        return sum(parts[1:], parts[0])

    def tile_rows(tile):
        return pl.ds(pl.multiple_of(tile * TILE_ROWS, TILE_ROWS), TILE_ROWS)

    def row_places(tile):
        return tile * TILE + lax.div(
            lax.broadcasted_iota(jnp.int32, (TILE_ROWS, 1), 0), jnp.int32(PIECE)
        )

    def running(tile):
        query, own = rows[tile_rows(tile), :], row_places(tile)

        def step(t, carry):
            top, total, summed = carry
            key_rows = pl.ds(pl.multiple_of(lax.rem(t, STEP) * SPAN, SPAN), SPAN)
            at = lax.div(t, STEP)
            seen = own >= keys_at[at, lax.rem(t, STEP)]
            scores = jnp.where(seen, scores_of(query, held[at, key_rows, :HEAD_DIM]), NEGATIVE)
            top_new = jnp.maximum(top, jnp.max(scores, axis=1, keepdims=True))
            weights = jnp.where(seen, jnp.exp2((scores - top_new) * SCALE), 0.0)
            factor = jnp.exp2((top - top_new) * SCALE)
            total = total * factor + jnp.sum(weights, axis=1, keepdims=True)
            summed = summed * factor + values_of(weights, held[at, key_rows, HEAD_DIM:])
            return top_new, total, summed

        start = (
            jnp.full((TILE_ROWS, 1), NEGATIVE, jnp.float32),
            jnp.zeros((TILE_ROWS, 1), jnp.float32),
            jnp.zeros((TILE_ROWS, HEAD_DIM), jnp.float32),
        )
        carry = lax.fori_loop(0, SPANS, step, start)
        return carry[2] / carry[1]

    @pl.when(row_ref[ACTIVE] == 1)
    def _():
        steps = len(places)
        for i, source in enumerate(sources):
            pltpu.make_async_copy(source, held.at[i], copied.at[i]).start()
        for span in range(SPANS):
            at = pl.ds(pl.multiple_of(place_of(span) * PIECE, PIECE), PIECE)
            rows[at, :] = pieces_ref[span]
        note_places(0, places)
        if begins:
            total_ref[...] = jnp.zeros_like(total_ref)
            summed_ref[...] = jnp.zeros_like(summed_ref)
        else:
            total_ref[...] = total_in[...]
            summed_ref[...] = summed_in[...]

        def wait_for(i):
            pltpu.make_async_copy(held.at[i], held.at[i], copied.at[i]).wait()

        if begins:
            wait_for(0)
            for tile in range(TILES):
                at = slice(tile * TILE_ROWS, (tile + 1) * TILE_ROWS)
                top = jnp.max(
                    scores_of(rows[at, :], held[0, :HEAD_DIM, :HEAD_DIM]), axis=1, keepdims=True
                )
                shift_ref[at, :] = jnp.broadcast_to(top * SCALE, (TILE_ROWS, HEAD_DIM))

        def add(tile, i, masked):
            at = tile_rows(tile)
            scores = scores_of(rows[at, :], held[i, :, :HEAD_DIM])
            shift = shift_ref[at, :1]
            if masked:
                own = row_places(tile)
                weights = []
                for u in range(STEP):
                    hidden = own < keys_at[i, u]
                    part = scores[:, u * SPAN : (u + 1) * SPAN] * SCALE
                    weights.append(jnp.exp2(part - jnp.where(hidden, LARGEST, shift)))
                weights = jnp.concatenate(weights, axis=1)
            else:
                weights = jnp.exp2(scores * SCALE - shift)
            total_ref[at, :] += lanes(weights)
            summed_ref[at, :] += values_of(weights, held[i, :, HEAD_DIM:])

        def one(n, unused):
            i, tile = lax.div(n, TILES), lax.rem(n, TILES)

            @pl.when((tile == 0) & (i >= int(begins)))
            def _():
                wait_for(i)

            found = [keys_at[i, u] for u in range(STEP)]
            lowest = functools.reduce(jnp.minimum, found)
            highest = functools.reduce(jnp.maximum, found)
            whole = highest <= tile * TILE

            @pl.when(whole)
            def _():
                add(tile, i, False)

            @pl.when(jnp.logical_not(whole) & (lowest < (tile + 1) * TILE))
            def _():
                add(tile, i, True)

            return unused

        lax.fori_loop(0, TILES * steps, one, 0)

        if ends:

            def put(tile, answer):
                for n in range(TILE):
                    slot = lax.rem(offset + (tile * TILE + n + 1), SPANS)
                    out_ref[slot] = answer[n * PIECE : (n + 1) * PIECE].astype(jnp.bfloat16)

            total = jnp.sum(total_ref[...], axis=1, keepdims=True)
            for tile in range(TILES):
                at = slice(tile * TILE_ROWS, (tile + 1) * TILE_ROWS)
                put(tile, summed_ref[at, :] / total[at])

            safe = (jnp.max(total) < LARGEST) & (jnp.min(total) > SMALLEST)

            @pl.when(jnp.logical_not(safe))
            def _():
                for i, source in enumerate(later_steps, steps):
                    pltpu.make_async_copy(source, held.at[i], copied.at[i]).start()
                for i in range(steps, STEPS):
                    wait_for(i)
                note_places(steps, OWN + BEHIND + AHEAD)
                for tile in range(TILES):
                    put(tile, running(tile))

    if begins:
        for copy in pass_on:
            copy.wait()


OWN = ((0, 0), (0, 1))
BEHIND = ((1, 0), (1, 1))
AHEAD = ((3, 0), (3, 1))
FAR = ((2, 0), (2, 1))


def attend_part(places, row, offset, pieces, sources, state=(), residual=None, level=None, table=None):
    held = shape(ROWS, HEAD_DIM, dtype=jnp.float32)
    begins = not state
    out_specs, outs = [in_vmem()] * 2, [held] * 2
    scratch = [
        pltpu.VMEM((len(sources), STEP_KEYS, 2 * HEAD_DIM), jnp.bfloat16),
        pltpu.VMEM((ROWS, HEAD_DIM), jnp.bfloat16),
        pltpu.SMEM((STEPS, STEP), jnp.int32),
        pltpu.SemaphoreType.DMA((STEPS,)),
    ]
    if begins:
        wide = residual.shape[1]
        out_specs = out_specs + [in_vmem(), anywhere()]
        outs = outs + [held, shape(SPAN + BELOW, wide)]
        scratch += [pltpu.VMEM((BELOW, wide), jnp.bfloat16), pltpu.SemaphoreType.DMA((2,))]
    found = pl.pallas_call(
        functools.partial(attend_kernel, places, begins, False),
        out_shape=outs,
        in_specs=[in_smem(), in_smem(), in_vmem()]
        + [anywhere()] * len(sources)
        + ([anywhere(), in_smem(), in_smem()] if begins else [in_vmem()] * len(state)),
        out_specs=out_specs,
        scratch_shapes=scratch,
        compiler_params=pltpu.CompilerParams(vmem_limit_bytes=28 * MIB),
        name="part",
    )(row, offset, pieces, *sources, *((residual, level, table) if begins else state))
    return found if begins else [*found, state[2]]


def attend_far(row, offset, pieces, far, state, near):
    return pl.pallas_call(
        functools.partial(attend_kernel, FAR, False, True),
        out_shape=shape(SPANS, PIECE, HEAD_DIM),
        in_specs=[in_smem(), in_smem(), in_vmem()]
        + [anywhere()] * len(far)
        + [in_vmem()] * len(state)
        + [anywhere()] * len(near),
        out_specs=in_vmem(),
        scratch_shapes=[
            pltpu.VMEM((STEPS, STEP_KEYS, 2 * HEAD_DIM), jnp.bfloat16),
            pltpu.VMEM((ROWS, HEAD_DIM), jnp.bfloat16),
            pltpu.VMEM((ROWS, HEAD_DIM), jnp.float32),
            pltpu.VMEM((ROWS, HEAD_DIM), jnp.float32),
            pltpu.SMEM((STEPS, STEP), jnp.int32),
            pltpu.SemaphoreType.DMA((STEPS,)),
        ],
        compiler_params=pltpu.CompilerParams(vmem_limit_bytes=28 * MIB),
        name="far",
    )(row, offset, pieces, *far, *state, *near)


def share_of(row_ref, rows, weight_ref, out_ref, other, places):
    wide = out_ref.shape[2]
    core = 1 - row_ref[CORE] if other else row_ref[CORE]
    for n, m in enumerate(places):
        block = lax.rem(row_ref[PLACE_Y] + m, Y) * C + core
        columns = pl.ds(pl.multiple_of(block * wide, HEAD_DIM), wide)
        out_ref[n] = jnp.dot(
            rows, weight_ref[:, columns], preferred_element_type=jnp.float32
        ).astype(jnp.bfloat16)


def first_kernel(row_ref, parts_ref, weight_ref, passed_ref, out_ref, rows_ref, passed_on, passing):
    pass_on = pltpu.make_async_copy(passed_ref, passed_on, passing)
    pass_on.start()
    for head in range(HERE):
        for x in range(X):
            rows_ref[x * PIECE : (x + 1) * PIECE, head * HEAD_DIM : (head + 1) * HEAD_DIM] = (
                parts_ref[x * Z + row_ref[PLANE + head]]
            )
    share_of(row_ref, rows_ref[...], weight_ref, out_ref, True, (2,))
    pass_on.wait()


def project_first(row, parts, weight, passed):
    wide = weight.shape[1] // (Y * C)
    return pl.pallas_call(
        first_kernel,
        out_shape=[shape(1, SPAN, wide), shape(SPAN, HERE * HEAD_DIM), shape(*passed.shape)],
        in_specs=[in_smem(), in_vmem(), in_vmem(), in_vmem()],
        out_specs=[in_vmem()] * 3,
        scratch_shapes=[pltpu.SemaphoreType.DMA],
        compiler_params=pltpu.CompilerParams(vmem_limit_bytes=16 * MIB),
        name="first",
    )(row, parts, weight, passed)


def project_kernel(other, places, waits, row_ref, rows_ref, weight_ref, *refs):
    share_of(row_ref, rows_ref[...], weight_ref, refs[waits], other, places)


def project(row, rows, weight, other, places, after=()):
    return pl.pallas_call(
        functools.partial(project_kernel, other, places, len(after)),
        out_shape=shape(len(places), SPAN, weight.shape[1] // (Y * C)),
        in_specs=[in_smem(), in_vmem(), in_vmem()] + [anywhere()] * len(after),
        out_specs=in_vmem(),
        compiler_params=pltpu.CompilerParams(vmem_limit_bytes=16 * MIB),
        name="project",
    )(row, rows, weight, *after)


def body(
    query_rows,
    key_rows,
    value_rows,
    residual_in,
    out_weight,
    time_proj,
    levels,
    timestep_table,
    window_offset,
):
    me = lax.axis_index("tm") * (Y * C) + lax.axis_index("head")
    row = lax.dynamic_slice(jnp.asarray(table()), (me, 0), (1, WIDTH))[0]
    packed = pack(key_rows, value_rows)
    arrived = [
        moved(part, plane_pairs(shift)) if shift else part for part, shift in zip(packed, SHIFTS)
    ]

    own = [jnp.concatenate(arrived[half * STEP : (half + 1) * STEP]) for half in range(2)]
    back = [moved(part, across_pairs(1)) for part in own]
    ahead = [moved(part, across_pairs(-1)) for part in own]
    pieces = cut_queries(row, query_rows, arrived[6])
    pieces = lax.all_to_all(pieces, "tm", 0, 0, tiled=True)
    far = [moved(ahead[0], across_pairs(-1)), moved(back[1], across_pairs(1))]

    *state, passed = attend_part(
        OWN, row, window_offset, pieces, own, (), residual_in, levels, timestep_table
    )
    state = attend_part(BEHIND, row, window_offset, pieces, back, state)
    state = attend_part(AHEAD, row, window_offset, pieces, ahead, state)
    near = own + back + ahead
    answers = attend_far(row, window_offset, pieces, far, state, near)
    answers = lax.all_to_all(answers, "tm", 0, 0, tiled=True)

    swap = [(device(x, z, y, c), device(x, z, y, 1 - c)) for x, z, y, c in ALL]
    along_y = {m: [(device(x, z, y, c), device(x, z, y + m, c)) for x, z, y, c in ALL] for m in (1, -1)}

    def over_cores(leaving, places, after=()):
        from_core = moved(leaving, swap)
        kept = project(row, attention, out_weight, False, places, after)
        return [
            kept[n].astype(jnp.float32) + from_core[n].astype(jnp.float32)
            for n in range(len(places))
        ]

    leaving, attention, passed = project_first(row, answers, out_weight, passed)
    next_slot = [
        (device(x, z, y, c), device((x * Z + z + 1) % SPANS // Z, z + 1, y, c)) for x, z, y, c in ALL
    ]
    passed = moved(passed, next_slot)
    residual, embedding = passed[:SPAN], passed[SPAN : SPAN + 1, : time_proj.shape[0]]
    gate_row = jnp.dot(embedding, time_proj, preferred_element_type=jnp.float32)

    (opposite,) = over_cores(leaving, (2,))
    opposite = opposite.astype(jnp.bfloat16)
    half = SPAN // 2
    forward = moved(opposite[:half], along_y[1])
    backward = moved(opposite[half:], along_y[-1])
    leaving = project(row, attention, out_weight, True, (1, 3, 0), [opposite])
    following, preceding, projected = over_cores(leaving, (1, 3, 0), [forward, backward])
    following = jnp.concatenate([following[:half] + forward.astype(jnp.float32), following[half:]])
    preceding = jnp.concatenate([preceding[:half], preceding[half:] + backward.astype(jnp.float32)])
    for share, m in ((following, 1), (preceding, -1)):
        projected = projected + moved(share.astype(jnp.bfloat16), along_y[m]).astype(jnp.float32)
    return (residual.astype(jnp.float32) + gate_row * projected).astype(jnp.bfloat16)


def solution(mesh):
    in_specs = (
        P("tm", "head"),
        P("tm", "head"),
        P("tm", "head"),
        P("tm", "head"),
        P("head", None),
        P(None, "head"),
        P("tm"),
        P(),
        P(),
    )
    out_specs = P("tm", "head")
    return jax.shard_map(body, mesh=mesh, in_specs=in_specs, out_specs=out_specs, check_vma=False)
```
